128 devices in a mesh: seq: 4 (over x_hi, core), fsdp: 32 (over z, x_lo, y).
Axes of the slice: x: 4 (x_hi: 2, x_lo: 2; x = x_hi * 2 + x_lo), y: 4, z: 4, core: 2. Of those that a mesh axis runs over, the one named last changes fastest.
Arguments:
- hidden_states: bfloat16 [32, 2048, 768], P('fsdp', 'seq'), may hold values from -6 to 6
- positions: int32 [32, 2048], P('fsdp', 'seq'), may hold values from 0 to 4095, as said below
- documents: int32 [32, 2048], P('fsdp', 'seq'), may hold values from 0 to 4, as said below
- cotangent: bfloat16 [32, 2048, 768], P('fsdp', 'seq'), may hold values from -6 to 6
- first_gain: bfloat16 [768], P('fsdp'), may hold values from 0.099609375 to 1.8984375
- first_shift: bfloat16 [768], P('fsdp'), may hold values from -1.75 to 1.75
- second_gain: bfloat16 [768], P('fsdp'), may hold values from 0.099609375 to 1.8984375
- second_shift: bfloat16 [768], P('fsdp'), may hold values from -1.75 to 1.75
- joint_weight: bfloat16 [768, 2304], P('fsdp'), may hold values from -0.21875 to 0.21875
- joint_bias: bfloat16 [2304], P('fsdp'), may hold values from -1.75 to 1.75
- output_weight: bfloat16 [768, 768], P('fsdp'), may hold values from -6 to 6
- output_bias: bfloat16 [768], P('fsdp'), may hold values from -1.75 to 1.75
- up_weight: bfloat16 [768, 3072], P('fsdp'), may hold values from -0.21875 to 0.21875
- up_bias: bfloat16 [3072], P('fsdp'), may hold values from -3 to 3
- down_weight: bfloat16 [3072, 768], P('fsdp'), may hold values from -0.109375 to 0.109375
- down_bias: bfloat16 [768], P('fsdp'), may hold values from -1.75 to 1.75
Outputs:
- layer_output: bfloat16 [32, 2048, 768], P('fsdp', 'seq')
- input_grad: bfloat16 [32, 2048, 768], P('fsdp', 'seq')
- first_gain_grad: float32 [768], P('fsdp')
- first_shift_grad: float32 [768], P('fsdp')
- second_gain_grad: float32 [768], P('fsdp')
- second_shift_grad: float32 [768], P('fsdp')
- joint_weight_grad: float32 [768, 2304], P('fsdp')
- joint_bias_grad: float32 [2304], P('fsdp')
- output_weight_grad: float32 [768, 768], P('fsdp')
- output_bias_grad: float32 [768], P('fsdp')
- up_weight_grad: float32 [768, 3072], P('fsdp')
- up_bias_grad: float32 [3072], P('fsdp')
- down_weight_grad: float32 [3072, 768], P('fsdp')
- down_bias_grad: float32 [768], P('fsdp')
The draws below stay inside these ranges and needn't reach their ends.
Inputs may be any that keep to these rules, and one draw needn't show every extreme that they name: `documents`: within a sequence document numbers never fall; in every sequence one document begins among the tokens of the first device along seq and ends among those of the last. `positions`: A token's position is its place in its document plus an offset for that document; the last token of every sequence holds the largest position.
All inputs are finite; a program needn't handle non-finite values.
Results may differ from the reference program's by a relative error of at most 0.025.
Values may be sent and summed in bfloat16 or wider, within the bound.
A program may use at most 192 MiB of HBM per device.

```python
import jax
import jax.numpy as jnp
from jax import lax

D = 768
HEADS = 12
HEAD_DIM = 64
ROT = 16
FF = 3072
TOK_DEV = 512
LENGTH = 2048
SEQS = 32


def doc_layout(key):
    streams = jax.random.split(key, 5)
    start_doc = jax.random.randint(streams[0], (SEQS, 1), 1, TOK_DEV, dtype=jnp.int32)
    finish_doc = jax.random.randint(streams[1], (SEQS, 1), 3 * TOK_DEV + 1, LENGTH, dtype=jnp.int32)
    first_cut = jax.random.randint(streams[2], (SEQS, 1), 1, start_doc + 1, dtype=jnp.int32)
    last_cut = jax.random.randint(streams[3], (SEQS, 1), finish_doc, LENGTH, dtype=jnp.int32)
    places = jnp.arange(LENGTH, dtype=jnp.int32)[None, :]
    labels = (places >= first_cut).astype(jnp.int32) + (places >= start_doc).astype(jnp.int32) + (places >= finish_doc).astype(jnp.int32) + (places >= last_cut).astype(jnp.int32)
    begins = jnp.where(places >= last_cut, last_cut, jnp.where(places >= finish_doc, finish_doc, jnp.where(places >= start_doc, start_doc, jnp.where(places >= first_cut, first_cut, 0))))
    drawn = jax.random.randint(streams[4], (SEQS, 5), 0, 2048, dtype=jnp.int32)
    numbers = jnp.arange(5, dtype=jnp.int32)
    offsets = jnp.where(numbers[None, :] == 4, 2048 + last_cut, drawn)
    picked = jnp.sum(jnp.where(labels[:, :, None] == numbers[None, None, :], offsets[:, None, :], 0), axis=2)
    return (labels.astype(jnp.int32), (places - begins + picked).astype(jnp.int32))


def draw_documents(key, part):
    labels, places = doc_layout(key)
    return labels


def draw_positions(key, part):
    labels, places = doc_layout(key)
    return places


def levels(rng, dims, cuts, least, largest):
    level = 1.0
    for axis_at, blocks in cuts:
        draws = jax.random.uniform(jax.random.fold_in(jax.random.fold_in(rng, 6), axis_at), (blocks,), jnp.float32, least / len(cuts), largest / len(cuts))
        level = level * jnp.repeat(jnp.exp(draws), dims[axis_at] // blocks).reshape((-1,) + (1,) * (len(dims) - 1 - axis_at))
    return level


def normal_values(own_key, extent, scale, reach, cuts=(), held_as=jnp.bfloat16):
    array = scale * jax.random.normal(own_key, extent, jnp.float32)
    if cuts:
        array = array * levels(own_key, extent, cuts, -0.22, 0.18)
    return jnp.clip(array, -reach, reach).astype(held_as)


def setup_inputs(seed: int = 0) -> dict:
    arg_keys = jax.random.split(jax.random.key(seed), 17)
    hidden_states = normal_values(arg_keys[0], (SEQS, LENGTH, D), 1.0, 6.0, ((0, 32), (1, 4)))
    positions = draw_positions(jax.random.fold_in(arg_keys[16], 71), 0)
    documents = draw_documents(jax.random.fold_in(arg_keys[16], 71), 0)
    cotangent = normal_values(arg_keys[3], (SEQS, LENGTH, D), 1.0, 6.0, ((0, 32), (1, 4)))
    first_gain = jnp.clip(1.0 + 0.18 * jax.random.normal(arg_keys[4], (D,), jnp.float32), 0.099609375, 1.8984375).astype(jnp.bfloat16)
    first_shift = normal_values(arg_keys[5], (D,), 0.3, 1.75, ((0, 32),))
    second_gain = jnp.clip(1.0 + 0.18 * jax.random.normal(arg_keys[6], (D,), jnp.float32), 0.099609375, 1.8984375).astype(jnp.bfloat16)
    second_shift = normal_values(arg_keys[7], (D,), 0.3, 1.75, ((0, 32),))
    joint_weight = normal_values(arg_keys[8], (D, 3 * D), D ** -0.5, 0.21875, ((0, 32),))
    joint_bias = normal_values(arg_keys[9], (3 * D,), 0.3, 1.75, ((0, 32),))
    output_weight = normal_values(arg_keys[10], (D, D), (max(2 * D // LENGTH, 1)) ** -0.5, 6.0, ((0, 32),))
    output_bias = normal_values(arg_keys[11], (D,), 0.3, 1.75, ((0, 32),))
    up_weight = normal_values(arg_keys[12], (D, FF), D ** -0.5, 0.21875, ((0, 32),))
    up_bias = normal_values(arg_keys[13], (FF,), 0.5, 3.0, ((0, 32),))
    down_weight = normal_values(arg_keys[14], (FF, D), FF ** -0.5, 0.109375, ((0, 32),))
    down_bias = normal_values(arg_keys[15], (D,), 0.3, 1.75, ((0, 32),))
    return dict(hidden_states=hidden_states, positions=positions, documents=documents, cotangent=cotangent, first_gain=first_gain, first_shift=first_shift, second_gain=second_gain, second_shift=second_shift, joint_weight=joint_weight, joint_bias=joint_bias, output_weight=output_weight, output_bias=output_bias, up_weight=up_weight, up_bias=up_bias, down_weight=down_weight, down_bias=down_bias)


@jax.custom_vjp
def low(v):
    return lax.optimization_barrier(v.astype(jnp.bfloat16)).astype(jnp.float32)

@jax.custom_vjp
def low_back(v):
    return v

def low_keep(v):
    return (low(v), None)

def low_pass(kept, grad):
    return (grad,)

def back_keep(v):
    return (v, None)

def back_low(kept, grad):
    return (low(grad),)
low.defvjp(low_keep, low_pass)
low_back.defvjp(back_keep, back_low)

def norm_parts(states, norm_gain, norm_shift):
    average = lax.optimization_barrier(jnp.mean(states, axis=-1, keepdims=True))
    centered = states - average
    spread = lax.optimization_barrier(jnp.mean(centered * centered, axis=-1, keepdims=True))
    return centered * lax.rsqrt(spread + 1e-05) * norm_gain + norm_shift

def angles(places):
    freqs = 10000.0 ** (-jnp.arange(0, ROT, 2).astype(jnp.float32) / ROT)
    turned = places.astype(jnp.float32)[:, None] * freqs[None, :]
    return (jnp.cos(turned)[:, None, :], jnp.sin(turned)[:, None, :])

def rotate(values, cosine, sine):
    half_rot = ROT // 2
    first_half = values[..., :half_rot]
    second_half = values[..., half_rot:ROT]
    return jnp.concatenate([first_half * cosine - second_half * sine, second_half * cosine + first_half * sine, values[..., ROT:]], axis=-1)

def layer_forward(states, labels, cosine, sine, weights):
    gain_one, shift_one, gain_two, shift_two, joint_matrix, joint_shift, output_matrix, output_shift, up_matrix, up_shift, down_matrix, down_shift = weights
    first_in = low(norm_parts(states, gain_one, shift_one))
    second_in = low(norm_parts(states, gain_two, shift_two))
    projected = low_back(jnp.dot(first_in, joint_matrix, precision=lax.Precision.HIGHEST) + joint_shift)
    queries = projected[:, :D].reshape(LENGTH, HEADS, HEAD_DIM)
    key_rows = projected[:, D:2 * D].reshape(LENGTH, HEADS, HEAD_DIM)
    values = projected[:, 2 * D:].reshape(LENGTH, HEADS, HEAD_DIM)
    queries = low(low_back(rotate(queries, cosine, sine)))
    key_rows = low(low_back(rotate(key_rows, cosine, sine)))
    values = low(low_back(values))
    block_rows = min(512, LENGTH)
    block_count = LENGTH // block_rows
    columns = jnp.arange(LENGTH)

    def attend(pieces):
        query_block, row_block, label_block = pieces
        scores = jnp.einsum('qhd,khd->hqk', query_block, key_rows, precision=lax.Precision.HIGHEST) * HEAD_DIM ** (-0.5)
        allowed = (row_block[:, None] >= columns[None, :]) & (label_block[:, None] == labels[None, :])
        scores = low_back(jnp.where(allowed[None], scores, -1e+30))
        probs = low(jax.nn.softmax(scores, axis=-1))
        return jnp.einsum('hqk,khd->qhd', probs, values, precision=lax.Precision.HIGHEST)
    mixed = lax.map(jax.checkpoint(attend), (queries.reshape(block_count, block_rows, HEADS, HEAD_DIM), columns.reshape(block_count, block_rows), labels.reshape(block_count, block_rows)))
    context = low(low_back(mixed.reshape(LENGTH, D)))
    attn_out = jnp.dot(context, output_matrix, precision=lax.Precision.HIGHEST) + output_shift
    hidden = low_back(jnp.dot(second_in, up_matrix, precision=lax.Precision.HIGHEST) + up_shift)
    activated = low(jax.nn.gelu(hidden, approximate=False))
    mlp_out = jnp.dot(activated, down_matrix, precision=lax.Precision.HIGHEST) + down_shift
    return states + attn_out + mlp_out

def reference(hidden_states, positions, documents, cotangent, first_gain, first_shift, second_gain, second_shift, joint_weight, joint_bias, output_weight, output_bias, up_weight, up_bias, down_weight, down_bias):
    params = tuple((param.astype(jnp.float32) for param in (first_gain, first_shift, second_gain, second_shift, joint_weight, joint_bias, output_weight, output_bias, up_weight, up_bias, down_weight, down_bias)))

    def one_sequence(carried, sequence):
        seq_states, places, labels, tangent = sequence
        cosine, sine = angles(places)

        def forward(states_in, *weights):
            return layer_forward(states_in, labels, cosine, sine, weights)
        result, pullback = jax.vjp(forward, seq_states.astype(jnp.float32), *params)
        grads = pullback(tangent.astype(jnp.float32))
        carried = tuple((running + update for running, update in zip(carried, grads[1:])))
        return (carried, (result.astype(jnp.bfloat16), grads[0].astype(jnp.bfloat16)))
    zeros_init = tuple((jnp.zeros(param.shape, jnp.float32) for param in params))
    summed, (layer_output, input_grad) = lax.scan(one_sequence, zeros_init, (hidden_states, positions, documents, cotangent))
    return (layer_output, input_grad, summed[0], summed[1], summed[2], summed[3], summed[4], summed[5], summed[6], summed[7], summed[8], summed[9], summed[10], summed[11])
```

```python
import functools
import jax
import jax.numpy as jnp
from jax import lax
from jax.sharding import PartitionSpec as P
from jax.experimental import pallas as pl
from jax.experimental.pallas import tpu as pltpu

MESH = pl.DeviceIdType.MESH


class Place:
    def __init__(self):
        self.seq = lax.axis_index("seq")
        self.fs = lax.axis_index("fsdp")
        self.core = lax.rem(self.seq, 2)
        self.hi = self.seq // 2
        z, xl, y = self.fs // 8, lax.rem(self.fs // 4, 2), lax.rem(self.fs, 4)
        c = self.core
        self.xl = xl
        self.pa, self.pb = y * (1 - c) + z * c, z * (1 - c) + y * c
        self.sa, self.sb = 1 + 7 * c, 8 - 7 * c

    def shard(self, da, dx, db):
        return (
            lax.rem(self.pa + da, 4) * self.sa
            + lax.rem(self.xl + dx, 2) * 4
            + lax.rem(self.pb + db, 4) * self.sb
        )

    def device(self, da, dx, db):
        return (self.seq, self.shard(da, dx, db))

    def sibling(self):
        return (self.seq + 1 - 2 * self.core, self.fs)

    def far(self, dx):
        return (self.seq + 2 - 4 * self.hi, self.shard(0, dx, 0))


def gather_partners(me):
    return [
        me.sibling(),
        me.device(0, 1, 0),
        me.device(1, 0, 0),
        me.device(3, 0, 0),
        me.device(0, 0, 1),
        me.device(0, 0, 3),
    ]


def enter(partners):
    barrier = pltpu.get_barrier_semaphore()
    for partner in partners:
        pl.semaphore_signal(barrier, inc=1, device_id=partner, device_id_type=MESH)
    pl.semaphore_wait(barrier, len(partners))


class Gather:
    def __init__(self, me, src, dst, send, recv, local):
        self.me, self.src, self.dst = me, src, dst
        self.send, self.recv, self.local = send, recv, local
        self.half = dst.shape[2] // 2
        self.sent = []
        self.cols = pl.ds(pl.multiple_of(me.core * self.half, 128), self.half)
        self.other = pl.ds(pl.multiple_of((1 - me.core) * self.half, 128), self.half)

    def slot(self, piece, cols=None):
        return self.dst.at[self.me.shard(*piece), :, self.cols if cols is None else cols]

    def key(self, piece):
        return piece[0] * 8 + piece[1] * 4 + piece[2]

    def push(self, piece, device, lands):
        own = piece == (0, 0, 0)
        src = self.src.at[:, self.cols] if own else self.slot(piece)
        copy = pltpu.make_async_remote_copy(
            src_ref=src,
            dst_ref=self.slot(piece),
            send_sem=self.send.at[len(self.sent)],
            recv_sem=self.recv.at[lands],
            device_id=device,
            device_id_type=MESH,
        )
        copy.start()
        self.sent.append(copy)

    def arrived(self, piece):
        ref = self.slot(piece)
        pltpu.make_async_copy(ref, ref, self.recv.at[self.key(piece)]).wait()
        self.push(piece, self.me.sibling(), 32 + self.key(piece))

    def ring_a(self, piece, step):
        da, dx, db = piece
        to = ((da - step) % 4, dx, db)
        self.push(piece, self.me.device(step % 4, 0, 0), self.key(to))

    def ring_b(self, piece, step):
        da, dx, db = piece
        to = (da, dx, (db - step) % 4)
        self.push(piece, self.me.device(0, 0, step % 4), self.key(to))

    def begin(self):
        self.keep = pltpu.make_async_copy(self.src, self.dst.at[self.me.fs], self.local)
        self.keep.start()
        self.push((0, 0, 0), self.me.device(0, 1, 0), self.key((0, 1, 0)))
        self.ring_a((0, 0, 0), 1)
        self.ring_a((0, 0, 0), -1)
        self.ring_b((0, 0, 0), 1)
        self.ring_b((0, 0, 0), -1)

    def spread_a(self):
        self.arrived((0, 1, 0))
        self.ring_a((0, 1, 0), 1)
        self.ring_a((0, 1, 0), -1)
        self.ring_b((0, 1, 0), 1)
        self.ring_b((0, 1, 0), -1)
        self.arrived((3, 0, 0))
        self.ring_a((3, 0, 0), 1)
        self.arrived((1, 0, 0))
        self.arrived((1, 1, 0))
        self.ring_a((1, 1, 0), -1)
        self.arrived((3, 1, 0))

    def spread_b(self):
        for da in (3, 1):
            for dx in range(2):
                self.ring_b((da, dx, 0), 1)
                self.ring_b((da, dx, 0), -1)
        for dx in range(2):
            self.arrived((2, dx, 0))
            self.ring_b((2, dx, 0), 1)
            self.ring_b((2, dx, 0), -1)

    def finish_b(self):
        for da in (0, 3, 1, 2):
            self.arrived((da, 0, 3))
            self.ring_b((da, 0, 3), 1)
            self.arrived((da, 1, 1))
            self.ring_b((da, 1, 1), -1)
            self.arrived((da, 0, 1))
            self.arrived((da, 1, 3))

    def last_b(self):
        for da in (0, 3, 1, 2):
            self.arrived((da, 0, 2))
            self.arrived((da, 1, 2))

    def end(self):
        for da in range(4):
            for dx in range(2):
                for db in range(4):
                    if (da, dx, db) != (0, 0, 0):
                        ref = self.slot((da, dx, db), self.other)
                        pltpu.make_async_copy(ref, ref, self.recv.at[32 + db * 8 + dx * 4 + da]).wait()
        self.keep.wait()
        for copy in self.sent:
            copy.wait_send()


def gather_kernel(*refs):
    n = 3
    srcs, dsts, (send, recv, local) = refs[:n], refs[n : 2 * n], refs[2 * n :]
    me = Place()
    groups = [Gather(me, srcs[g], dsts[g], send.at[g], recv.at[g], local.at[g]) for g in range(n)]
    enter(gather_partners(me))
    a, b, c = groups
    a.begin()
    a.spread_a()
    b.begin()
    a.spread_b()
    b.spread_a()
    a.finish_b()
    c.begin()
    b.spread_b()
    c.spread_a()
    a.last_b()
    b.finish_b()
    c.spread_b()
    b.last_b()
    c.finish_b()
    c.last_b()
    for group in groups:
        group.end()


def gather_weights(*packs):
    return pl.pallas_call(
        gather_kernel,
        out_shape=[jax.ShapeDtypeStruct((32,) + p.shape, p.dtype) for p in packs],
        in_specs=[pl.BlockSpec(memory_space=pl.ANY)] * len(packs),
        out_specs=[pl.BlockSpec(memory_space=pl.ANY)] * len(packs),
        scratch_shapes=[
            pltpu.SemaphoreType.DMA((len(packs), 64)),
            pltpu.SemaphoreType.DMA((len(packs), 64)),
            pltpu.SemaphoreType.DMA((len(packs),)),
        ],
        compiler_params=pltpu.CompilerParams(collective_id=1, has_side_effects=True),
        name="gather_weights",
    )(*packs)


def total_partners(me):
    return gather_partners(me) + [me.far(0), me.far(1)]


class Total:
    def __init__(self, me, part, out, acc, sib, inbox, mine, theirs, send, recv, local):
        self.me, self.part, self.out = me, part, out
        self.acc, self.sib, self.inbox, self.mine, self.theirs = acc, sib, inbox, mine, theirs
        self.send, self.recv, self.local = send, recv, local
        self.half = part.shape[2] // 2
        self.cols = pl.ds(pl.multiple_of(me.core * self.half, 128), self.half)
        self.other = pl.ds(pl.multiple_of((1 - me.core) * self.half, 128), self.half)
        self.sent = []

    def key(self, da, dx, db):
        return (da % 4) * 8 + dx * 4 + db % 4

    def push(self, src, dst, device, lands):
        copy = pltpu.make_async_remote_copy(
            src_ref=src,
            dst_ref=dst,
            send_sem=self.send.at[len(self.sent)],
            recv_sem=self.recv.at[lands],
            device_id=device,
            device_id_type=MESH,
        )
        copy.start()
        self.sent.append(copy)

    def arrived(self, ref, lands):
        pltpu.make_async_copy(ref, ref, self.recv.at[lands]).wait()

    def begin(self):
        self.loads = {}
        for da, dx, db in self.order():
            k = self.key(da, dx, db)
            self.push(
                self.part.at[self.me.shard(db, dx, da), :, self.other],
                self.sib.at[k],
                self.me.sibling(),
                k,
            )
            load = pltpu.make_async_copy(
                self.part.at[self.me.shard(da, dx, db), :, self.cols], self.acc.at[k], self.local.at[k]
            )
            load.start()
            self.loads[k] = load

    def order(self):
        return [(da, dx, db) for db in (2, 1, 3, 0) for da in (2, 1, 3, 0) for dx in range(2)]

    def add(self, k, ref):
        self.acc[k] = (self.acc[k].astype(jnp.float32) + ref[...].astype(jnp.float32)).astype(jnp.bfloat16)

    def add_sib(self, da, dx, db):
        k = self.key(da, dx, db)
        self.loads[k].wait()
        self.arrived(self.sib.at[k], k)
        self.add(k, self.sib.at[k])

    def hop(self, piece, device, slot):
        self.push(self.acc.at[self.key(*piece)], self.inbox.at[slot], device, 32 + slot)

    def take(self, piece, slot):
        self.arrived(self.inbox.at[slot], 32 + slot)
        self.add(self.key(*piece), self.inbox.at[slot])

    def first_b(self):
        me = self.me
        up, down = me.device(0, 0, 1), me.device(0, 0, 3)
        for da in (2, 1, 3, 0):
            self.add_sib(da, 0, 2)
            self.hop((da, 0, 2), up, da * 2)
            self.add_sib(da, 1, 2)
            self.hop((da, 1, 2), down, da * 2 + 1)
        for da in (2, 1, 3, 0):
            self.add_sib(da, 1, 1)
            self.hop((da, 1, 1), up, 8 + da * 4 + 2)
            self.add_sib(da, 0, 3)
            self.hop((da, 0, 3), down, 8 + da * 4 + 1)
        for da in (2, 1, 3, 0):
            self.add_sib(da, 0, 1)
            self.add_sib(da, 1, 3)

    def second_b(self):
        me = self.me
        up, down = me.device(0, 0, 1), me.device(0, 0, 3)
        for da in (2, 1, 3, 0):
            self.take((da, 0, 1), da * 2)
            self.hop((da, 0, 1), up, 8 + da * 4)
            self.take((da, 1, 3), da * 2 + 1)
            self.hop((da, 1, 3), down, 8 + da * 4 + 3)
        for da in (2, 1, 3, 0):
            for dx in range(2):
                self.add_sib(da, dx, 0)

    def first_a(self):
        me = self.me
        up, down = me.device(1, 0, 0), me.device(3, 0, 0)
        for da in (2, 1, 3, 0):
            for dx in range(2):
                for side in range(2):
                    self.take((da, dx, 0), 8 + da * 4 + dx * 2 + side)
            if da == 2:
                self.hop((2, 0, 0), up, 24)
                self.hop((2, 1, 0), down, 25)
            if da == 1:
                self.hop((1, 1, 0), up, 28)
            if da == 3:
                self.hop((3, 0, 0), down, 27)

    def second_a(self):
        me = self.me
        self.take((1, 0, 0), 24)
        self.hop((1, 0, 0), me.device(1, 0, 0), 26)
        self.take((3, 1, 0), 25)
        self.hop((3, 1, 0), me.device(3, 0, 0), 29)

    def along_x(self):
        me = self.me
        for dx in (1, 0):
            for side in range(2):
                self.take((0, dx, 0), 26 + dx * 2 + side)
            if dx == 1:
                self.hop((0, 1, 0), me.device(0, 1, 0), 30)
                self.hop((0, 1, 0), me.far(1), 31)
        self.hop((0, 0, 0), me.far(0), 32)

    def total(self):
        for slot in (30, 31, 32):
            self.arrived(self.inbox.at[slot], 32 + slot)
        wide = lambda ref: ref[...].astype(jnp.float32)
        own = wide(self.acc.at[0]) + wide(self.inbox.at[32])
        near = wide(self.inbox.at[30]) + wide(self.inbox.at[31])
        done = (own + near).astype(jnp.bfloat16)
        self.mine[...] = done
        self.push(self.mine, self.theirs, self.me.sibling(), 65)
        self.out[:, self.cols] = done.astype(jnp.float32)

    def end(self):
        self.arrived(self.theirs, 65)
        self.out[:, self.other] = self.theirs[...].astype(jnp.float32)
        for copy in self.sent:
            copy.wait_send()


def total_scratch(shape):
    rows, half = shape[1], shape[2] // 2
    return [
        pltpu.VMEM((32, rows, half), jnp.bfloat16),
        pltpu.VMEM((32, rows, half), jnp.bfloat16),
        pltpu.VMEM((33, rows, half), jnp.bfloat16),
        pltpu.VMEM((rows, half), jnp.bfloat16),
        pltpu.VMEM((rows, half), jnp.bfloat16),
        pltpu.SemaphoreType.DMA((80,)),
        pltpu.SemaphoreType.DMA((66,)),
        pltpu.SemaphoreType.DMA((32,)),
    ]


def run_totals(groups):
    n = len(groups)
    stages = ["first_b", "second_b", "first_a", "second_a", "along_x", "total"]
    for tick in range(len(stages) + 2 * (n - 1)):
        for g in range(n):
            s = tick - 2 * g
            if 0 <= s < len(stages):
                getattr(groups[g], stages[s])()
    for group in groups:
        group.end()


def total_kernel(n, *refs):
    parts, outs, scratch = refs[:n], refs[n : 2 * n], refs[2 * n :]
    me = Place()
    groups = [Total(me, parts[g], outs[g], *scratch[8 * g : 8 * g + 8]) for g in range(n)]
    enter(total_partners(me))
    for group in groups:
        group.begin()
    run_totals(groups)


def sum_grads(*parts):
    scratch = []
    for p in parts:
        scratch += total_scratch(p.shape)
    return pl.pallas_call(
        functools.partial(total_kernel, len(parts)),
        out_shape=[jax.ShapeDtypeStruct(p.shape[1:], jnp.float32) for p in parts],
        in_specs=[pl.BlockSpec(memory_space=pl.ANY)] * len(parts),
        out_specs=[pl.BlockSpec(memory_space=pltpu.VMEM)] * len(parts),
        scratch_shapes=scratch,
        compiler_params=pltpu.CompilerParams(
            collective_id=2, has_side_effects=True, vmem_limit_bytes=56 << 20
        ),
        name="sum_grads",
    )(*parts)


def exchange_kernel(src, dst, send, recv, local):
    seq, fs = lax.axis_index("seq"), lax.axis_index("fsdp")
    enter([(lax.rem(seq + k, 4), fs) for k in (1, 2, 3)])
    keep = pltpu.make_async_copy(src.at[seq], dst.at[seq], local)
    keep.start()
    copies = []
    for k in (2, 1, 3):
        to = lax.rem(seq + k, 4)
        copy = pltpu.make_async_remote_copy(
            src_ref=src.at[to],
            dst_ref=dst.at[seq],
            send_sem=send.at[k - 1],
            recv_sem=recv.at[k - 1],
            device_id=(to, fs),
            device_id_type=MESH,
        )
        copy.start()
        copies.append(copy)
    keep.wait()
    for copy in copies:
        copy.wait()


def exchange(x, channel):
    return pl.pallas_call(
        exchange_kernel,
        out_shape=jax.ShapeDtypeStruct(x.shape, x.dtype),
        in_specs=[pl.BlockSpec(memory_space=pl.ANY)],
        out_specs=pl.BlockSpec(memory_space=pl.ANY),
        scratch_shapes=[pltpu.SemaphoreType.DMA((3,)), pltpu.SemaphoreType.DMA((3,)), pltpu.SemaphoreType.DMA],
        compiler_params=pltpu.CompilerParams(collective_id=channel, has_side_effects=True),
        name="exchange",
    )(x)


BLK = 512
F32, BF16 = jnp.float32, jnp.bfloat16


def dot(a, b):
    return jnp.dot(a, b, preferred_element_type=F32)


def split_heads(x_ref, rows, s):
    q, qt, k, kt, v, vt, g, gt = s
    sl = pl.ds(rows * BLK, BLK)
    x = x_ref[rows]
    for h in range(3):
        for a, (r, t) in enumerate(((q, qt), (k, kt), (v, vt), (g, gt))):
            part = x[:, a * 192 + h * 64 : a * 192 + h * 64 + 64]
            if a == 0:
                part = part * jnp.asarray(0.125, BF16)
            r[h, sl, :] = part
            t[h, :, sl] = part.T


def masked(scores, i, j, doc_row, doc_col):
    if i == j:
        key = lax.broadcasted_iota(jnp.int32, (BLK, BLK), 0)
        query = lax.broadcasted_iota(jnp.int32, (BLK, BLK), 1)
        allowed = key <= query
        if i in (0, 3):
            allowed = allowed & (doc_col[pl.ds(j * BLK, BLK), :] == doc_row[:, pl.ds(i * BLK, BLK)])
        return jnp.where(allowed, scores, -1e30)
    if i == 3 or j == 0:
        allowed = doc_col[pl.ds(j * BLK, BLK), :] == doc_row[:, pl.ds(i * BLK, BLK)]
        return jnp.where(allowed, scores, -1e30)
    return scores


def attend_block(h, i, s, doc_row, doc_col, score, expo, dk, dv, out):
    q, qt, k, kt, v, vt, g, gt = s
    me = pl.ds(i * BLK, BLK)
    q_i, qt_i, gt_i = q[h, me, :], qt[h, :, me], gt[h, :, me]
    peak = None
    for j in range(i + 1):
        rows = pl.ds(j * BLK, BLK)
        sc = masked(dot(k[h, rows, :], qt_i), i, j, doc_row, doc_col)
        score[rows, :] = sc
        top = jnp.max(sc, axis=0, keepdims=True)
        peak = top if peak is None else jnp.maximum(peak, top)
    total, ctx = 0.0, 0.0
    for j in range(i + 1):
        rows = pl.ds(j * BLK, BLK)
        e = jnp.exp(score[rows, :] - peak)
        total = total + jnp.sum(e, axis=0, keepdims=True)
        e = e.astype(BF16)
        expo[rows, :] = e
        ctx = ctx + dot(vt[h, :, rows], e)
    inverse = 1.0 / total
    ctx = ctx * inverse
    gt_wide = gt_i.astype(F32)
    weighted = jnp.sum(ctx * gt_wide, axis=0, keepdims=True) * inverse
    scaled = (gt_wide * inverse).astype(BF16)
    scaled_rows = scaled.T
    dq = 0.0
    for j in range(i, -1, -1):
        rows = pl.ds(j * BLK, BLK)
        e = expo[rows, :]
        dp = dot(v[h, rows, :], scaled)
        ds = (e.astype(F32) * (dp - weighted)).astype(BF16)
        add_v, add_k = dot(e, scaled_rows), dot(ds, q_i)
        if i == 3:
            dv[h, rows, :], dk[h, rows, :] = add_v, add_k
        else:
            dv[h, rows, :] += add_v
            dk[h, rows, :] += add_k
        dq = dq + dot(kt[h, :, rows], ds)
    out[h, 0] = ctx.T.astype(BF16)
    out[h, 1] = (dq * 0.125).T.astype(BF16)


def join_heads(i, out, dk, dv, y_ref):
    me = pl.ds(i * BLK, BLK)
    parts = [out[h, 0] for h in range(3)] + [out[h, 1] for h in range(3)]
    parts += [dk[h, me, :].astype(BF16) for h in range(3)] + [dv[h, me, :].astype(BF16) for h in range(3)]
    y_ref[i] = jnp.concatenate(parts, axis=1)


def attn_scratch():
    rows, cols = pltpu.VMEM((3, 2048, 64), BF16), pltpu.VMEM((3, 64, 2048), BF16)
    return [rows, cols] * 4 + [
        pltpu.VMEM((2048, BLK), F32),
        pltpu.VMEM((2048, BLK), BF16),
        pltpu.VMEM((3, 2048, 64), F32),
        pltpu.VMEM((3, 2048, 64), F32),
        pltpu.VMEM((3, 2, BLK, 64), BF16),
    ]


def attn_kernel(x_ref, doc_row, doc_col, y_ref, *scr):
    s, (score, expo, dk, dv, out) = scr[:8], scr[8:]
    for b in range(4):
        split_heads(x_ref, b, s)
    for i in (3, 2, 1, 0):
        def head(h, c):
            attend_block(h, i, s, doc_row, doc_col, score, expo, dk, dv, out)
            return c
        lax.fori_loop(0, 3, head, 0)
        join_heads(i, out, dk, dv, y_ref)


def attention(x, labels):
    return pl.pallas_call(
        attn_kernel,
        out_shape=jax.ShapeDtypeStruct((4, BLK, 768), BF16),
        in_specs=[pl.BlockSpec(memory_space=pltpu.VMEM)] * 3,
        out_specs=pl.BlockSpec(memory_space=pltpu.VMEM),
        scratch_shapes=attn_scratch(),
        compiler_params=pltpu.CompilerParams(vmem_limit_bytes=56 << 20),
        name="attention",
    )(x, labels.reshape(1, 2048), labels.reshape(2048, 1))


HEADS = 12
HEAD_DIM = 64
ROT = 16


def gelu_exact(values):
    return jax.nn.gelu(values, approximate=False)


def rotary_tables(places):
    freqs = 10000.0 ** (-jnp.arange(0, ROT, 2).astype(jnp.float32) / ROT)
    turned = places.astype(jnp.float32)[:, None] * freqs[None, :]
    cosine, sine = jnp.cos(turned), jnp.sin(turned)
    rest = places.shape[0], HEAD_DIM - ROT
    none = jnp.zeros_like(sine)
    wide = lambda parts: jnp.tile(jnp.concatenate(parts, axis=1), (1, 3))
    return (
        wide([cosine, cosine, jnp.ones(rest, jnp.float32)]),
        wide([sine, none, jnp.zeros(rest, jnp.float32)]),
        wide([none, sine, jnp.zeros(rest, jnp.float32)]),
    )


def rotate(x, tables, sign):
    cosine, low, high = tables
    return (
        x * cosine
        - sign * jnp.roll(x, -8, axis=-1) * low
        + sign * jnp.roll(x, 8, axis=-1) * high
    )


def by_group(w):
    return w.reshape(w.shape[:-1] + (3, 4, 192)).swapaxes(-3, -2).reshape(w.shape)


def by_array(w):
    return w.reshape(w.shape[:-1] + (4, 3, 192)).swapaxes(-3, -2).reshape(w.shape)


def body(
    hidden_states,
    positions,
    documents,
    cotangent,
    first_gain,
    first_shift,
    second_gain,
    second_shift,
    joint_weight,
    joint_bias,
    output_weight,
    output_bias,
    up_weight,
    up_bias,
    down_weight,
    down_bias,
):
    small = jnp.concatenate(
        [v[:, None] for v in (first_gain, first_shift, second_gain, second_shift, output_bias, down_bias)]
        + [joint_bias.reshape(24, 3), up_bias.reshape(24, 4), jnp.zeros((24, 243), BF16)],
        axis=1,
    )
    pack = jnp.concatenate([by_group(joint_weight), output_weight, small], axis=1)
    pack_all, up_all, down_all = gather_weights(pack, up_weight, down_weight)
    pack_all = pack_all.reshape(768, 3328)
    up_full, down_full = up_all.reshape(768, 3072), down_all.reshape(3072, 768)
    joint_full, output_full = pack_all[:, :2304], pack_all[:, 2304:3072]
    vectors = pack_all[:, 3072:3200].astype(jnp.float32)
    gain_one, shift_one, gain_two, shift_two, output_shift, down_shift = (vectors[:, i] for i in range(6))
    joint_shift = by_group(vectors[:, 6:9].reshape(2304))
    up_shift = vectors[:, 9:13].reshape(3072)

    states = hidden_states[0].astype(jnp.float32)
    average = jnp.mean(states, axis=-1, keepdims=True)
    centered = states - average
    root = lax.rsqrt(jnp.mean(centered * centered, axis=-1, keepdims=True) + 1e-05)
    xhat = centered * root
    first_in = (xhat * gain_one + shift_one).astype(BF16)
    second_in = (xhat * gain_two + shift_two).astype(BF16)
    tangent = cotangent[0]
    tables = rotary_tables(positions[0])
    projected = (jnp.dot(first_in, joint_full, preferred_element_type=F32) + joint_shift).reshape(512, 4, 3, 192)
    wide_tables = tuple(t[:, None, :] for t in tables)
    context_grad = lax.dot_general(tangent, output_full, (((1,), (1,)), ((), ())), preferred_element_type=F32)
    to_heads = jnp.concatenate(
        [
            rotate(projected[:, :, 0], wide_tables, 1.0).astype(BF16),
            rotate(projected[:, :, 1], wide_tables, 1.0).astype(BF16),
            projected[:, :, 2].astype(BF16),
            context_grad.reshape(512, 4, 192).astype(BF16),
        ],
        axis=2,
    ).swapaxes(0, 1)
    labels = lax.all_gather(documents[0], "seq", axis=0, tiled=True)
    by_heads = exchange(to_heads, 3)
    by_tokens = exchange(attention(by_heads, labels), 4)
    by_tokens = by_tokens.swapaxes(0, 1)
    context = by_tokens[:, :, :192].reshape(512, 768)
    attn_out = jnp.dot(context, output_full, preferred_element_type=F32) + output_shift
    hidden_pre = jnp.dot(second_in, up_full, preferred_element_type=F32) + up_shift
    activated, gelu_pull = jax.vjp(gelu_exact, hidden_pre)
    act_low = activated.astype(BF16)
    mlp_out = jnp.dot(act_low, down_full, preferred_element_type=F32) + down_shift
    layer_output = (states + attn_out + mlp_out).astype(BF16)

    tangent_wide = tangent.astype(F32)
    bias_sum = jnp.sum(tangent_wide, axis=0)
    down_weight_grad = jnp.einsum("tf,td->fd", act_low, tangent, preferred_element_type=F32)
    act_grad = jnp.einsum("td,fd->tf", tangent, down_full, preferred_element_type=F32)
    hidden_grad = gelu_pull(act_grad)[0].astype(BF16)
    up_weight_grad = jnp.einsum("td,tf->df", second_in, hidden_grad, preferred_element_type=F32)
    up_bias_grad = jnp.sum(hidden_grad.astype(F32), axis=0)
    second_grad = jnp.einsum("tf,df->td", hidden_grad, up_full, preferred_element_type=F32)
    output_weight_grad = jnp.einsum("td,te->de", context, tangent, preferred_element_type=F32)
    wide = by_tokens.astype(F32)
    joint_grad = jnp.concatenate(
        [
            rotate(wide[:, :, 192:384], wide_tables, -1.0),
            rotate(wide[:, :, 384:576], wide_tables, -1.0),
            wide[:, :, 576:],
        ],
        axis=2,
    ).astype(BF16).reshape(512, 2304)
    joint_weight_grad = jnp.einsum("td,tc->dc", first_in, joint_grad, preferred_element_type=F32)
    joint_bias_grad = by_array(jnp.sum(joint_grad.astype(F32), axis=0))
    first_grad = jnp.einsum("tc,dc->td", joint_grad, joint_full, preferred_element_type=F32)

    def norm_back(grad, gain):
        scaled = grad * gain
        mean_one = jnp.mean(scaled, axis=-1, keepdims=True)
        mean_two = jnp.mean(scaled * xhat, axis=-1, keepdims=True)
        return root * (scaled - mean_one - xhat * mean_two)

    input_grad = (tangent_wide + norm_back(first_grad, gain_one) + norm_back(second_grad, gain_two)).astype(BF16)
    sums = [
        jnp.sum(first_grad * xhat, axis=0),
        jnp.sum(first_grad, axis=0),
        jnp.sum(second_grad * xhat, axis=0),
        jnp.sum(second_grad, axis=0),
        bias_sum,
        bias_sum,
    ]
    small_grad = jnp.concatenate(
        [v[:, None] for v in sums]
        + [joint_bias_grad.reshape(768, 3), up_bias_grad.reshape(768, 4), jnp.zeros((768, 243), F32)],
        axis=1,
    )
    pack_grad = jnp.concatenate(
        [joint_weight_grad.astype(BF16), output_weight_grad.astype(BF16), small_grad.astype(BF16)], axis=1
    )
    pack_sum, up_sum, down_sum = sum_grads(
        pack_grad.reshape(32, 24, 3328),
        up_weight_grad.astype(BF16).reshape(32, 24, 3072),
        down_weight_grad.astype(BF16).reshape(32, 96, 768),
    )
    vector_sums = pack_sum[:, 3072:3200]
    return (
        layer_output[None],
        input_grad[None],
        vector_sums[:, 0],
        vector_sums[:, 1],
        vector_sums[:, 2],
        vector_sums[:, 3],
        by_array(pack_sum[:, :2304]),
        vector_sums[:, 6:9].reshape(72),
        pack_sum[:, 2304:3072],
        vector_sums[:, 4],
        up_sum,
        vector_sums[:, 9:13].reshape(96),
        down_sum,
        vector_sums[:, 5],
    )


def solution(mesh):
    in_specs = (
        P("fsdp", "seq", None),
        P("fsdp", "seq"),
        P("fsdp", "seq"),
        P("fsdp", "seq", None),
        P("fsdp"),
        P("fsdp"),
        P("fsdp"),
        P("fsdp"),
        P("fsdp", None),
        P("fsdp"),
        P("fsdp", None),
        P("fsdp"),
        P("fsdp", None),
        P("fsdp"),
        P("fsdp", None),
        P("fsdp"),
    )
    out_specs = (
        P("fsdp", "seq", None),
        P("fsdp", "seq", None),
        P("fsdp"),
        P("fsdp"),
        P("fsdp"),
        P("fsdp"),
        P("fsdp", None),
        P("fsdp"),
        P("fsdp", None),
        P("fsdp"),
        P("fsdp", None),
        P("fsdp"),
        P("fsdp", None),
        P("fsdp"),
    )
    return jax.shard_map(body, mesh=mesh, in_specs=in_specs, out_specs=out_specs, check_vma=False)
```

```python
import functools
import jax
import jax.numpy as jnp
from jax import lax
from jax.sharding import PartitionSpec as P
from jax.experimental import pallas as pl
from jax.experimental.pallas import tpu as pltpu

MESH = pl.DeviceIdType.MESH


class Place:
    def __init__(self):
        self.seq = lax.axis_index("seq")
        self.fs = lax.axis_index("fsdp")
        self.core = lax.rem(self.seq, 2)
        self.hi = self.seq // 2
        z, xl, y = self.fs // 8, lax.rem(self.fs // 4, 2), lax.rem(self.fs, 4)
        c = self.core
        self.xl = xl
        self.pa, self.pb = y * (1 - c) + z * c, z * (1 - c) + y * c
        self.sa, self.sb = 1 + 7 * c, 8 - 7 * c

    def shard(self, da, dx, db):
        return (
            lax.rem(self.pa + da, 4) * self.sa
            + lax.rem(self.xl + dx, 2) * 4
            + lax.rem(self.pb + db, 4) * self.sb
        )

    def device(self, da, dx, db):
        return (self.seq, self.shard(da, dx, db))

    def sibling(self):
        return (self.seq + 1 - 2 * self.core, self.fs)

    def far(self, dx):
        return (self.seq + 2 - 4 * self.hi, self.shard(0, dx, 0))


def gather_partners(me):
    return [
        me.sibling(),
        me.device(0, 1, 0),
        me.device(1, 0, 0),
        me.device(3, 0, 0),
        me.device(0, 0, 1),
        me.device(0, 0, 3),
    ]


def enter(partners):
    barrier = pltpu.get_barrier_semaphore()
    for partner in partners:
        pl.semaphore_signal(barrier, inc=1, device_id=partner, device_id_type=MESH)
    pl.semaphore_wait(barrier, len(partners))


class Gather:
    def __init__(self, me, src, dst, send, recv, local):
        self.me, self.src, self.dst = me, src, dst
        self.send, self.recv, self.local = send, recv, local
        self.half = dst.shape[2] // 2
        self.sent = []
        self.cols = pl.ds(pl.multiple_of(me.core * self.half, 128), self.half)
        self.other = pl.ds(pl.multiple_of((1 - me.core) * self.half, 128), self.half)

    def slot(self, piece, cols=None):
        return self.dst.at[self.me.shard(*piece), :, self.cols if cols is None else cols]

    def key(self, piece):
        return piece[0] * 8 + piece[1] * 4 + piece[2]

    def push(self, piece, device, lands):
        own = piece == (0, 0, 0)
        src = self.src.at[:, self.cols] if own else self.slot(piece)
        copy = pltpu.make_async_remote_copy(
            src_ref=src,
            dst_ref=self.slot(piece),
            send_sem=self.send.at[len(self.sent)],
            recv_sem=self.recv.at[lands],
            device_id=device,
            device_id_type=MESH,
        )
        copy.start()
        self.sent.append(copy)

    def arrived(self, piece):
        ref = self.slot(piece)
        pltpu.make_async_copy(ref, ref, self.recv.at[self.key(piece)]).wait()
        self.push(piece, self.me.sibling(), 32 + self.key(piece))

    def ring_a(self, piece, step):
        da, dx, db = piece
        to = ((da - step) % 4, dx, db)
        self.push(piece, self.me.device(step % 4, 0, 0), self.key(to))

    def ring_b(self, piece, step):
        da, dx, db = piece
        to = (da, dx, (db - step) % 4)
        self.push(piece, self.me.device(0, 0, step % 4), self.key(to))

    def begin(self):
        self.keep = pltpu.make_async_copy(self.src, self.dst.at[self.me.fs], self.local)
        self.keep.start()
        self.push((0, 0, 0), self.me.device(0, 1, 0), self.key((0, 1, 0)))
        self.ring_a((0, 0, 0), 1)
        self.ring_a((0, 0, 0), -1)
        self.ring_b((0, 0, 0), 1)
        self.ring_b((0, 0, 0), -1)

    def spread_a(self):
        self.arrived((0, 1, 0))
        self.ring_a((0, 1, 0), 1)
        self.ring_a((0, 1, 0), -1)
        self.ring_b((0, 1, 0), 1)
        self.ring_b((0, 1, 0), -1)
        self.arrived((3, 0, 0))
        self.ring_a((3, 0, 0), 1)
        self.arrived((1, 0, 0))
        self.arrived((1, 1, 0))
        self.ring_a((1, 1, 0), -1)
        self.arrived((3, 1, 0))

    def spread_b(self):
        for da in (3, 1):
            for dx in range(2):
                self.ring_b((da, dx, 0), 1)
                self.ring_b((da, dx, 0), -1)
        for dx in range(2):
            self.arrived((2, dx, 0))
            self.ring_b((2, dx, 0), 1)
            self.ring_b((2, dx, 0), -1)

    def finish_b(self):
        for da in (0, 3, 1, 2):
            self.arrived((da, 0, 3))
            self.ring_b((da, 0, 3), 1)
            self.arrived((da, 1, 1))
            self.ring_b((da, 1, 1), -1)
            self.arrived((da, 0, 1))
            self.arrived((da, 1, 3))

    def last_b(self):
        for da in (0, 3, 1, 2):
            self.arrived((da, 0, 2))
            self.arrived((da, 1, 2))

    def settle(self):
        for da in range(4):
            for dx in range(2):
                for db in range(4):
                    if (da, dx, db) != (0, 0, 0):
                        ref = self.slot((da, dx, db), self.other)
                        pltpu.make_async_copy(ref, ref, self.recv.at[32 + db * 8 + dx * 4 + da]).wait()
        self.keep.wait()

    def drain(self):
        for copy in self.sent:
            copy.wait_send()


def total_partners(me):
    return gather_partners(me) + [me.far(0), me.far(1)]


class Total:
    def __init__(self, me, part, out, acc, sib, inbox, mine, theirs, send, recv, local):
        self.me, self.part, self.out = me, part, out
        self.acc, self.sib, self.inbox, self.mine, self.theirs = acc, sib, inbox, mine, theirs
        self.send, self.recv, self.local = send, recv, local
        self.half = part.shape[2] // 2
        self.cols = pl.ds(pl.multiple_of(me.core * self.half, 128), self.half)
        self.other = pl.ds(pl.multiple_of((1 - me.core) * self.half, 128), self.half)
        self.sent = []

    def key(self, da, dx, db):
        return (da % 4) * 8 + dx * 4 + db % 4

    def push(self, src, dst, device, lands):
        copy = pltpu.make_async_remote_copy(
            src_ref=src,
            dst_ref=dst,
            send_sem=self.send.at[len(self.sent)],
            recv_sem=self.recv.at[lands],
            device_id=device,
            device_id_type=MESH,
        )
        copy.start()
        self.sent.append(copy)

    def arrived(self, ref, lands):
        pltpu.make_async_copy(ref, ref, self.recv.at[lands]).wait()

    def begin(self):
        self.loads = {}
        for da, dx, db in self.order():
            k = self.key(da, dx, db)
            self.push(
                self.part.at[self.me.shard(db, dx, da), :, self.other],
                self.sib.at[k],
                self.me.sibling(),
                k,
            )
            load = pltpu.make_async_copy(
                self.part.at[self.me.shard(da, dx, db), :, self.cols], self.acc.at[k], self.local.at[k]
            )
            load.start()
            self.loads[k] = load

    def order(self):
        return [(da, dx, db) for db in (2, 1, 3, 0) for da in (2, 1, 3, 0) for dx in range(2)]

    def add(self, k, ref):
        self.acc[k] = (self.acc[k].astype(jnp.float32) + ref[...].astype(jnp.float32)).astype(jnp.bfloat16)

    def add_sib(self, da, dx, db):
        k = self.key(da, dx, db)
        self.loads[k].wait()
        self.arrived(self.sib.at[k], k)
        self.add(k, self.sib.at[k])

    def hop(self, piece, device, slot):
        self.push(self.acc.at[self.key(*piece)], self.inbox.at[slot], device, 32 + slot)

    def take(self, piece, slot):
        self.arrived(self.inbox.at[slot], 32 + slot)
        self.add(self.key(*piece), self.inbox.at[slot])

    def first_b(self):
        me = self.me
        up, down = me.device(0, 0, 1), me.device(0, 0, 3)
        for da in (2, 1, 3, 0):
            self.add_sib(da, 0, 2)
            self.hop((da, 0, 2), up, da * 2)
            self.add_sib(da, 1, 2)
            self.hop((da, 1, 2), down, da * 2 + 1)
        for da in (2, 1, 3, 0):
            self.add_sib(da, 1, 1)
            self.hop((da, 1, 1), up, 8 + da * 4 + 2)
            self.add_sib(da, 0, 3)
            self.hop((da, 0, 3), down, 8 + da * 4 + 1)
        for da in (2, 1, 3, 0):
            self.add_sib(da, 0, 1)
            self.add_sib(da, 1, 3)

    def second_b(self):
        me = self.me
        up, down = me.device(0, 0, 1), me.device(0, 0, 3)
        for da in (2, 1, 3, 0):
            self.take((da, 0, 1), da * 2)
            self.hop((da, 0, 1), up, 8 + da * 4)
            self.take((da, 1, 3), da * 2 + 1)
            self.hop((da, 1, 3), down, 8 + da * 4 + 3)
        for da in (2, 1, 3, 0):
            for dx in range(2):
                self.add_sib(da, dx, 0)

    def first_a(self):
        me = self.me
        up, down = me.device(1, 0, 0), me.device(3, 0, 0)
        for da in (2, 1, 3, 0):
            for dx in range(2):
                for side in range(2):
                    self.take((da, dx, 0), 8 + da * 4 + dx * 2 + side)
            if da == 2:
                self.hop((2, 0, 0), up, 24)
                self.hop((2, 1, 0), down, 25)
            if da == 1:
                self.hop((1, 1, 0), up, 28)
            if da == 3:
                self.hop((3, 0, 0), down, 27)

    def second_a(self):
        me = self.me
        self.take((1, 0, 0), 24)
        self.hop((1, 0, 0), me.device(1, 0, 0), 26)
        self.take((3, 1, 0), 25)
        self.hop((3, 1, 0), me.device(3, 0, 0), 29)

    def along_x(self):
        me = self.me
        for dx in (1, 0):
            for side in range(2):
                self.take((0, dx, 0), 26 + dx * 2 + side)
            if dx == 1:
                self.hop((0, 1, 0), me.device(0, 1, 0), 30)
                self.hop((0, 1, 0), me.far(1), 31)
        self.hop((0, 0, 0), me.far(0), 32)

    def total(self):
        for slot in (30, 31, 32):
            self.arrived(self.inbox.at[slot], 32 + slot)
        wide = lambda ref: ref[...].astype(jnp.float32)
        own = wide(self.acc.at[0]) + wide(self.inbox.at[32])
        near = wide(self.inbox.at[30]) + wide(self.inbox.at[31])
        done = (own + near).astype(jnp.bfloat16)
        self.mine[...] = done
        self.push(self.mine, self.theirs, self.me.sibling(), 65)
        self.out[:, self.cols] = done.astype(jnp.float32)

    def end(self):
        self.arrived(self.theirs, 65)
        self.out[:, self.other] = self.theirs[...].astype(jnp.float32)
        for copy in self.sent:
            copy.wait_send()


def total_scratch(shape):
    rows, half = shape[1], shape[2] // 2
    return [
        pltpu.VMEM((32, rows, half), jnp.bfloat16),
        pltpu.VMEM((32, rows, half), jnp.bfloat16),
        pltpu.VMEM((33, rows, half), jnp.bfloat16),
        pltpu.VMEM((rows, half), jnp.bfloat16),
        pltpu.VMEM((rows, half), jnp.bfloat16),
        pltpu.SemaphoreType.DMA((80,)),
        pltpu.SemaphoreType.DMA((66,)),
        pltpu.SemaphoreType.DMA((32,)),
    ]


def run_totals(groups):
    n = len(groups)
    stages = ["first_b", "second_b", "first_a", "second_a", "along_x", "total"]
    for tick in range(len(stages) + 2 * (n - 1)):
        for g in range(n):
            s = tick - 2 * g
            if 0 <= s < len(stages):
                getattr(groups[g], stages[s])()
    for group in groups:
        group.end()


def total_kernel(n, *refs):
    parts, outs, scratch = refs[:n], refs[n : 2 * n], refs[2 * n :]
    me = Place()
    groups = [Total(me, parts[g], outs[g], *scratch[8 * g : 8 * g + 8]) for g in range(n)]
    enter(total_partners(me))
    for group in groups:
        group.begin()
    run_totals(groups)


def sum_grads(*parts):
    scratch = []
    for p in parts:
        scratch += total_scratch(p.shape)
    return pl.pallas_call(
        functools.partial(total_kernel, len(parts)),
        out_shape=[jax.ShapeDtypeStruct(p.shape[1:], jnp.float32) for p in parts],
        in_specs=[pl.BlockSpec(memory_space=pl.ANY)] * len(parts),
        out_specs=[pl.BlockSpec(memory_space=pltpu.VMEM)] * len(parts),
        scratch_shapes=scratch,
        compiler_params=pltpu.CompilerParams(
            collective_id=2, has_side_effects=True, vmem_limit_bytes=56 << 20
        ),
        name="sum_grads",
    )(*parts)


def exchange_kernel(src, dst, send, recv, local):
    seq, fs = lax.axis_index("seq"), lax.axis_index("fsdp")
    enter([(lax.rem(seq + k, 4), fs) for k in (1, 2, 3)])
    keep = pltpu.make_async_copy(src.at[seq], dst.at[seq], local)
    keep.start()
    copies = []
    for k in (2, 1, 3):
        to = lax.rem(seq + k, 4)
        copy = pltpu.make_async_remote_copy(
            src_ref=src.at[to],
            dst_ref=dst.at[seq],
            send_sem=send.at[k - 1],
            recv_sem=recv.at[k - 1],
            device_id=(to, fs),
            device_id_type=MESH,
        )
        copy.start()
        copies.append(copy)
    keep.wait()
    for copy in copies:
        copy.wait()


def exchange(x, channel):
    return pl.pallas_call(
        exchange_kernel,
        out_shape=jax.ShapeDtypeStruct(x.shape, x.dtype),
        in_specs=[pl.BlockSpec(memory_space=pl.ANY)],
        out_specs=pl.BlockSpec(memory_space=pl.ANY),
        scratch_shapes=[pltpu.SemaphoreType.DMA((3,)), pltpu.SemaphoreType.DMA((3,)), pltpu.SemaphoreType.DMA],
        compiler_params=pltpu.CompilerParams(collective_id=channel, has_side_effects=True),
        name="exchange",
    )(x)


BLK = 512
F32, BF16 = jnp.float32, jnp.bfloat16


def dot(a, b):
    return jnp.dot(a, b, preferred_element_type=F32)


def split_heads(x_ref, rows, s):
    q, qt, k, kt, v, vt, g, gt = s
    sl = pl.ds(rows * BLK, BLK)
    x = x_ref[rows]
    for h in range(3):
        for a, (r, t) in enumerate(((q, qt), (k, kt), (v, vt), (g, gt))):
            part = x[:, a * 192 + h * 64 : a * 192 + h * 64 + 64]
            if a == 0:
                part = part * jnp.asarray(0.125, BF16)
            r[h, sl, :] = part
            t[h, :, sl] = part.T


def masked(scores, i, j, doc_row, doc_col):
    if i == j:
        key = lax.broadcasted_iota(jnp.int32, (BLK, BLK), 0)
        query = lax.broadcasted_iota(jnp.int32, (BLK, BLK), 1)
        allowed = key <= query
        if i in (0, 3):
            allowed = allowed & (doc_col[pl.ds(j * BLK, BLK), :] == doc_row[:, pl.ds(i * BLK, BLK)])
        return jnp.where(allowed, scores, -1e30)
    if i == 3 or j == 0:
        allowed = doc_col[pl.ds(j * BLK, BLK), :] == doc_row[:, pl.ds(i * BLK, BLK)]
        return jnp.where(allowed, scores, -1e30)
    return scores


def attend_block(h, i, s, doc_row, doc_col, score, expo, dk, dv, out):
    q, qt, k, kt, v, vt, g, gt = s
    me = pl.ds(i * BLK, BLK)
    q_i, qt_i, gt_i = q[h, me, :], qt[h, :, me], gt[h, :, me]
    peak = None
    for j in range(i + 1):
        rows = pl.ds(j * BLK, BLK)
        sc = masked(dot(k[h, rows, :], qt_i), i, j, doc_row, doc_col)
        score[rows, :] = sc
        top = jnp.max(sc, axis=0, keepdims=True)
        peak = top if peak is None else jnp.maximum(peak, top)
    total, ctx = 0.0, 0.0
    for j in range(i + 1):
        rows = pl.ds(j * BLK, BLK)
        e = jnp.exp(score[rows, :] - peak)
        total = total + jnp.sum(e, axis=0, keepdims=True)
        e = e.astype(BF16)
        expo[rows, :] = e
        ctx = ctx + dot(vt[h, :, rows], e)
    inverse = 1.0 / total
    ctx = ctx * inverse
    gt_wide = gt_i.astype(F32)
    weighted = jnp.sum(ctx * gt_wide, axis=0, keepdims=True) * inverse
    scaled = (gt_wide * inverse).astype(BF16)
    scaled_rows = scaled.T
    dq = 0.0
    for j in range(i, -1, -1):
        rows = pl.ds(j * BLK, BLK)
        e = expo[rows, :]
        dp = dot(v[h, rows, :], scaled)
        ds = (e.astype(F32) * (dp - weighted)).astype(BF16)
        add_v, add_k = dot(e, scaled_rows), dot(ds, q_i)
        if i == 3:
            dv[h, rows, :], dk[h, rows, :] = add_v, add_k
        else:
            dv[h, rows, :] += add_v
            dk[h, rows, :] += add_k
        dq = dq + dot(kt[h, :, rows], ds)
    out[h, 0] = ctx.T.astype(BF16)
    out[h, 1] = (dq * 0.125).T.astype(BF16)


def join_heads(i, out, dk, dv, y_ref):
    me = pl.ds(i * BLK, BLK)
    parts = [out[h, 0] for h in range(3)] + [out[h, 1] for h in range(3)]
    parts += [dk[h, me, :].astype(BF16) for h in range(3)] + [dv[h, me, :].astype(BF16) for h in range(3)]
    y_ref[i] = jnp.concatenate(parts, axis=1)


def attn_scratch():
    rows, cols = pltpu.VMEM((3, 2048, 64), BF16), pltpu.VMEM((3, 64, 2048), BF16)
    return [rows, cols] * 4 + [
        pltpu.VMEM((2048, BLK), F32),
        pltpu.VMEM((2048, BLK), BF16),
        pltpu.VMEM((3, 2048, 64), F32),
        pltpu.VMEM((3, 2048, 64), F32),
        pltpu.VMEM((3, 2, BLK, 64), BF16),
    ]


def attn_kernel(x_ref, doc_row, doc_col, y_ref, *scr):
    s, (score, expo, dk, dv, out) = scr[:8], scr[8:]
    for b in range(4):
        split_heads(x_ref, b, s)
    for i in (3, 2, 1, 0):
        def head(h, c):
            attend_block(h, i, s, doc_row, doc_col, score, expo, dk, dv, out)
            return c
        lax.fori_loop(0, 3, head, 0)
        join_heads(i, out, dk, dv, y_ref)


def attention(x, labels):
    return pl.pallas_call(
        attn_kernel,
        out_shape=jax.ShapeDtypeStruct((4, BLK, 768), BF16),
        in_specs=[pl.BlockSpec(memory_space=pltpu.VMEM)] * 3,
        out_specs=pl.BlockSpec(memory_space=pltpu.VMEM),
        scratch_shapes=attn_scratch(),
        compiler_params=pltpu.CompilerParams(vmem_limit_bytes=56 << 20),
        name="attention",
    )(x, labels.reshape(1, 2048), labels.reshape(2048, 1))


D = 768
FF = 3072
ROWS = 128
SQRT_HALF = 0.7071067811865476
PHI_SCALE = 0.3989422804014327


def dot_nt(a, b):
    return lax.dot_general(a, b, (((1,), (1,)), ((), ())), preferred_element_type=F32)


def dot_tn(a, b):
    return lax.dot_general(a, b, (((0,), (0,)), ((), ())), preferred_element_type=F32)


def move_lane(tile, lane, source, target):
    if source != target:
        tile = pltpu.roll(tile, (target - source) % 128, axis=1)
    return jnp.where(lane == target, tile, 0.0)


def planes_to_columns(plane):
    lane = lax.broadcasted_iota(jnp.int32, (24, 128), 1)
    tiles = [plane(s) for s in range(32)]
    out = []
    for r in range(32):
        tile = jnp.where(lane < 6, tiles[r], 0.0)
        for count, base in ((3, 6), (4, 9)):
            for a in range(count):
                chunk = 32 * a + r
                tile = tile + move_lane(tiles[chunk // count], lane, base + chunk % count, base + a)
        out.append(tile)
    return jnp.concatenate(out, axis=0)


def columns_to_planes(columns):
    lane = lax.broadcasted_iota(jnp.int32, (24, 128), 1)
    tiles = [columns[24 * r : 24 * r + 24] for r in range(32)]
    out = []
    for s in range(32):
        tile = jnp.where(lane < 6, tiles[s], 0.0)
        for count, base in ((3, 6), (4, 9)):
            for c in range(count):
                chunk = count * s + c
                tile = tile + move_lane(tiles[chunk % 32], lane, base + chunk // 32, base + c)
        out.append(tile)
    return out


def join_planes(planes, out, cols):
    def pair(p, c):
        tile = jnp.concatenate(
            [planes[2 * p, :, cols].astype(F32), planes[2 * p + 1, :, cols].astype(F32)], axis=0
        )
        out[pl.ds(pl.multiple_of(48 * p, 16), 48), cols] = tile.astype(BF16)
        return c

    lax.fori_loop(0, 16, pair, 0)


def turn(x, cosine, low, high):
    n = x.shape[1]
    wide = lambda t: jnp.concatenate([t[...]] * (n // 128), axis=1)
    return (
        x * wide(cosine)
        + pltpu.roll(x, n - 8, axis=1) * wide(low)
        + pltpu.roll(x, 8, axis=1) * wide(high)
    )


def normalized(x):
    wide = x.astype(F32)
    centered = wide - jnp.mean(wide, axis=1, keepdims=True)
    root = lax.rsqrt(jnp.mean(centered * centered, axis=1, keepdims=True) + 1e-05)
    return wide, centered * root, root


def norm_back(grad, gain, xhat, root):
    scaled = grad * gain
    mean_one = jnp.mean(scaled, axis=1, keepdims=True)
    mean_two = jnp.mean(scaled * xhat, axis=1, keepdims=True)
    return root * (scaled - mean_one - xhat * mean_two)


def column_sum(x):
    return jnp.sum(x, axis=0, keepdims=True)


def front_kernel(
    joint_src, output_src, up_src, down_src, small_ref, x_ref, g_ref, cos_ref, low_ref, high_ref, doc_ref,
    heads_out, docs_out, jo_out, du_out, dd_out, first_out, vec_out, base_out, grad_out, sums_out,
    pack_src, pack_all, up_all, down_all, jo, uw, first, second, second_t, heads, act, slope,
    bias_rows, up_stage, down_stage,
    g_send, g_recv, g_local, x_send, x_recv, d_send, d_recv, local,
):
    me = Place()
    far = lax.rem(me.seq + 2, 4)
    far_sibling = far + 1 - 2 * me.core
    peers = [(far, me.fs), (far_sibling, me.fs), me.sibling()]

    loads = [
        pltpu.make_async_copy(joint_src, pack_src.at[:, pl.ds(0, 2304)], local.at[0]),
        pltpu.make_async_copy(output_src, pack_src.at[:, pl.ds(2304, D)], local.at[1]),
    ]
    for load in loads:
        load.start()
    turned = small_ref[...].T
    tile = jnp.concatenate(
        [turned[:24, :6]]
        + [turned[24 * c : 24 * c + 24, 6:7] for c in range(3)]
        + [turned[24 * c : 24 * c + 24, 7:8] for c in range(4)]
        + [jnp.zeros((24, 243), F32)],
        axis=1,
    )
    pack_src[:, 3072:] = tile.astype(BF16)
    a = Gather(me, pack_src, pack_all, g_send.at[0], g_recv.at[0], g_local.at[0])
    b = Gather(me, up_src, up_all, g_send.at[1], g_recv.at[1], g_local.at[1])
    c = Gather(me, down_src, down_all, g_send.at[2], g_recv.at[2], g_local.at[2])
    enter(gather_partners(me) + peers[:2])
    for load in loads:
        load.wait()
    a.begin()
    docs = []
    for k, peer in enumerate(peers):
        copy = pltpu.make_async_remote_copy(
            src_ref=doc_ref, dst_ref=docs_out.at[me.seq], send_sem=d_send.at[k], recv_sem=d_recv.at[k],
            device_id=peer, device_id_type=MESH,
        )
        copy.start()
        docs.append(copy)
    keep_docs = pltpu.make_async_copy(doc_ref, docs_out.at[me.seq], local.at[2])
    keep_docs.start()
    wide, xhat, root = normalized(x_ref[...])
    a.spread_a()
    b.begin()
    a.spread_b()
    b.spread_a()
    a.finish_b()
    c.begin()
    b.spread_b()
    c.spread_a()
    a.last_b()
    a.settle()

    columns = planes_to_columns(lambda s: pack_all[s, :, 3072:3200].astype(F32))
    vec = columns.T[:16]
    vec_out[...] = vec
    for f in range(4):
        for part in range(3):
            bias_rows[3 * f + part : 3 * f + part + 1, :] = vec[9 + f : 10 + f, 256 * part : 256 * part + 256]
    join_planes(pack_all, jo, pl.ds(0, 3072))
    keep_jo = pltpu.make_async_copy(jo, jo_out, local.at[3])
    keep_jo.start()
    first[...] = (xhat * vec[0:1] + vec[1:2]).astype(BF16)
    second_wide = xhat * vec[2:3] + vec[3:4]
    second[...] = second_wide.astype(BF16)
    first_out[...] = first[...]
    base_out[...] = wide + vec[4:5] + vec[5:6]

    sends = []
    for r in range(4):
        rows = pl.ds(r * ROWS, ROWS)
        tables = [t.at[rows, :] for t in (cos_ref, low_ref, high_ref)]
        x_r = first[rows, :]
        parts = []
        for n in range(2):
            y = dot(x_r, jo[:, n * D : n * D + D]) + vec[6 + n : 7 + n]
            parts.append(turn(y, *tables).astype(BF16))
        parts.append((dot(x_r, jo[:, 2 * D : 3 * D]) + vec[8:9]).astype(BF16))
        parts.append(dot_nt(g_ref[rows, :], jo[:, 3 * D :]).astype(BF16))
        for d in range(4):
            heads[d, rows, :] = jnp.concatenate([p[:, 192 * d : 192 * d + 192] for p in parts], axis=1)
        for k, peer in enumerate(peers):
            copy = pltpu.make_async_remote_copy(
                src_ref=heads.at[peer[0], rows, :], dst_ref=heads_out.at[me.seq, rows, :],
                send_sem=x_send.at[r, k], recv_sem=x_recv.at[r, k], device_id=peer, device_id_type=MESH,
            )
            copy.start()
            sends.append(copy)
        if r == 0:
            b.finish_b()
        if r == 2:
            c.spread_b()
    keep_heads = pltpu.make_async_copy(heads.at[me.seq], heads_out.at[me.seq], local.at[4])
    keep_heads.start()
    b.last_b()
    b.settle()

    join_planes(up_all, uw, pl.ds(0, FF))
    second_t[...] = second_wide.T.astype(BF16)
    c.finish_b()

    def hidden(n, carry):
        cols = pl.ds(pl.multiple_of(256 * n, 256), 256)
        h = dot(second[...], uw[:, cols]) + bias_rows[pl.ds(n, 1), :]
        half = 0.5 + 0.5 * lax.erf(h * SQRT_HALF)
        act[:, cols] = (h * half).astype(BF16)
        slope[:, cols] = (half + h * (jnp.exp(-0.5 * (h * h)) * PHI_SCALE)).astype(BF16)
        return carry

    lax.fori_loop(0, 12, hidden, 0)
    c.last_b()
    c.settle()
    down = down_all.reshape(FF, D)

    def hidden_back(n, carry):
        cols = pl.ds(pl.multiple_of(256 * n, 256), 256)
        back = dot_nt(g_ref[...], down[cols, :])
        grad = (back * slope[:, cols].astype(F32)).astype(BF16)
        slope[:, cols] = grad
        bias_rows[pl.ds(n, 1), :] = column_sum(grad.astype(F32))
        return carry

    lax.fori_loop(0, 12, hidden_back, 0)

    def up_copy(n):
        cols = pl.ds(pl.multiple_of(256 * n, 256), 256)
        slot = lax.rem(n, 2)
        return pltpu.make_async_copy(up_stage.at[slot], du_out.at[:, :, cols], local.at[6 + slot])

    def down_copy(n):
        rows = pl.ds(pl.multiple_of(256 * n, 256), 256)
        slot = lax.rem(n, 2)
        return pltpu.make_async_copy(down_stage.at[slot], dd_out.at[rows, :], local.at[8 + slot])

    def weight_grads(n, carry):
        cols = pl.ds(pl.multiple_of(256 * n, 256), 256)
        slot = lax.rem(n, 2)

        @pl.when(n >= 2)
        def _():
            up_copy(n - 2).wait()
            down_copy(n - 2).wait()

        up_grad = dot(second_t[...], slope[:, cols])
        for s in range(32):
            up_stage[slot, s] = up_grad[24 * s : 24 * s + 24].astype(BF16)
        up_copy(n).start()
        down_stage[slot] = dot_tn(act[:, cols], g_ref[...]).astype(BF16)
        down_copy(n).start()
        return carry

    lax.fori_loop(0, 12, weight_grads, 0)
    for n in (10, 11):
        up_copy(jnp.int32(n)).wait()
        down_copy(jnp.int32(n)).wait()

    for n in range(3):
        cols = pl.ds(256 * n, 256)
        base_out[:, cols] += dot(act[...], down[:, cols])
        grad_out[:, cols] = dot_nt(slope[...], uw[cols, :])
    second_grad = grad_out[...]
    wide, xhat, root = normalized(x_ref[...])
    g_wide = g_ref[...].astype(F32)
    sums_out[...] = jnp.zeros_like(sums_out)
    sums_out[2:3, :] = column_sum(second_grad * xhat)
    sums_out[3:4, :] = column_sum(second_grad)
    total = column_sum(g_wide)
    sums_out[4:5, :] = total
    sums_out[5:6, :] = total
    for f in range(4):
        for part in range(3):
            sums_out[9 + f : 10 + f, 256 * part : 256 * part + 256] = bias_rows[3 * f + part : 3 * f + part + 1, :]
    grad_out[...] = g_wide + norm_back(second_grad, vec_out[2:3, :], xhat, root)

    keep_docs.wait()
    keep_jo.wait()
    keep_heads.wait()
    for copy in docs + sends:
        copy.wait()
    for group in (a, b, c):
        group.drain()


def front(joint, output, up, down, small, x, g, tables, docs):
    any_spec, vmem = pl.BlockSpec(memory_space=pl.ANY), pl.BlockSpec(memory_space=pltpu.VMEM)
    shape = jax.ShapeDtypeStruct
    dma = pltpu.SemaphoreType.DMA
    return pl.pallas_call(
        front_kernel,
        out_shape=[
            shape((4, 512, D), BF16),
            shape((4, 8, 512), F32),
            shape((D, 3072), BF16),
            shape((32, 24, FF), BF16),
            shape((FF, D), BF16),
            shape((512, D), BF16),
            shape((16, D), F32),
            shape((512, D), F32),
            shape((512, D), F32),
            shape((16, D), F32),
        ],
        in_specs=[any_spec] * 4 + [vmem] * 7,
        out_specs=[any_spec] * 5 + [vmem] * 5,
        scratch_shapes=[
            pltpu.VMEM((24, 3328), BF16),
            pltpu.VMEM((32, 24, 3328), BF16),
            pltpu.VMEM((32, 24, FF), BF16),
            pltpu.VMEM((32, 96, D), BF16),
            pltpu.VMEM((D, 3072), BF16),
            pltpu.VMEM((D, FF), BF16),
            pltpu.VMEM((512, D), BF16),
            pltpu.VMEM((512, D), BF16),
            pltpu.VMEM((D, 512), BF16),
            pltpu.VMEM((4, 512, D), BF16),
            pltpu.VMEM((512, FF), BF16),
            pltpu.VMEM((512, FF), BF16),
            pltpu.VMEM((16, 256), F32),
            pltpu.VMEM((2, 32, 24, 256), BF16),
            pltpu.VMEM((2, 256, D), BF16),
            dma((3, 64)),
            dma((3, 64)),
            dma((3,)),
            dma((4, 3)),
            dma((4, 3)),
            dma((3,)),
            dma((3,)),
            dma((10,)),
        ],
        compiler_params=pltpu.CompilerParams(
            collective_id=1, has_side_effects=True, vmem_limit_bytes=60 << 20
        ),
        cost_estimate=pl.CostEstimate(flops=20_000_000_000, bytes_accessed=60_000_000, transcendentals=3_000_000),
        name="front",
    )(joint, output, up, down, small, x, g, *tables, docs)


HEAD_DIM = 64
ROT = 16


def rotary_tables(places):
    dim = jnp.arange(128, dtype=jnp.int32) % HEAD_DIM
    freqs = jnp.where(dim < ROT, 10000.0 ** (-2.0 * (dim % 8).astype(F32) / ROT), 0.0)
    turned = places.astype(F32)[:, None] * freqs[None, :]
    sine = jnp.sin(turned)
    return jnp.cos(turned), jnp.where(dim < 8, -sine, 0.0), jnp.where(dim >= 8, sine, 0.0)


def by_head_table(t):
    return jnp.concatenate([t, t[:, :64]], axis=1)


def pad_row(v):
    return jnp.pad(v.astype(F32), (0, 128 - v.shape[0]))[None]


def body(
    hidden_states,
    positions,
    documents,
    cotangent,
    first_gain,
    first_shift,
    second_gain,
    second_shift,
    joint_weight,
    joint_bias,
    output_weight,
    output_bias,
    up_weight,
    up_bias,
    down_weight,
    down_bias,
):
    small = jnp.concatenate(
        [
            pad_row(v)
            for v in (first_gain, first_shift, second_gain, second_shift, output_bias, down_bias, joint_bias, up_bias)
        ],
        axis=0,
    )
    tables = rotary_tables(positions[0])
    docs = jnp.broadcast_to(documents[0].astype(F32)[None], (8, 512))
    by_heads, doc_rows, jo, du, dd, first_in, vec, base, base_grad, sums = front(
        joint_weight, output_weight, up_weight, down_weight, small, hidden_states[0], cotangent[0], tables, docs
    )
    labels = doc_rows[:, 0].reshape(2048)
    by_tokens = exchange(attention(by_heads, labels), 4)
    tangent = cotangent[0]
    joint_full, output_full = jo[:, :2304], jo[:, 2304:]
    by_tokens = by_tokens.swapaxes(0, 1)
    context = by_tokens[:, :, :192].reshape(512, D)
    attn_out = jnp.dot(context, output_full, preferred_element_type=F32)
    layer_output = (base + attn_out).astype(BF16)
    output_weight_grad = jnp.einsum("td,te->de", context, tangent, preferred_element_type=F32)
    wide = by_tokens.astype(F32)
    cosine, low, high = (by_head_table(t)[:, None, :] for t in tables)

    def back(y):
        return y * cosine - jnp.roll(y, -8, axis=-1) * low - jnp.roll(y, 8, axis=-1) * high

    joint_grad = jnp.stack(
        [back(wide[:, :, 192:384]), back(wide[:, :, 384:576]), wide[:, :, 576:]], axis=1
    ).astype(BF16).reshape(512, 2304)
    joint_weight_grad = jnp.einsum("td,tc->dc", first_in, joint_grad, preferred_element_type=F32)
    joint_bias_grad = jnp.sum(joint_grad.astype(F32), axis=0)
    first_grad = jnp.einsum("tc,dc->td", joint_grad, joint_full, preferred_element_type=F32)
    states, xhat, root = normalized(hidden_states[0])
    input_grad = (base_grad + norm_back(first_grad, vec[0], xhat, root)).astype(BF16)
    small_grad = jnp.concatenate(
        [
            jnp.sum(first_grad * xhat, axis=0)[:, None],
            jnp.sum(first_grad, axis=0)[:, None],
            sums[2:6].T,
            joint_bias_grad.reshape(D, 3),
            sums[9:13].reshape(D, 4),
            jnp.zeros((D, 243), F32),
        ],
        axis=1,
    )
    pack_grad = jnp.concatenate(
        [joint_weight_grad.astype(BF16), output_weight_grad.astype(BF16), small_grad.astype(BF16)], axis=1
    )
    pack_sum, up_sum, down_sum = sum_grads(
        pack_grad.reshape(32, 24, 3328), du, dd.reshape(32, 96, D)
    )
    vector_sums = pack_sum[:, 3072:3200]
    return (
        layer_output[None],
        input_grad[None],
        vector_sums[:, 0],
        vector_sums[:, 1],
        vector_sums[:, 2],
        vector_sums[:, 3],
        pack_sum[:, :2304],
        vector_sums[:, 6:9].reshape(72),
        pack_sum[:, 2304:3072],
        vector_sums[:, 4],
        up_sum,
        vector_sums[:, 9:13].reshape(96),
        down_sum,
        vector_sums[:, 5],
    )


def solution(mesh):
    in_specs = (
        P("fsdp", "seq", None),
        P("fsdp", "seq"),
        P("fsdp", "seq"),
        P("fsdp", "seq", None),
        P("fsdp"),
        P("fsdp"),
        P("fsdp"),
        P("fsdp"),
        P("fsdp", None),
        P("fsdp"),
        P("fsdp", None),
        P("fsdp"),
        P("fsdp", None),
        P("fsdp"),
        P("fsdp", None),
        P("fsdp"),
    )
    out_specs = (
        P("fsdp", "seq", None),
        P("fsdp", "seq", None),
        P("fsdp"),
        P("fsdp"),
        P("fsdp"),
        P("fsdp"),
        P("fsdp", None),
        P("fsdp"),
        P("fsdp", None),
        P("fsdp"),
        P("fsdp", None),
        P("fsdp"),
        P("fsdp", None),
        P("fsdp"),
    )
    return jax.shard_map(body, mesh=mesh, in_specs=in_specs, out_specs=out_specs, check_vma=False)
```

```python
import functools
import jax
import jax.numpy as jnp
from jax import lax
from jax.sharding import PartitionSpec as P
from jax.experimental import pallas as pl
from jax.experimental.pallas import tpu as pltpu

MESH = pl.DeviceIdType.MESH


class Place:
    def __init__(self):
        self.seq = lax.axis_index("seq")
        self.fs = lax.axis_index("fsdp")
        self.core = lax.rem(self.seq, 2)
        self.hi = self.seq // 2
        z, xl, y = self.fs // 8, lax.rem(self.fs // 4, 2), lax.rem(self.fs, 4)
        c = self.core
        self.xl = xl
        self.pa, self.pb = y * (1 - c) + z * c, z * (1 - c) + y * c
        self.sa, self.sb = 1 + 7 * c, 8 - 7 * c

    def shard(self, da, dx, db):
        return (
            lax.rem(self.pa + da, 4) * self.sa
            + lax.rem(self.xl + dx, 2) * 4
            + lax.rem(self.pb + db, 4) * self.sb
        )

    def device(self, da, dx, db):
        return (self.seq, self.shard(da, dx, db))

    def sibling(self):
        return (self.seq + 1 - 2 * self.core, self.fs)

    def far(self, dx):
        return (self.seq + 2 - 4 * self.hi, self.shard(0, dx, 0))


def gather_partners(me):
    return [
        me.sibling(),
        me.device(0, 1, 0),
        me.device(1, 0, 0),
        me.device(3, 0, 0),
        me.device(0, 0, 1),
        me.device(0, 0, 3),
    ]


def enter(partners):
    barrier = pltpu.get_barrier_semaphore()
    for partner in partners:
        pl.semaphore_signal(barrier, inc=1, device_id=partner, device_id_type=MESH)
    pl.semaphore_wait(barrier, len(partners))


class Gather:
    def __init__(self, me, src, dst, send, recv, local):
        self.me, self.src, self.dst = me, src, dst
        self.send, self.recv, self.local = send, recv, local
        self.half = dst.shape[2] // 2
        self.sent = []
        self.cols = pl.ds(pl.multiple_of(me.core * self.half, 128), self.half)
        self.other = pl.ds(pl.multiple_of((1 - me.core) * self.half, 128), self.half)

    def slot(self, piece, cols=None):
        return self.dst.at[self.me.shard(*piece), :, self.cols if cols is None else cols]

    def key(self, piece):
        return piece[0] * 8 + piece[1] * 4 + piece[2]

    def push(self, piece, device, lands):
        own = piece == (0, 0, 0)
        src = self.src.at[:, self.cols] if own else self.slot(piece)
        copy = pltpu.make_async_remote_copy(
            src_ref=src,
            dst_ref=self.slot(piece),
            send_sem=self.send.at[len(self.sent)],
            recv_sem=self.recv.at[lands],
            device_id=device,
            device_id_type=MESH,
        )
        copy.start()
        self.sent.append(copy)

    def arrived(self, piece):
        ref = self.slot(piece)
        pltpu.make_async_copy(ref, ref, self.recv.at[self.key(piece)]).wait()
        self.push(piece, self.me.sibling(), 32 + self.key(piece))

    def ring_a(self, piece, step):
        da, dx, db = piece
        to = ((da - step) % 4, dx, db)
        self.push(piece, self.me.device(step % 4, 0, 0), self.key(to))

    def ring_b(self, piece, step):
        da, dx, db = piece
        to = (da, dx, (db - step) % 4)
        self.push(piece, self.me.device(0, 0, step % 4), self.key(to))

    def begin(self):
        self.keep = pltpu.make_async_copy(self.src, self.dst.at[self.me.fs], self.local)
        self.keep.start()
        self.push((0, 0, 0), self.me.device(0, 1, 0), self.key((0, 1, 0)))
        self.ring_a((0, 0, 0), 1)
        self.ring_a((0, 0, 0), -1)
        self.ring_b((0, 0, 0), 1)
        self.ring_b((0, 0, 0), -1)

    def spread_a(self):
        self.arrived((0, 1, 0))
        self.ring_a((0, 1, 0), 1)
        self.ring_a((0, 1, 0), -1)
        self.ring_b((0, 1, 0), 1)
        self.ring_b((0, 1, 0), -1)
        self.arrived((3, 0, 0))
        self.ring_a((3, 0, 0), 1)
        self.arrived((1, 0, 0))
        self.arrived((1, 1, 0))
        self.ring_a((1, 1, 0), -1)
        self.arrived((3, 1, 0))

    def spread_b(self):
        for da in (3, 1):
            for dx in range(2):
                self.ring_b((da, dx, 0), 1)
                self.ring_b((da, dx, 0), -1)
        for dx in range(2):
            self.arrived((2, dx, 0))
            self.ring_b((2, dx, 0), 1)
            self.ring_b((2, dx, 0), -1)

    def finish_b(self):
        for da in (0, 3, 1, 2):
            self.arrived((da, 0, 3))
            self.ring_b((da, 0, 3), 1)
            self.arrived((da, 1, 1))
            self.ring_b((da, 1, 1), -1)
            self.arrived((da, 0, 1))
            self.arrived((da, 1, 3))

    def last_b(self):
        for da in (0, 3, 1, 2):
            self.arrived((da, 0, 2))
            self.arrived((da, 1, 2))

    def settle(self):
        for da in range(4):
            for dx in range(2):
                for db in range(4):
                    if (da, dx, db) != (0, 0, 0):
                        ref = self.slot((da, dx, db), self.other)
                        pltpu.make_async_copy(ref, ref, self.recv.at[32 + db * 8 + dx * 4 + da]).wait()
        self.keep.wait()

    def drain(self):
        for copy in self.sent:
            copy.wait_send()


def total_partners(me):
    return gather_partners(me) + [me.far(0), me.far(1)]


class Total:
    def __init__(self, me, part, out, acc, sib, inbox, mine, theirs, send, recv, local):
        self.me, self.part, self.out = me, part, out
        self.acc, self.sib, self.inbox, self.mine, self.theirs = acc, sib, inbox, mine, theirs
        self.send, self.recv, self.local = send, recv, local
        self.half = part.shape[2] // 2
        self.cols = pl.ds(pl.multiple_of(me.core * self.half, 128), self.half)
        self.other = pl.ds(pl.multiple_of((1 - me.core) * self.half, 128), self.half)
        self.sent = 0

    def key(self, da, dx, db):
        return (da % 4) * 8 + dx * 4 + db % 4

    def push(self, src, dst, device, lands):
        copy = pltpu.make_async_remote_copy(
            src_ref=src,
            dst_ref=dst,
            send_sem=self.send.at[self.sent],
            recv_sem=self.recv.at[lands],
            device_id=device,
            device_id_type=MESH,
        )
        copy.start()
        self.sent += 1

    def arrived(self, ref, lands):
        pltpu.make_async_copy(ref, ref, self.recv.at[lands]).wait()

    def load(self, da, dx, db):
        k = self.key(da, dx, db)
        return pltpu.make_async_copy(
            self.part.at[self.me.shard(da, dx, db), :, self.cols], self.acc.at[k], self.local.at[k]
        )

    def begin(self):
        for da, dx, db in self.order():
            k = self.key(da, dx, db)
            self.push(
                self.part.at[self.me.shard(db, dx, da), :, self.other],
                self.sib.at[k],
                self.me.sibling(),
                k,
            )
            self.load(da, dx, db).start()

    def order(self):
        return [(da, dx, db) for db in (2, 1, 3, 0) for da in (2, 1, 3, 0) for dx in range(2)]

    def add(self, k, ref):
        self.acc[k] = (self.acc[k].astype(jnp.float32) + ref[...].astype(jnp.float32)).astype(jnp.bfloat16)

    def add_sib(self, da, dx, db):
        k = self.key(da, dx, db)
        self.load(da, dx, db).wait()
        self.arrived(self.sib.at[k], k)
        self.add(k, self.sib.at[k])

    def hop(self, piece, device, slot):
        self.push(self.acc.at[self.key(*piece)], self.inbox.at[slot], device, 32 + slot)

    def take(self, piece, slot):
        self.arrived(self.inbox.at[slot], 32 + slot)
        self.add(self.key(*piece), self.inbox.at[slot])

    def first_b(self):
        me = self.me
        up, down = me.device(0, 0, 1), me.device(0, 0, 3)
        for da in (2, 1, 3, 0):
            self.add_sib(da, 0, 2)
            self.hop((da, 0, 2), up, da * 2)
            self.add_sib(da, 1, 2)
            self.hop((da, 1, 2), down, da * 2 + 1)
        for da in (2, 1, 3, 0):
            self.add_sib(da, 1, 1)
            self.hop((da, 1, 1), up, 8 + da * 4 + 2)
            self.add_sib(da, 0, 3)
            self.hop((da, 0, 3), down, 8 + da * 4 + 1)
        for da in (2, 1, 3, 0):
            self.add_sib(da, 0, 1)
            self.add_sib(da, 1, 3)

    def second_b(self):
        me = self.me
        up, down = me.device(0, 0, 1), me.device(0, 0, 3)
        for da in (2, 1, 3, 0):
            self.take((da, 0, 1), da * 2)
            self.hop((da, 0, 1), up, 8 + da * 4)
            self.take((da, 1, 3), da * 2 + 1)
            self.hop((da, 1, 3), down, 8 + da * 4 + 3)
        for da in (2, 1, 3, 0):
            for dx in range(2):
                self.add_sib(da, dx, 0)

    def first_a(self):
        me = self.me
        up, down = me.device(1, 0, 0), me.device(3, 0, 0)
        for da in (2, 1, 3, 0):
            for dx in range(2):
                for side in range(2):
                    self.take((da, dx, 0), 8 + da * 4 + dx * 2 + side)
            if da == 2:
                self.hop((2, 0, 0), up, 24)
                self.hop((2, 1, 0), down, 25)
            if da == 1:
                self.hop((1, 1, 0), up, 28)
            if da == 3:
                self.hop((3, 0, 0), down, 27)

    def second_a(self):
        me = self.me
        self.take((1, 0, 0), 24)
        self.hop((1, 0, 0), me.device(1, 0, 0), 26)
        self.take((3, 1, 0), 25)
        self.hop((3, 1, 0), me.device(3, 0, 0), 29)

    def along_x(self):
        me = self.me
        for dx in (1, 0):
            for side in range(2):
                self.take((0, dx, 0), 26 + dx * 2 + side)
            if dx == 1:
                self.hop((0, 1, 0), me.device(0, 1, 0), 30)
                self.hop((0, 1, 0), me.far(1), 31)
        self.hop((0, 0, 0), me.far(0), 32)

    def total(self):
        for slot in (30, 31, 32):
            self.arrived(self.inbox.at[slot], 32 + slot)
        wide = lambda ref: ref[...].astype(jnp.float32)
        own = wide(self.acc.at[0]) + wide(self.inbox.at[32])
        near = wide(self.inbox.at[30]) + wide(self.inbox.at[31])
        done = (own + near).astype(jnp.bfloat16)
        self.mine[...] = done
        self.push(self.mine, self.theirs, self.me.sibling(), 65)
        self.out[:, self.cols] = done

    def end(self):
        self.arrived(self.theirs, 65)
        self.out[:, self.other] = self.theirs[...]
        for k in range(self.sent):
            pltpu.make_async_copy(self.mine, self.mine, self.send.at[k]).wait()


def total_scratch(shape):
    rows, half = shape[1], shape[2] // 2
    return [
        pltpu.VMEM((32, rows, half), jnp.bfloat16),
        pltpu.VMEM((32, rows, half), jnp.bfloat16),
        pltpu.VMEM((33, rows, half), jnp.bfloat16),
        pltpu.VMEM((rows, half), jnp.bfloat16),
        pltpu.VMEM((rows, half), jnp.bfloat16),
        pltpu.SemaphoreType.DMA((80,)),
        pltpu.SemaphoreType.DMA((66,)),
        pltpu.SemaphoreType.DMA((32,)),
    ]


def total_ticks(groups, lag=2):
    stages = ["first_b", "second_b", "first_a", "second_a", "along_x", "total"]

    def run(tick):
        for g, group in enumerate(groups):
            if 0 <= tick - lag * g < len(stages):
                getattr(group, stages[tick - lag * g])()

    count = len(stages) + lag * (len(groups) - 1) if groups else 0
    return [functools.partial(run, tick) for tick in range(count)]


BLK = 512
F32, BF16 = jnp.float32, jnp.bfloat16


def dot(a, b):
    return jnp.dot(a, b, preferred_element_type=F32)


def split_heads(x_ref, rows, s):
    q, qt, k, kt, v, vt, g, gt = s
    sl = pl.ds(rows * BLK, BLK)
    x = x_ref[rows]
    for h in range(3):
        for a, (r, t) in enumerate(((q, qt), (k, kt), (v, vt), (g, gt))):
            part = x[:, a * 192 + h * 64 : a * 192 + h * 64 + 64]
            if a == 0:
                part = part * jnp.asarray(0.125, BF16)
            r[h, sl, :] = part
            t[h, :, sl] = part.T


def wide(doc_col, j):
    return jnp.concatenate([doc_col[pl.ds(j * BLK, BLK), :]] * (BLK // 128), axis=1)


def masked(scores, i, j, doc_row, doc_col):
    if i == j:
        key = lax.broadcasted_iota(jnp.int32, (BLK, BLK), 0)
        query = lax.broadcasted_iota(jnp.int32, (BLK, BLK), 1)
        allowed = key <= query
        if i in (0, 3):
            allowed = allowed & (wide(doc_col, j) == doc_row[:, pl.ds(i * BLK, BLK)])
        return jnp.where(allowed, scores, -1e30)
    if i == 3 or j == 0:
        allowed = wide(doc_col, j) == doc_row[:, pl.ds(i * BLK, BLK)]
        return jnp.where(allowed, scores, -1e30)
    return scores


def attend_block(h, i, s, doc_row, doc_col, score, expo, dk, dv, out):
    q, qt, k, kt, v, vt, g, gt = s
    me = pl.ds(i * BLK, BLK)
    q_i, qt_i, gt_i = q[h, me, :], qt[h, :, me], gt[h, :, me]
    peak = None
    for j in range(i + 1):
        rows = pl.ds(j * BLK, BLK)
        sc = masked(dot(k[h, rows, :], qt_i), i, j, doc_row, doc_col)
        score[rows, :] = sc
        top = jnp.max(sc, axis=0, keepdims=True)
        peak = top if peak is None else jnp.maximum(peak, top)
    total, ctx = 0.0, 0.0
    for j in range(i + 1):
        rows = pl.ds(j * BLK, BLK)
        e = jnp.exp(score[rows, :] - peak)
        total = total + jnp.sum(e, axis=0, keepdims=True)
        e = e.astype(BF16)
        expo[rows, :] = e
        ctx = ctx + dot(vt[h, :, rows], e)
    inverse = 1.0 / total
    ctx = ctx * inverse
    gt_wide = gt_i.astype(F32)
    weighted = jnp.sum(ctx * gt_wide, axis=0, keepdims=True) * inverse
    scaled = (gt_wide * inverse).astype(BF16)
    scaled_rows = scaled.T
    dq = 0.0
    for j in range(i, -1, -1):
        rows = pl.ds(j * BLK, BLK)
        e = expo[rows, :]
        dp = dot(v[h, rows, :], scaled)
        ds = (e.astype(F32) * (dp - weighted)).astype(BF16)
        add_v, add_k = dot(e, scaled_rows), dot(ds, q_i)
        if i == 3:
            dv[rows, :], dk[rows, :] = add_v, add_k
        else:
            dv[rows, :] += add_v
            dk[rows, :] += add_k
        dq = dq + dot(kt[h, :, rows], ds)
    parts = [ctx.T, (dq * 0.125).T, dk[me, :], dv[me, :]]
    out[i, :, pl.ds(pl.multiple_of(256 * h, 256), 256)] = jnp.concatenate(
        [p.astype(BF16) for p in parts], axis=1
    )


def attn_scratch():
    rows, cols = pltpu.VMEM((3, 2048, 64), BF16), pltpu.VMEM((3, 64, 2048), BF16)
    return [rows, cols] * 4 + [
        pltpu.VMEM((2048, BLK), F32),
        pltpu.VMEM((2048, BLK), BF16),
        pltpu.VMEM((2048, 64), F32),
        pltpu.VMEM((2048, 64), F32),
    ]


D = 768
FF = 3072
ROWS = 128
SQRT_HALF = 0.7071067811865476
PHI_SCALE = 0.3989422804014327


def dot_nt(a, b):
    return lax.dot_general(a, b, (((1,), (1,)), ((), ())), preferred_element_type=F32)


def dot_tn(a, b):
    return lax.dot_general(a, b, (((0,), (0,)), ((), ())), preferred_element_type=F32)


def move_lane(tile, lane, source, target):
    if source != target:
        tile = pltpu.roll(tile, (target - source) % 128, axis=1)
    return jnp.where(lane == target, tile, 0.0)


def planes_to_columns(plane):
    lane = lax.broadcasted_iota(jnp.int32, (24, 128), 1)
    tiles = [plane(s) for s in range(32)]
    out = []
    for r in range(32):
        tile = jnp.where(lane < 6, tiles[r], 0.0)
        for count, base in ((3, 6), (4, 9)):
            for a in range(count):
                chunk = 32 * a + r
                tile = tile + move_lane(tiles[chunk // count], lane, base + chunk % count, base + a)
        out.append(tile)
    return jnp.concatenate(out, axis=0)


def columns_to_planes(columns):
    lane = lax.broadcasted_iota(jnp.int32, (24, 128), 1)
    tiles = [columns[24 * r : 24 * r + 24] for r in range(32)]
    out = []
    for s in range(32):
        tile = jnp.where(lane < 6, tiles[s], 0.0)
        for count, base in ((3, 6), (4, 9)):
            for c in range(count):
                chunk = count * s + c
                tile = tile + move_lane(tiles[chunk % 32], lane, base + chunk // 32, base + c)
        out.append(tile)
    return out


def join_planes(planes, out, cols):
    def pair(p, c):
        tile = jnp.concatenate(
            [planes[2 * p, :, cols].astype(F32), planes[2 * p + 1, :, cols].astype(F32)], axis=0
        )
        out[pl.ds(pl.multiple_of(48 * p, 16), 48), cols] = tile.astype(BF16)
        return c

    lax.fori_loop(0, 16, pair, 0)


def turn(x, cosine, low, high):
    n = x.shape[1]
    wide = lambda t: jnp.concatenate([t[...]] * (n // 128), axis=1)
    return (
        x * wide(cosine)
        + pltpu.roll(x, n - 8, axis=1) * wide(low)
        + pltpu.roll(x, 8, axis=1) * wide(high)
    )


def normalized(x):
    wide = x.astype(F32)
    centered = wide - jnp.mean(wide, axis=1, keepdims=True)
    root = lax.rsqrt(jnp.mean(centered * centered, axis=1, keepdims=True) + 1e-05)
    return wide, centered * root, root


def norm_back(grad, gain, xhat, root):
    scaled = grad * gain
    mean_one = jnp.mean(scaled, axis=1, keepdims=True)
    mean_two = jnp.mean(scaled * xhat, axis=1, keepdims=True)
    return root * (scaled - mean_one - xhat * mean_two)


def column_sum(x):
    return jnp.sum(x, axis=0, keepdims=True)


def front_kernel(
    joint_src, output_src, up_src, down_src, small_ref, x_ref, g_ref, cos_ref, low_ref, high_ref, doc_ref,
    heads_out, docs_out, jo_out, du_out, dd_out, first_out, vec_out, base_out, grad_out, sums_out,
    pack_src, pack_all, up_all, down_all, jo, uw, first, second, second_t, heads, act, slope,
    bias_rows, up_stage, down_stage,
    g_send, g_recv, g_local, x_send, x_recv, d_send, d_recv, local,
):
    me = Place()
    far = lax.rem(me.seq + 2, 4)
    far_sibling = far + 1 - 2 * me.core
    peers = [(far, me.fs), (far_sibling, me.fs), me.sibling()]

    loads = [
        pltpu.make_async_copy(joint_src, pack_src.at[:, pl.ds(0, 2304)], local.at[0]),
        pltpu.make_async_copy(output_src, pack_src.at[:, pl.ds(2304, D)], local.at[1]),
    ]
    for load in loads:
        load.start()
    turned = small_ref[...].T
    tile = jnp.concatenate(
        [turned[:24, :6]]
        + [turned[24 * c : 24 * c + 24, 6:7] for c in range(3)]
        + [turned[24 * c : 24 * c + 24, 7:8] for c in range(4)]
        + [jnp.zeros((24, 243), F32)],
        axis=1,
    )
    pack_src[:, 3072:] = tile.astype(BF16)
    a = Gather(me, pack_src, pack_all, g_send.at[0], g_recv.at[0], g_local.at[0])
    b = Gather(me, up_src, up_all, g_send.at[1], g_recv.at[1], g_local.at[1])
    c = Gather(me, down_src, down_all, g_send.at[2], g_recv.at[2], g_local.at[2])
    enter(gather_partners(me) + peers[:2])
    for load in loads:
        load.wait()
    a.begin()
    docs = []
    for k, peer in enumerate(peers):
        copy = pltpu.make_async_remote_copy(
            src_ref=doc_ref, dst_ref=docs_out.at[me.seq], send_sem=d_send.at[k], recv_sem=d_recv.at[k],
            device_id=peer, device_id_type=MESH,
        )
        copy.start()
        docs.append(copy)
    keep_docs = pltpu.make_async_copy(doc_ref, docs_out.at[me.seq], local.at[2])
    keep_docs.start()
    wide, xhat, root = normalized(x_ref[...])
    a.spread_a()
    b.begin()
    a.spread_b()
    b.spread_a()
    a.finish_b()
    c.begin()
    b.spread_b()
    c.spread_a()
    a.last_b()
    a.settle()

    columns = planes_to_columns(lambda s: pack_all[s, :, 3072:3200].astype(F32))
    vec = columns.T[:16]
    vec_out[...] = vec
    for f in range(4):
        for part in range(3):
            bias_rows[3 * f + part : 3 * f + part + 1, :] = vec[9 + f : 10 + f, 256 * part : 256 * part + 256]
    join_planes(pack_all, jo, pl.ds(0, 3072))
    keep_jo = pltpu.make_async_copy(jo, jo_out, local.at[3])
    keep_jo.start()
    first[...] = (xhat * vec[0:1] + vec[1:2]).astype(BF16)
    second_wide = xhat * vec[2:3] + vec[3:4]
    second[...] = second_wide.astype(BF16)
    first_out[...] = first[...]
    base_out[...] = wide + vec[4:5] + vec[5:6]

    sends = []
    for r in range(4):
        rows = pl.ds(r * ROWS, ROWS)
        tables = [t.at[rows, :] for t in (cos_ref, low_ref, high_ref)]
        x_r = first[rows, :]
        parts = []
        for n in range(2):
            y = dot(x_r, jo[:, n * D : n * D + D]) + vec[6 + n : 7 + n]
            parts.append(turn(y, *tables).astype(BF16))
        parts.append((dot(x_r, jo[:, 2 * D : 3 * D]) + vec[8:9]).astype(BF16))
        parts.append(dot_nt(g_ref[rows, :], jo[:, 3 * D :]).astype(BF16))
        for d in range(4):
            heads[d, rows, :] = jnp.concatenate([p[:, 192 * d : 192 * d + 192] for p in parts], axis=1)
        for k, peer in enumerate(peers):
            copy = pltpu.make_async_remote_copy(
                src_ref=heads.at[peer[0], rows, :], dst_ref=heads_out.at[me.seq, rows, :],
                send_sem=x_send.at[r, k], recv_sem=x_recv.at[r, k], device_id=peer, device_id_type=MESH,
            )
            copy.start()
            sends.append(copy)
        if r == 0:
            b.finish_b()
        if r == 2:
            c.spread_b()
    keep_heads = pltpu.make_async_copy(heads.at[me.seq], heads_out.at[me.seq], local.at[4])
    keep_heads.start()
    b.last_b()
    b.settle()

    join_planes(up_all, uw, pl.ds(0, FF))
    second_t[...] = second_wide.T.astype(BF16)
    c.finish_b()

    def hidden(n, carry):
        cols = pl.ds(pl.multiple_of(256 * n, 256), 256)
        h = dot(second[...], uw[:, cols]) + bias_rows[pl.ds(n, 1), :]
        half = 0.5 + 0.5 * lax.erf(h * SQRT_HALF)
        act[:, cols] = (h * half).astype(BF16)
        slope[:, cols] = (half + h * (jnp.exp(-0.5 * (h * h)) * PHI_SCALE)).astype(BF16)
        return carry

    lax.fori_loop(0, 12, hidden, 0)
    c.last_b()
    c.settle()
    down = down_all.reshape(FF, D)

    def hidden_back(n, carry):
        cols = pl.ds(pl.multiple_of(256 * n, 256), 256)
        back = dot_nt(g_ref[...], down[cols, :])
        grad = (back * slope[:, cols].astype(F32)).astype(BF16)
        slope[:, cols] = grad
        bias_rows[pl.ds(n, 1), :] = column_sum(grad.astype(F32))
        return carry

    lax.fori_loop(0, 12, hidden_back, 0)

    def up_copy(n):
        cols = pl.ds(pl.multiple_of(256 * n, 256), 256)
        slot = lax.rem(n, 2)
        return pltpu.make_async_copy(up_stage.at[slot], du_out.at[:, :, cols], local.at[6 + slot])

    def down_copy(n):
        rows = pl.ds(pl.multiple_of(256 * n, 256), 256)
        slot = lax.rem(n, 2)
        return pltpu.make_async_copy(down_stage.at[slot], dd_out.at[rows, :], local.at[8 + slot])

    def weight_grads(n, carry):
        cols = pl.ds(pl.multiple_of(256 * n, 256), 256)
        slot = lax.rem(n, 2)

        @pl.when(n >= 2)
        def _():
            up_copy(n - 2).wait()
            down_copy(n - 2).wait()

        up_grad = dot(second_t[...], slope[:, cols])
        for s in range(32):
            up_stage[slot, s] = up_grad[24 * s : 24 * s + 24].astype(BF16)
        up_copy(n).start()
        down_stage[slot] = dot_tn(act[:, cols], g_ref[...]).astype(BF16)
        down_copy(n).start()
        return carry

    lax.fori_loop(0, 12, weight_grads, 0)
    for n in (10, 11):
        up_copy(jnp.int32(n)).wait()
        down_copy(jnp.int32(n)).wait()

    for n in range(3):
        cols = pl.ds(256 * n, 256)
        base_out[:, cols] += dot(act[...], down[:, cols])
        grad_out[:, cols] = dot_nt(slope[...], uw[cols, :])
    second_grad = grad_out[...]
    wide, xhat, root = normalized(x_ref[...])
    g_wide = g_ref[...].astype(F32)
    sums_out[...] = jnp.zeros_like(sums_out)
    sums_out[2:3, :] = column_sum(second_grad * xhat)
    sums_out[3:4, :] = column_sum(second_grad)
    total = column_sum(g_wide)
    sums_out[4:5, :] = total
    sums_out[5:6, :] = total
    for f in range(4):
        for part in range(3):
            sums_out[9 + f : 10 + f, 256 * part : 256 * part + 256] = bias_rows[3 * f + part : 3 * f + part + 1, :]
    grad_out[...] = g_wide + norm_back(second_grad, vec_out[2:3, :], xhat, root)

    keep_docs.wait()
    keep_jo.wait()
    keep_heads.wait()
    for copy in docs + sends:
        copy.wait()
    for group in (a, b, c):
        group.drain()


def front(joint, output, up, down, small, x, g, tables, docs):
    any_spec, vmem = pl.BlockSpec(memory_space=pl.ANY), pl.BlockSpec(memory_space=pltpu.VMEM)
    shape = jax.ShapeDtypeStruct
    dma = pltpu.SemaphoreType.DMA
    return pl.pallas_call(
        front_kernel,
        out_shape=[
            shape((4, 512, D), BF16),
            shape((4, 8, 512), F32),
            shape((D, 3072), BF16),
            shape((32, 24, FF), BF16),
            shape((FF, D), BF16),
            shape((512, D), BF16),
            shape((16, D), F32),
            shape((512, D), F32),
            shape((512, D), F32),
            shape((16, D), F32),
        ],
        in_specs=[any_spec] * 4 + [vmem] * 7,
        out_specs=[any_spec] * 5 + [vmem] * 5,
        scratch_shapes=[
            pltpu.VMEM((24, 3328), BF16),
            pltpu.VMEM((32, 24, 3328), BF16),
            pltpu.VMEM((32, 24, FF), BF16),
            pltpu.VMEM((32, 96, D), BF16),
            pltpu.VMEM((D, 3072), BF16),
            pltpu.VMEM((D, FF), BF16),
            pltpu.VMEM((512, D), BF16),
            pltpu.VMEM((512, D), BF16),
            pltpu.VMEM((D, 512), BF16),
            pltpu.VMEM((4, 512, D), BF16),
            pltpu.VMEM((512, FF), BF16),
            pltpu.VMEM((512, FF), BF16),
            pltpu.VMEM((16, 256), F32),
            pltpu.VMEM((2, 32, 24, 256), BF16),
            pltpu.VMEM((2, 256, D), BF16),
            dma((3, 64)),
            dma((3, 64)),
            dma((3,)),
            dma((4, 3)),
            dma((4, 3)),
            dma((3,)),
            dma((3,)),
            dma((10,)),
        ],
        compiler_params=pltpu.CompilerParams(
            collective_id=1, has_side_effects=True, vmem_limit_bytes=60 << 20
        ),
        cost_estimate=pl.CostEstimate(flops=20_000_000_000, bytes_accessed=60_000_000, transcendentals=3_000_000),
        name="front",
    )(joint, output, up, down, small, x, g, *tables, docs)


SLOTS = {1: (0,), 3: (1,), 4: (2,), 6: (3,), 8: (4,), 9: (5,), 10: (6,), 11: (7,)}


def middle_kernel(
    heads_ref, docs_ref, du, dd, tokens_out, up_out, down_out, *scr
):
    attn, rest = scr[:12], scr[12:]
    s, (score, expo, dk, dv) = attn[:8], attn[8:]
    y, doc_row, doc_col, t_send, t_recv, t_local = rest[:6]
    up_scr, down_scr = rest[6:14], rest[14:22]
    me = Place()
    groups = [Total(me, du, up_out, *up_scr), Total(me, dd, down_out, *down_scr)]
    far_sibling = (lax.rem(me.seq + 2, 4) + 1 - 2 * me.core, me.fs)
    enter(total_partners(me) + [far_sibling])
    for group in groups:
        group.begin()
    for b in range(4):
        split_heads(heads_ref, b, s)
        doc_row[:, b * BLK : b * BLK + BLK] = docs_ref[b][:1]
        doc_col[b * BLK : b * BLK + BLK, :] = jnp.broadcast_to(docs_ref[b][:1], (128, BLK)).T
    ticks = total_ticks(groups)

    def columns(h):
        return pl.ds(pl.multiple_of(256 * h, 256), 256)

    def remote(h, i):
        return pltpu.make_async_remote_copy(
            src_ref=y.at[i, :, columns(h)],
            dst_ref=tokens_out.at[me.seq, :, columns(h)],
            send_sem=t_send.at[h, i],
            recv_sem=t_recv.at[h, lax.rem(i + 4 - me.seq, 4)],
            device_id=(jnp.int32(i), me.fs),
            device_id_type=MESH,
        )

    def kept(h, i):
        return pltpu.make_async_copy(y.at[i, :, columns(h)], tokens_out.at[i, :, columns(h)], t_local.at[h])

    def each(h, act):
        for i in (3, 2, 1, 0):
            pl.when(me.seq != i)(lambda i=i: act(remote(h, i), True))
            pl.when(me.seq == i)(lambda i=i: act(kept(h, i), False))

    def head(h, carry):
        for n, i in enumerate((3, 2, 1, 0)):
            attend_block(h, i, s, doc_row, doc_col, score, expo, dk, dv, y)
            pl.when(me.seq != i)(lambda: remote(h, i).start())
            pl.when(me.seq == i)(lambda: kept(h, i).start())
            for turn_of in range(3):
                for tick in SLOTS.get(4 * turn_of + n, ()):
                    pl.when(h == turn_of)(ticks[tick])
        return carry

    lax.fori_loop(0, 3, head, 0)
    for group in groups:
        group.end()
    for h in range(3):
        each(h, lambda copy, sent: copy.wait_send() if sent else copy.wait())
        for k in (1, 2, 3):
            ref = tokens_out.at[lax.rem(me.seq + 4 - k, 4), :, pl.ds(256 * h, 256)]
            pltpu.make_async_copy(ref, ref, t_recv.at[h, k]).wait()


def middle(heads, docs, du, dd):
    any_spec, vmem = pl.BlockSpec(memory_space=pl.ANY), pl.BlockSpec(memory_space=pltpu.VMEM)
    shape = jax.ShapeDtypeStruct
    dma = pltpu.SemaphoreType.DMA
    return pl.pallas_call(
        middle_kernel,
        out_shape=[shape((4, BLK, D), BF16), shape((24, FF), BF16), shape((96, D), BF16)],
        in_specs=[vmem, vmem, any_spec, any_spec],
        out_specs=[any_spec, vmem, vmem],
        scratch_shapes=attn_scratch()
        + [
            pltpu.VMEM((4, BLK, D), BF16),
            pltpu.VMEM((1, 2048), F32),
            pltpu.VMEM((2048, 128), F32),
            dma((3, 4)),
            dma((3, 4)),
            dma((3,)),
        ]
        + total_scratch((32, 24, FF))
        + total_scratch((32, 96, D)),
        compiler_params=pltpu.CompilerParams(
            collective_id=2, has_side_effects=True, vmem_limit_bytes=60 << 20
        ),
        cost_estimate=pl.CostEstimate(flops=12_000_000_000, bytes_accessed=40_000_000, transcendentals=8_000_000),
        name="middle",
    )(heads, docs, du, dd)


def back_kernel(
    tokens_ref, g_ref, jo_ref, first_ref, x_ref, base_ref, grad_ref, vec_ref, sums_ref, cos_ref, low_ref, high_ref,
    layer_out, input_out, pack_out, small_out,
    ctx, jg, part, part_small, small_sum, *scr
):
    me = Place()
    groups = [
        Total(me, part, pack_out, *scr[:8]),
        Total(me, part_small, small_sum, *scr[8:16]),
    ]
    enter(total_partners(me))
    for r in range(4):
        rows = pl.ds(r * ROWS, ROWS)
        cosine, low, high = (t[rows, :] for t in (cos_ref, low_ref, high_ref))
        tokens = [tokens_ref[s, rows, :] for s in range(4)]
        column = lambda a: jnp.concatenate(
            [t[:, 256 * h + 64 * a : 256 * h + 64 * a + 64] for t in tokens for h in range(3)], axis=1
        )
        ctx[rows, :] = column(0)
        for n in range(2):
            y = column(1 + n).astype(F32)
            jg[rows, n * D : n * D + D] = turn(y, cosine, -low, -high).astype(BF16)
        jg[rows, 2 * D :] = column(3)
    first_t = first_ref[...].astype(F32).T.astype(BF16)
    ctx_t = ctx[...].astype(F32).T.astype(BF16)
    for n in range(12):
        cols = slice(256 * n, 256 * n + 256)
        if n < 9:
            grad = dot(first_t, jg[:, cols])
        else:
            grad = dot(ctx_t, g_ref[:, 256 * n - 2304 : 256 * n - 2048])
        for s in range(32):
            part[s, :, cols] = grad[24 * s : 24 * s + 24].astype(BF16)
    groups[0].begin()
    first_grad = dot_nt(jg[...], jo_ref[:, :2304])
    wide, xhat, root = normalized(x_ref[...])
    input_out[...] = (grad_ref[...] + norm_back(first_grad, vec_ref[0:1, :], xhat, root)).astype(BF16)
    rows = jnp.concatenate(
        [column_sum(first_grad * xhat), column_sum(first_grad), sums_ref[2:6, :]]
        + [column_sum(jg[:, n * D : n * D + D].astype(F32)) for n in range(3)]
        + [sums_ref[9:13, :], jnp.zeros((115, D), F32)],
        axis=0,
    )
    for s, tile in enumerate(columns_to_planes(rows.T)):
        part_small[s, :, :128] = tile.astype(BF16)
        part_small[s, :, 128:] = jnp.zeros((24, 128), BF16)
    groups[1].begin()
    ticks = total_ticks(groups, 1)
    ticks[0]()
    layer_out[...] = (base_ref[...] + dot(ctx[...], jo_ref[:, 2304:])).astype(BF16)
    for tick in ticks[1:]:
        tick()
    for group in groups:
        group.end()
    columns = jnp.concatenate([small_sum[:, :128].astype(F32), jnp.zeros((104, 128), F32)], axis=0)
    turned = columns.T
    small_out[...] = jnp.concatenate(
        [
            turned[:6],
            jnp.concatenate([turned[6 + c : 7 + c, :24] for c in range(3)] + [jnp.zeros((1, 56), F32)], axis=1),
            jnp.concatenate([turned[9 + c : 10 + c, :24] for c in range(4)] + [jnp.zeros((1, 32), F32)], axis=1),
        ],
        axis=0,
    )


def back(tokens, g, jo, first_in, x, base, base_grad, vec, sums, tables):
    any_spec, vmem = pl.BlockSpec(memory_space=pl.ANY), pl.BlockSpec(memory_space=pltpu.VMEM)
    shape = jax.ShapeDtypeStruct
    return pl.pallas_call(
        back_kernel,
        out_shape=[shape((BLK, D), BF16), shape((BLK, D), BF16), shape((24, 3072), BF16), shape((8, 128), F32)],
        in_specs=[vmem] * 12,
        out_specs=[vmem] * 4,
        scratch_shapes=[
            pltpu.VMEM((BLK, D), BF16),
            pltpu.VMEM((BLK, 2304), BF16),
            pltpu.VMEM((32, 24, 3072), BF16),
            pltpu.VMEM((32, 24, 256), BF16),
            pltpu.VMEM((24, 256), BF16),
        ]
        + total_scratch((32, 24, 3072))
        + total_scratch((32, 24, 256)),
        compiler_params=pltpu.CompilerParams(
            collective_id=3, has_side_effects=True, vmem_limit_bytes=60 << 20
        ),
        cost_estimate=pl.CostEstimate(flops=6_000_000_000, bytes_accessed=20_000_000, transcendentals=1000),
        name="back",
    )(tokens, g, jo, first_in, x, base, base_grad, vec, sums, *tables)


HEAD_DIM = 64
ROT = 16


def rotary_tables(places):
    dim = jnp.arange(128, dtype=jnp.int32) % HEAD_DIM
    freqs = jnp.where(dim < ROT, 10000.0 ** (-2.0 * (dim % 8).astype(F32) / ROT), 0.0)
    turned = places.astype(F32)[:, None] * freqs[None, :]
    sine = jnp.sin(turned)
    return jnp.cos(turned), jnp.where(dim < 8, -sine, 0.0), jnp.where(dim >= 8, sine, 0.0)


def pad_row(v):
    return jnp.pad(v.astype(F32), (0, 128 - v.shape[0]))[None]


def body(
    hidden_states,
    positions,
    documents,
    cotangent,
    first_gain,
    first_shift,
    second_gain,
    second_shift,
    joint_weight,
    joint_bias,
    output_weight,
    output_bias,
    up_weight,
    up_bias,
    down_weight,
    down_bias,
):
    small = jnp.concatenate(
        [
            pad_row(v)
            for v in (first_gain, first_shift, second_gain, second_shift, output_bias, down_bias, joint_bias, up_bias)
        ],
        axis=0,
    )
    tables = rotary_tables(positions[0])
    docs = jnp.broadcast_to(documents[0].astype(F32)[None], (8, 512))
    by_heads, doc_rows, jo, du, dd, first_in, vec, base, base_grad, sums = front(
        joint_weight, output_weight, up_weight, down_weight, small, hidden_states[0], cotangent[0], tables, docs
    )
    tokens, up_sum, down_sum = middle(by_heads, doc_rows, du, dd.reshape(32, 96, D))
    layer_output, input_grad, pack_sum, small_sum = back(
        tokens, cotangent[0], jo, first_in, hidden_states[0], base, base_grad, vec, sums, tables
    )
    pack_sum = pack_sum.astype(F32)
    return (
        layer_output[None],
        input_grad[None],
        small_sum[0, :24],
        small_sum[1, :24],
        small_sum[2, :24],
        small_sum[3, :24],
        pack_sum[:, :2304],
        small_sum[6, :72],
        pack_sum[:, 2304:3072],
        small_sum[4, :24],
        up_sum.astype(F32),
        small_sum[7, :96],
        down_sum.astype(F32),
        small_sum[5, :24],
    )


def solution(mesh):
    in_specs = (
        P("fsdp", "seq", None),
        P("fsdp", "seq"),
        P("fsdp", "seq"),
        P("fsdp", "seq", None),
        P("fsdp"),
        P("fsdp"),
        P("fsdp"),
        P("fsdp"),
        P("fsdp", None),
        P("fsdp"),
        P("fsdp", None),
        P("fsdp"),
        P("fsdp", None),
        P("fsdp"),
        P("fsdp", None),
        P("fsdp"),
    )
    out_specs = (
        P("fsdp", "seq", None),
        P("fsdp", "seq", None),
        P("fsdp"),
        P("fsdp"),
        P("fsdp"),
        P("fsdp"),
        P("fsdp", None),
        P("fsdp"),
        P("fsdp", None),
        P("fsdp"),
        P("fsdp", None),
        P("fsdp"),
        P("fsdp", None),
        P("fsdp"),
    )
    return jax.shard_map(body, mesh=mesh, in_specs=in_specs, out_specs=out_specs, check_vma=False)
```

```python
import functools
import jax
import jax.numpy as jnp
from jax import lax
from jax.sharding import PartitionSpec as P
from jax.experimental import pallas as pl
from jax.experimental.pallas import tpu as pltpu

MESH = pl.DeviceIdType.MESH


class Place:
    def __init__(self):
        self.seq = lax.axis_index("seq")
        self.fs = lax.axis_index("fsdp")
        self.core = lax.rem(self.seq, 2)
        self.hi = self.seq // 2
        z, xl, y = self.fs // 8, lax.rem(self.fs // 4, 2), lax.rem(self.fs, 4)
        c = self.core
        self.xl = xl
        self.pa, self.pb = y * (1 - c) + z * c, z * (1 - c) + y * c
        self.sa, self.sb = 1 + 7 * c, 8 - 7 * c

    def shard(self, da, dx, db):
        return (
            lax.rem(self.pa + da, 4) * self.sa
            + lax.rem(self.xl + dx, 2) * 4
            + lax.rem(self.pb + db, 4) * self.sb
        )

    def device(self, da, dx, db):
        return (self.seq, self.shard(da, dx, db))

    def sibling(self):
        return (self.seq + 1 - 2 * self.core, self.fs)

    def far(self, dx):
        return (self.seq + 2 - 4 * self.hi, self.shard(0, dx, 0))


def gather_partners(me):
    return [
        me.sibling(),
        me.device(0, 1, 0),
        me.device(1, 0, 0),
        me.device(3, 0, 0),
        me.device(0, 0, 1),
        me.device(0, 0, 3),
    ]


def enter(partners):
    barrier = pltpu.get_barrier_semaphore()
    for partner in partners:
        pl.semaphore_signal(barrier, inc=1, device_id=partner, device_id_type=MESH)
    pl.semaphore_wait(barrier, len(partners))


class Gather:
    def __init__(self, me, src, dst, send, recv, local):
        self.me, self.src, self.dst = me, src, dst
        self.send, self.recv, self.local = send, recv, local
        self.half = dst.shape[2] // 2
        self.sent = []
        self.cols = pl.ds(pl.multiple_of(me.core * self.half, 128), self.half)
        self.other = pl.ds(pl.multiple_of((1 - me.core) * self.half, 128), self.half)

    def slot(self, piece, cols=None):
        return self.dst.at[self.me.shard(*piece), :, self.cols if cols is None else cols]

    def key(self, piece):
        return piece[0] * 8 + piece[1] * 4 + piece[2]

    def push(self, piece, device, lands):
        own = piece == (0, 0, 0)
        src = self.src.at[:, self.cols] if own else self.slot(piece)
        copy = pltpu.make_async_remote_copy(
            src_ref=src,
            dst_ref=self.slot(piece),
            send_sem=self.send.at[len(self.sent)],
            recv_sem=self.recv.at[lands],
            device_id=device,
            device_id_type=MESH,
        )
        copy.start()
        self.sent.append(copy)

    def arrived(self, piece):
        ref = self.slot(piece)
        pltpu.make_async_copy(ref, ref, self.recv.at[self.key(piece)]).wait()
        self.push(piece, self.me.sibling(), 32 + self.key(piece))

    def ring_a(self, piece, step):
        da, dx, db = piece
        to = ((da - step) % 4, dx, db)
        self.push(piece, self.me.device(step % 4, 0, 0), self.key(to))

    def ring_b(self, piece, step):
        da, dx, db = piece
        to = (da, dx, (db - step) % 4)
        self.push(piece, self.me.device(0, 0, step % 4), self.key(to))

    def begin(self):
        self.keep = pltpu.make_async_copy(self.src, self.dst.at[self.me.fs], self.local)
        self.keep.start()
        self.push((0, 0, 0), self.me.device(0, 1, 0), self.key((0, 1, 0)))
        self.ring_a((0, 0, 0), 1)
        self.ring_a((0, 0, 0), -1)
        self.ring_b((0, 0, 0), 1)
        self.ring_b((0, 0, 0), -1)

    def spread_a(self):
        self.arrived((0, 1, 0))
        self.ring_a((0, 1, 0), 1)
        self.ring_a((0, 1, 0), -1)
        self.ring_b((0, 1, 0), 1)
        self.ring_b((0, 1, 0), -1)
        self.arrived((3, 0, 0))
        self.ring_a((3, 0, 0), 1)
        self.arrived((1, 0, 0))
        self.arrived((1, 1, 0))
        self.ring_a((1, 1, 0), -1)
        self.arrived((3, 1, 0))

    def spread_b(self):
        for da in (3, 1):
            for dx in range(2):
                self.ring_b((da, dx, 0), 1)
                self.ring_b((da, dx, 0), -1)
        for dx in range(2):
            self.arrived((2, dx, 0))
            self.ring_b((2, dx, 0), 1)
            self.ring_b((2, dx, 0), -1)

    def finish_b(self, offsets=(0, 3, 1, 2)):
        for da in offsets:
            self.arrived((da, 0, 3))
            self.ring_b((da, 0, 3), 1)
            self.arrived((da, 1, 1))
            self.ring_b((da, 1, 1), -1)
            self.arrived((da, 0, 1))
            self.arrived((da, 1, 3))

    def last_b(self):
        for da in (0, 3, 1, 2):
            self.arrived((da, 0, 2))
            self.arrived((da, 1, 2))

    def settle(self):
        for da in range(4):
            for dx in range(2):
                for db in range(4):
                    if (da, dx, db) != (0, 0, 0):
                        ref = self.slot((da, dx, db), self.other)
                        pltpu.make_async_copy(ref, ref, self.recv.at[32 + db * 8 + dx * 4 + da]).wait()
        self.keep.wait()

    def drain(self):
        for copy in self.sent:
            copy.wait_send()


def total_partners(me):
    return gather_partners(me) + [me.far(0), me.far(1)]


class Total:
    def __init__(self, me, part, out, acc, sib, inbox, mine, theirs, send, recv, local, near=False):
        self.me, self.part, self.out = me, part, out
        self.acc, self.sib, self.inbox, self.mine, self.theirs = acc, sib, inbox, mine, theirs
        self.send, self.recv, self.local = send, recv, local
        self.half = part.shape[2] // 2
        self.cols = pl.ds(pl.multiple_of(me.core * self.half, 128), self.half)
        self.other = pl.ds(pl.multiple_of((1 - me.core) * self.half, 128), self.half)
        self.near = near
        self.planes = 4
        self.sent = 0

    def push(self, src, dst, device, lands):
        copy = pltpu.make_async_remote_copy(
            src_ref=src,
            dst_ref=dst,
            send_sem=self.send.at[self.sent],
            recv_sem=self.recv.at[lands],
            device_id=device,
            device_id_type=MESH,
        )
        copy.start()
        self.sent += 1

    def arrived(self, ref, lands):
        pltpu.make_async_copy(ref, ref, self.recv.at[lands]).wait()

    def plane(self, n):
        return pl.ds(8 * n, 8)

    def load(self):
        return pltpu.make_async_copy(self.part.at[:, :, self.cols], self.acc, self.local.at[0])

    def begin(self):
        for n in range(4):
            self.push(self.part.at[self.plane(n), :, self.other], self.sib.at[self.plane(n)], self.me.sibling(), n)
        if not self.near:
            self.load().start()

    def meet(self):
        for n in range(4):
            self.arrived(self.sib.at[self.plane(n)], n)
        if not self.near:
            self.load().wait()

    def at(self, da, dx, db):
        return self.me.shard(da % 4, dx, db % 4)

    def add(self, k, ref):
        self.acc[k] = self.acc[k] + ref[...]

    def add_sib(self, da, dx, db):
        k = self.at(da, dx, db)
        if self.near:
            self.acc[k] = self.part[k, :, self.cols] + self.sib[k]
        else:
            self.add(k, self.sib.at[k])

    def hop(self, piece, device, slot):
        self.push(self.acc.at[self.at(*piece)], self.inbox.at[slot], device, 32 + slot)

    def take(self, piece, slot):
        self.arrived(self.inbox.at[slot], 32 + slot)
        self.add(self.at(*piece), self.inbox.at[slot])

    def first_b(self):
        me = self.me
        up, down = me.device(0, 0, 1), me.device(0, 0, 3)
        self.meet()
        for da in (2, 1, 3, 0):
            self.add_sib(da, 0, 2)
            self.hop((da, 0, 2), up, da * 2)
            self.add_sib(da, 1, 2)
            self.hop((da, 1, 2), down, da * 2 + 1)
        for da in (2, 1, 3, 0):
            self.add_sib(da, 1, 1)
            self.hop((da, 1, 1), up, 8 + da * 4 + 2)
            self.add_sib(da, 0, 3)
            self.hop((da, 0, 3), down, 8 + da * 4 + 1)
        for da in (2, 1, 3, 0):
            self.add_sib(da, 0, 1)
            self.add_sib(da, 1, 3)

    def second_b(self):
        me = self.me
        up, down = me.device(0, 0, 1), me.device(0, 0, 3)
        for da in (2, 1, 3, 0):
            self.take((da, 0, 1), da * 2)
            self.hop((da, 0, 1), up, 8 + da * 4)
            self.take((da, 1, 3), da * 2 + 1)
            self.hop((da, 1, 3), down, 8 + da * 4 + 3)
        for da in (2, 1, 3, 0):
            for dx in range(2):
                self.add_sib(da, dx, 0)

    def first_a(self):
        me = self.me
        up, down = me.device(1, 0, 0), me.device(3, 0, 0)
        for da in (2, 1, 3, 0):
            for dx in range(2):
                for side in range(2):
                    self.take((da, dx, 0), 8 + da * 4 + dx * 2 + side)
            if da == 2:
                self.hop((2, 0, 0), up, 24)
                self.hop((2, 1, 0), down, 25)
            if da == 1:
                self.hop((1, 1, 0), up, 28)
            if da == 3:
                self.hop((3, 0, 0), down, 27)

    def second_a(self):
        me = self.me
        self.take((1, 0, 0), 24)
        self.hop((1, 0, 0), me.device(1, 0, 0), 26)
        self.take((3, 1, 0), 25)
        self.hop((3, 1, 0), me.device(3, 0, 0), 29)

    def last_a(self):
        for dx in (1, 0):
            for side in range(2):
                self.take((0, dx, 0), 26 + dx * 2 + side)

    def own(self, dx):
        return self.acc.at[self.at(0, dx, 0)]

    def along_x(self):
        me = self.me
        for slot, dx, device in ((30, 1, me.device(0, 1, 0)), (31, 1, me.far(1)), (32, 0, me.far(0))):
            self.push(self.own(dx), self.inbox.at[slot], device, 32 + slot)

    def total(self):
        for slot in (30, 31, 32):
            self.arrived(self.inbox.at[slot], 32 + slot)
        wide = lambda ref: ref[...].astype(jnp.float32)
        own = wide(self.own(0)) + wide(self.inbox.at[32])
        near = wide(self.inbox.at[30]) + wide(self.inbox.at[31])
        done = (own + near).astype(jnp.bfloat16)
        self.mine[...] = done
        self.push(self.mine, self.theirs, self.me.sibling(), 65)
        self.out[:, self.cols] = done

    def drain(self):
        for k in range(self.sent):
            ref = self.sib.at[self.plane(k)] if k < self.planes else self.mine
            pltpu.make_async_copy(ref, ref, self.send.at[k]).wait()

    def end(self):
        self.arrived(self.theirs, 65)
        self.out[:, self.other] = self.theirs[...]
        self.drain()


class Across(Total):
    def __init__(self, me, left, out, *scratch):
        super().__init__(me, left, out, left, None, *scratch)
        self.half = out.shape[1] // 2
        self.cols = pl.ds(pl.multiple_of(me.core * self.half, 128), self.half)
        self.other = pl.ds(pl.multiple_of((1 - me.core) * self.half, 128), self.half)
        self.planes = 0

    def own(self, dx):
        return self.acc.at[dx]


def total_scratch(shape):
    rows, half = shape[1], shape[2] // 2
    return [
        pltpu.VMEM((32, rows, half), jnp.bfloat16),
        pltpu.VMEM((32, rows, half), jnp.bfloat16),
        pltpu.VMEM((33, rows, half), jnp.bfloat16),
        pltpu.VMEM((rows, half), jnp.bfloat16),
        pltpu.VMEM((rows, half), jnp.bfloat16),
        pltpu.SemaphoreType.DMA((80,)),
        pltpu.SemaphoreType.DMA((66,)),
        pltpu.SemaphoreType.DMA((1,)),
    ]


RINGS = ("first_b", "second_b", "first_a", "second_a", "last_a")
CROSS = ("along_x", "total")


def total_ticks(groups, lag, stages):
    def run(tick):
        for g, group in enumerate(groups):
            if 0 <= tick - lag * g < len(stages):
                getattr(group, stages[tick - lag * g])()

    count = len(stages) + lag * (len(groups) - 1)
    return [functools.partial(run, tick) for tick in range(count)]


BLK = 512
F32, BF16 = jnp.float32, jnp.bfloat16


def dot(a, b):
    return jnp.dot(a, b, preferred_element_type=F32)


def split_heads(x_ref, rows, s):
    q, qt, k, kt, v, vt, g, gt = s
    sl = pl.ds(rows * BLK, BLK)
    x = x_ref[rows]
    for h in range(3):
        for a, (r, t) in enumerate(((q, qt), (k, kt), (v, vt), (g, gt))):
            part = x[:, a * 192 + h * 64 : a * 192 + h * 64 + 64]
            if a == 0:
                part = part * jnp.asarray(0.125, BF16)
            r[h, sl, :] = part
            t[h, :, sl] = part.T


def wide(doc_col, j):
    return jnp.concatenate([doc_col[pl.ds(j * BLK, BLK), :]] * (BLK // 128), axis=1)


def masked(scores, i, j, doc_row, doc_col):
    if i == j:
        key = lax.broadcasted_iota(jnp.int32, (BLK, BLK), 0)
        query = lax.broadcasted_iota(jnp.int32, (BLK, BLK), 1)
        allowed = key <= query
        if i in (0, 3):
            allowed = allowed & (wide(doc_col, j) == doc_row[:, pl.ds(i * BLK, BLK)])
        return jnp.where(allowed, scores, -1e30)
    if i == 3 or j == 0:
        allowed = wide(doc_col, j) == doc_row[:, pl.ds(i * BLK, BLK)]
        return jnp.where(allowed, scores, -1e30)
    return scores


def attend_block(h, i, s, doc_row, doc_col, score, expo, dk, dv, out):
    q, qt, k, kt, v, vt, g, gt = s
    me = pl.ds(i * BLK, BLK)
    q_i, qt_i, gt_i = q[h, me, :], qt[h, :, me], gt[h, :, me]
    peak = None
    for j in range(i + 1):
        rows = pl.ds(j * BLK, BLK)
        sc = masked(dot(k[h, rows, :], qt_i), i, j, doc_row, doc_col)
        score[rows, :] = sc
        top = jnp.max(sc, axis=0, keepdims=True)
        peak = top if peak is None else jnp.maximum(peak, top)
    total, ctx = 0.0, 0.0
    for j in range(i + 1):
        rows = pl.ds(j * BLK, BLK)
        e = jnp.exp(score[rows, :] - peak)
        total = total + jnp.sum(e, axis=0, keepdims=True)
        e = e.astype(BF16)
        expo[rows, :] = e
        ctx = ctx + dot(vt[h, :, rows], e)
    inverse = 1.0 / total
    ctx = ctx * inverse
    gt_wide = gt_i.astype(F32)
    weighted = jnp.sum(ctx * gt_wide, axis=0, keepdims=True) * inverse
    scaled = (gt_wide * inverse).astype(BF16)
    scaled_rows = scaled.T
    dq = 0.0
    for j in range(i, -1, -1):
        rows = pl.ds(j * BLK, BLK)
        e = expo[rows, :]
        dp = dot(v[h, rows, :], scaled)
        ds = (e.astype(F32) * (dp - weighted)).astype(BF16)
        add_v, add_k = dot(e, scaled_rows), dot(ds, q_i)
        if (i, j) in ((0, 0), (1, 1), (3, 3), (3, 2)):
            dv[rows, :], dk[rows, :] = add_v, add_k
        else:
            dv[rows, :] += add_v
            dk[rows, :] += add_k
        dq = dq + dot(kt[h, :, rows], ds)
    out[i, :, pl.ds(pl.multiple_of(256 * h, 128), 128)] = jnp.concatenate(
        [ctx.T.astype(BF16), (dq * 0.125).T.astype(BF16)], axis=1
    )


def keep_block(h, j, dk, dv, out):
    rows = pl.ds(j * BLK, BLK)
    out[j, :, pl.ds(pl.multiple_of(256 * h + 128, 128), 128)] = jnp.concatenate(
        [dk[rows, :].astype(BF16), dv[rows, :].astype(BF16)], axis=1
    )


def attn_scratch():
    rows, cols = pltpu.VMEM((3, 2048, 64), BF16), pltpu.VMEM((3, 64, 2048), BF16)
    return [rows, cols] * 4 + [
        pltpu.VMEM((2048, BLK), F32),
        pltpu.VMEM((2048, BLK), BF16),
        pltpu.VMEM((2048, 64), F32),
        pltpu.VMEM((2048, 64), F32),
    ]


D = 768
FF = 3072
ROWS = 128
SQRT_HALF = 0.7071067811865476
PHI_SCALE = 0.3989422804014327


def dot_nt(a, b):
    return lax.dot_general(a, b, (((1,), (1,)), ((), ())), preferred_element_type=F32)


def dot_tn(a, b):
    return lax.dot_general(a, b, (((0,), (0,)), ((), ())), preferred_element_type=F32)


def move_lane(tile, lane, source, target):
    if source != target:
        tile = pltpu.roll(tile, (target - source) % 128, axis=1)
    return jnp.where(lane == target, tile, 0.0)


def planes_to_columns(plane):
    lane = lax.broadcasted_iota(jnp.int32, (24, 128), 1)
    tiles = [plane(s) for s in range(32)]
    out = []
    for r in range(32):
        tile = jnp.where(lane < 6, tiles[r], 0.0)
        for count, base in ((3, 6), (4, 9)):
            for a in range(count):
                chunk = 32 * a + r
                tile = tile + move_lane(tiles[chunk // count], lane, base + chunk % count, base + a)
        out.append(tile)
    return jnp.concatenate(out, axis=0)


def columns_to_planes(columns):
    lane = lax.broadcasted_iota(jnp.int32, (24, 128), 1)
    tiles = [columns[24 * r : 24 * r + 24] for r in range(32)]
    out = []
    for s in range(32):
        tile = jnp.where(lane < 6, tiles[s], 0.0)
        for count, base in ((3, 6), (4, 9)):
            for c in range(count):
                chunk = count * s + c
                tile = tile + move_lane(tiles[chunk % 32], lane, base + chunk // 32, base + c)
        out.append(tile)
    return out


def join_planes(planes, out, cols):
    def pair(p, c):
        tile = jnp.concatenate(
            [planes[2 * p, :, cols].astype(F32), planes[2 * p + 1, :, cols].astype(F32)], axis=0
        )
        out[pl.ds(pl.multiple_of(48 * p, 16), 48), cols] = tile.astype(BF16)
        return c

    lax.fori_loop(0, 16, pair, 0)


def turn(x, cosine, low, high):
    n = x.shape[1]
    wide = lambda t: jnp.concatenate([t[...]] * (n // 128), axis=1)
    return (
        x * wide(cosine)
        + pltpu.roll(x, n - 8, axis=1) * wide(low)
        + pltpu.roll(x, 8, axis=1) * wide(high)
    )


def normalized(x):
    wide = x.astype(F32)
    centered = wide - jnp.mean(wide, axis=1, keepdims=True)
    root = lax.rsqrt(jnp.mean(centered * centered, axis=1, keepdims=True) + 1e-05)
    return wide, centered * root, root


def norm_back(grad, gain, xhat, root):
    scaled = grad * gain
    mean_one = jnp.mean(scaled, axis=1, keepdims=True)
    mean_two = jnp.mean(scaled * xhat, axis=1, keepdims=True)
    return root * (scaled - mean_one - xhat * mean_two)


def column_sum(x):
    return jnp.sum(x, axis=0, keepdims=True)


def front_kernel(
    joint_src, output_src, up_src, down_src, small_ref, x_ref, g_ref, cos_ref, low_ref, high_ref, doc_ref,
    heads_out, docs_out, jo_out, du_out, dd_out, first_out, vec_out, base_out, grad_out, sums_out,
    pack_src, pack_all, up_all, down_all, jo, uw, first, second, second_t, heads, act, slope,
    bias_rows, up_stage, down_stage,
    g_send, g_recv, g_local, x_send, x_recv, d_send, d_recv, local,
):
    me = Place()
    far = lax.rem(me.seq + 2, 4)
    far_sibling = far + 1 - 2 * me.core
    peers = [(far, me.fs), (far_sibling, me.fs), me.sibling()]

    loads = [
        pltpu.make_async_copy(joint_src, pack_src.at[:, pl.ds(0, 2304)], local.at[0]),
        pltpu.make_async_copy(output_src, pack_src.at[:, pl.ds(2304, D)], local.at[1]),
    ]
    for load in loads:
        load.start()
    turned = small_ref[...].T
    tile = jnp.concatenate(
        [turned[:24, :6]]
        + [turned[24 * c : 24 * c + 24, 6:7] for c in range(3)]
        + [turned[24 * c : 24 * c + 24, 7:8] for c in range(4)]
        + [jnp.zeros((24, 243), F32)],
        axis=1,
    )
    pack_src[:, 3072:] = tile.astype(BF16)
    a = Gather(me, pack_src, pack_all, g_send.at[0], g_recv.at[0], g_local.at[0])
    b = Gather(me, up_src, up_all, g_send.at[1], g_recv.at[1], g_local.at[1])
    c = Gather(me, down_src, down_all, g_send.at[2], g_recv.at[2], g_local.at[2])
    enter(gather_partners(me) + peers[:2])
    for load in loads:
        load.wait()
    a.begin()
    docs = []
    for k, peer in enumerate(peers):
        copy = pltpu.make_async_remote_copy(
            src_ref=doc_ref, dst_ref=docs_out.at[me.seq], send_sem=d_send.at[k], recv_sem=d_recv.at[k],
            device_id=peer, device_id_type=MESH,
        )
        copy.start()
        docs.append(copy)
    keep_docs = pltpu.make_async_copy(doc_ref, docs_out.at[me.seq], local.at[2])
    keep_docs.start()
    wide, xhat, root = normalized(x_ref[...])
    a.spread_a()
    b.begin()
    a.spread_b()
    b.spread_a()
    a.finish_b()
    c.begin()
    b.spread_b()
    c.spread_a()
    a.last_b()
    a.settle()

    columns = planes_to_columns(lambda s: pack_all[s, :, 3072:3200].astype(F32))
    vec = columns.T[:16]
    vec_out[...] = vec
    for f in range(4):
        for part in range(3):
            bias_rows[3 * f + part : 3 * f + part + 1, :] = vec[9 + f : 10 + f, 256 * part : 256 * part + 256]
    join_planes(pack_all, jo, pl.ds(0, 3072))
    keep_jo = pltpu.make_async_copy(jo, jo_out, local.at[3])
    keep_jo.start()
    first[...] = (xhat * vec[0:1] + vec[1:2]).astype(BF16)
    second_wide = xhat * vec[2:3] + vec[3:4]
    second[...] = second_wide.astype(BF16)
    first_out[...] = first[...]
    base_out[...] = wide + vec[4:5] + vec[5:6]

    sends = []
    for r in range(4):
        rows = pl.ds(r * ROWS, ROWS)
        tables = [t.at[rows, :] for t in (cos_ref, low_ref, high_ref)]
        x_r = first[rows, :]
        parts = []
        for n in range(2):
            y = dot(x_r, jo[:, n * D : n * D + D]) + vec[6 + n : 7 + n]
            parts.append(turn(y, *tables).astype(BF16))
        parts.append((dot(x_r, jo[:, 2 * D : 3 * D]) + vec[8:9]).astype(BF16))
        parts.append(dot_nt(g_ref[rows, :], jo[:, 3 * D :]).astype(BF16))
        for d in range(4):
            heads[d, rows, :] = jnp.concatenate([p[:, 192 * d : 192 * d + 192] for p in parts], axis=1)
        for k, peer in enumerate(peers):
            copy = pltpu.make_async_remote_copy(
                src_ref=heads.at[peer[0], rows, :], dst_ref=heads_out.at[me.seq, rows, :],
                send_sem=x_send.at[r, k], recv_sem=x_recv.at[r, k], device_id=peer, device_id_type=MESH,
            )
            copy.start()
            sends.append(copy)
        if r == 0:
            b.finish_b()
        if r == 2:
            c.spread_b()
    keep_heads = pltpu.make_async_copy(heads.at[me.seq], heads_out.at[me.seq], local.at[4])
    keep_heads.start()
    b.last_b()
    b.settle()

    join_planes(up_all, uw, pl.ds(0, FF))
    second_t[...] = second_wide.T.astype(BF16)

    def hidden(n, carry):
        cols = pl.ds(pl.multiple_of(256 * n, 256), 256)
        h = dot(second[...], uw[:, cols]) + bias_rows[pl.ds(n, 1), :]
        half = 0.5 + 0.5 * lax.erf(h * SQRT_HALF)
        act[:, cols] = (h * half).astype(BF16)
        slope[:, cols] = (half + h * (jnp.exp(-0.5 * (h * h)) * PHI_SCALE)).astype(BF16)
        return carry

    for n, da in enumerate((0, 3, 1, 2)):
        c.finish_b((da,))
        lax.fori_loop(3 * n, 3 * n + 3, hidden, 0)
    c.last_b()
    c.settle()
    down = down_all.reshape(FF, D)

    def hidden_back(n, carry):
        cols = pl.ds(pl.multiple_of(256 * n, 256), 256)
        back = dot_nt(g_ref[...], down[cols, :])
        grad = (back * slope[:, cols].astype(F32)).astype(BF16)
        slope[:, cols] = grad
        bias_rows[pl.ds(n, 1), :] = column_sum(grad.astype(F32))
        return carry

    lax.fori_loop(0, 12, hidden_back, 0)

    def up_copy(n):
        cols = pl.ds(pl.multiple_of(256 * n, 256), 256)
        slot = lax.rem(n, 2)
        return pltpu.make_async_copy(up_stage.at[slot], du_out.at[:, :, cols], local.at[6 + slot])

    def down_copy(n):
        rows = pl.ds(pl.multiple_of(256 * n, 256), 256)
        slot = lax.rem(n, 2)
        return pltpu.make_async_copy(down_stage.at[slot], dd_out.at[rows, :], local.at[8 + slot])

    def weight_grads(n, carry):
        cols = pl.ds(pl.multiple_of(256 * n, 256), 256)
        slot = lax.rem(n, 2)

        @pl.when(n >= 2)
        def _():
            up_copy(n - 2).wait()
            down_copy(n - 2).wait()

        up_grad = dot(second_t[...], slope[:, cols])
        for s in range(32):
            up_stage[slot, s] = up_grad[24 * s : 24 * s + 24].astype(BF16)
        up_copy(n).start()
        down_stage[slot] = dot_tn(act[:, cols], g_ref[...]).astype(BF16)
        down_copy(n).start()
        return carry

    lax.fori_loop(0, 12, weight_grads, 0)
    for n in (10, 11):
        up_copy(jnp.int32(n)).wait()
        down_copy(jnp.int32(n)).wait()

    for n in range(3):
        cols = pl.ds(256 * n, 256)
        base_out[:, cols] += dot(act[...], down[:, cols])
        grad_out[:, cols] = dot_nt(slope[...], uw[cols, :])
    second_grad = grad_out[...]
    wide, xhat, root = normalized(x_ref[...])
    g_wide = g_ref[...].astype(F32)
    sums_out[...] = jnp.zeros_like(sums_out)
    sums_out[2:3, :] = column_sum(second_grad * xhat)
    sums_out[3:4, :] = column_sum(second_grad)
    total = column_sum(g_wide)
    sums_out[4:5, :] = total
    sums_out[5:6, :] = total
    for f in range(4):
        for part in range(3):
            sums_out[9 + f : 10 + f, 256 * part : 256 * part + 256] = bias_rows[3 * f + part : 3 * f + part + 1, :]
    grad_out[...] = g_wide + norm_back(second_grad, vec_out[2:3, :], xhat, root)

    keep_docs.wait()
    keep_jo.wait()
    keep_heads.wait()
    for copy in docs + sends:
        copy.wait()
    for group in (a, b, c):
        group.drain()


def front(joint, output, up, down, small, x, g, tables, docs):
    any_spec, vmem = pl.BlockSpec(memory_space=pl.ANY), pl.BlockSpec(memory_space=pltpu.VMEM)
    shape = jax.ShapeDtypeStruct
    dma = pltpu.SemaphoreType.DMA
    return pl.pallas_call(
        front_kernel,
        out_shape=[
            shape((4, 512, D), BF16),
            shape((4, 8, 512), F32),
            shape((D, 3072), BF16),
            shape((32, 24, FF), BF16),
            shape((FF, D), BF16),
            shape((512, D), BF16),
            shape((16, D), F32),
            shape((512, D), F32),
            shape((512, D), F32),
            shape((16, D), F32),
        ],
        in_specs=[any_spec] * 4 + [vmem] * 7,
        out_specs=[any_spec] * 5 + [vmem] * 5,
        scratch_shapes=[
            pltpu.VMEM((24, 3328), BF16),
            pltpu.VMEM((32, 24, 3328), BF16),
            pltpu.VMEM((32, 24, FF), BF16),
            pltpu.VMEM((32, 96, D), BF16),
            pltpu.VMEM((D, 3072), BF16),
            pltpu.VMEM((D, FF), BF16),
            pltpu.VMEM((512, D), BF16),
            pltpu.VMEM((512, D), BF16),
            pltpu.VMEM((D, 512), BF16),
            pltpu.VMEM((4, 512, D), BF16),
            pltpu.VMEM((512, FF), BF16),
            pltpu.VMEM((512, FF), BF16),
            pltpu.VMEM((16, 256), F32),
            pltpu.VMEM((2, 32, 24, 256), BF16),
            pltpu.VMEM((2, 256, D), BF16),
            dma((3, 64)),
            dma((3, 64)),
            dma((3,)),
            dma((4, 3)),
            dma((4, 3)),
            dma((3,)),
            dma((3,)),
            dma((10,)),
        ],
        compiler_params=pltpu.CompilerParams(
            collective_id=1, has_side_effects=True, vmem_limit_bytes=60 << 20
        ),
        cost_estimate=pl.CostEstimate(flops=20_000_000_000, bytes_accessed=60_000_000, transcendentals=3_000_000),
        name="front",
    )(joint, output, up, down, small, x, g, *tables, docs)


SLOTS = {2: (0,), 4: (1,), 6: (2,), 7: (3,), 9: (4,), 10: (5,)}


def middle_kernel(
    heads_ref, docs_ref, du, dd, tokens_out, up_left, down_left, *scr
):
    attn, rest = scr[:12], scr[12:]
    s, (score, expo, dk, dv) = attn[:8], attn[8:]
    y, doc_row, doc_col, t_send, t_recv, t_local = rest[:6]
    up_scr, down_scr = rest[6:14], rest[14:22]
    me = Place()
    groups = [Total(me, du, None, *up_scr), Total(me, dd, None, *down_scr)]
    far_sibling = (lax.rem(me.seq + 2, 4) + 1 - 2 * me.core, me.fs)
    enter(total_partners(me) + [far_sibling])
    for group in groups:
        group.begin()
    for b in range(4):
        split_heads(heads_ref, b, s)
        doc_row[:, b * BLK : b * BLK + BLK] = docs_ref[b][:1]
        doc_col[b * BLK : b * BLK + BLK, :] = jnp.broadcast_to(docs_ref[b][:1], (128, BLK)).T
    ticks = total_ticks(groups, 1, RINGS)

    def columns(h, part):
        return pl.ds(pl.multiple_of(256 * h + 128 * part, 128), 128)

    def remote(h, part, i):
        return pltpu.make_async_remote_copy(
            src_ref=y.at[i, :, columns(h, part)],
            dst_ref=tokens_out.at[me.seq, :, columns(h, part)],
            send_sem=t_send.at[h, part, i],
            recv_sem=t_recv.at[h, part, lax.rem(i + 4 - me.seq, 4)],
            device_id=(jnp.int32(i), me.fs),
            device_id_type=MESH,
        )

    def kept(h, part, i):
        return pltpu.make_async_copy(
            y.at[i, :, columns(h, part)], tokens_out.at[i, :, columns(h, part)], t_local.at[h, part]
        )

    def leave(h, part, i):
        pl.when(me.seq != i)(lambda: remote(h, part, i).start())
        pl.when(me.seq == i)(lambda: kept(h, part, i).start())

    def head(h, carry):
        for n, i in enumerate((0, 1, 3, 2)):
            attend_block(h, i, s, doc_row, doc_col, score, expo, dk, dv, y)
            leave(h, 0, i)
            for j in {3: (3,), 2: (1, 2, 0)}.get(i, ()):
                keep_block(h, j, dk, dv, y)
                leave(h, 1, j)
            for turn_of in range(3):
                for tick in SLOTS.get(4 * turn_of + n, ()):
                    pl.when(h == turn_of)(ticks[tick])
        return carry

    lax.fori_loop(0, 3, head, 0)
    for group, left in zip(groups, (up_left, down_left)):
        for dx in range(2):
            left[dx] = group.own(dx)[...]
        group.drain()
    for h in range(3):
        for part in range(2):
            for i in range(4):
                pl.when(me.seq != i)(lambda: remote(h, part, i).wait_send())
                pl.when(me.seq == i)(lambda: kept(h, part, i).wait())
            for k in (1, 2, 3):
                ref = tokens_out.at[lax.rem(me.seq + 4 - k, 4), :, columns(h, part)]
                pltpu.make_async_copy(ref, ref, t_recv.at[h, part, k]).wait()


def middle(heads, docs, du, dd):
    any_spec, vmem = pl.BlockSpec(memory_space=pl.ANY), pl.BlockSpec(memory_space=pltpu.VMEM)
    shape = jax.ShapeDtypeStruct
    dma = pltpu.SemaphoreType.DMA
    return pl.pallas_call(
        middle_kernel,
        out_shape=[shape((4, BLK, D), BF16), shape((2, 24, FF // 2), BF16), shape((2, 96, D // 2), BF16)],
        in_specs=[vmem, vmem, any_spec, any_spec],
        out_specs=[any_spec, vmem, vmem],
        scratch_shapes=attn_scratch()
        + [
            pltpu.VMEM((4, BLK, D), BF16),
            pltpu.VMEM((1, 2048), F32),
            pltpu.VMEM((2048, 128), F32),
            dma((3, 2, 4)),
            dma((3, 2, 4)),
            dma((3, 2)),
        ]
        + total_scratch((32, 24, FF))
        + total_scratch((32, 96, D)),
        compiler_params=pltpu.CompilerParams(
            collective_id=2, has_side_effects=True, vmem_limit_bytes=60 << 20
        ),
        cost_estimate=pl.CostEstimate(flops=12_000_000_000, bytes_accessed=40_000_000, transcendentals=8_000_000),
        name="middle",
    )(heads, docs, du, dd)


def back_kernel(
    tokens_ref, g_ref, jo_ref, first_ref, x_ref, base_ref, grad_ref, vec_ref, sums_ref, cos_ref, low_ref, high_ref,
    up_left, down_left,
    layer_out, input_out, pack_out, small_out, up_out, down_out,
    ctx, jg, part, part_small, small_sum, *scr
):
    me = Place()
    groups = [
        Total(me, part, pack_out, *scr[:8], near=True),
        Total(me, part_small, small_sum, *scr[8:16], near=True),
    ]
    across = [Across(me, up_left, up_out, *scr[16:22]), Across(me, down_left, down_out, *scr[22:28])]
    enter(total_partners(me))
    for group in across:
        group.along_x()
    for r in range(4):
        rows = pl.ds(r * ROWS, ROWS)
        cosine, low, high = (t[rows, :] for t in (cos_ref, low_ref, high_ref))
        tokens = [tokens_ref[s, rows, :] for s in range(4)]
        column = lambda a: jnp.concatenate(
            [t[:, 256 * h + 64 * a : 256 * h + 64 * a + 64] for t in tokens for h in range(3)], axis=1
        )
        ctx[rows, :] = column(0)
        for n in range(2):
            y = column(1 + n).astype(F32)
            jg[rows, n * D : n * D + D] = turn(y, cosine, -low, -high).astype(BF16)
        jg[rows, 2 * D :] = column(3)
    first_t = first_ref[...].astype(F32).T.astype(BF16)
    ctx_t = ctx[...].astype(F32).T.astype(BF16)
    for n in range(12):
        cols = slice(256 * n, 256 * n + 256)
        if n < 9:
            grad = dot(first_t, jg[:, cols])
        else:
            grad = dot(ctx_t, g_ref[:, 256 * n - 2304 : 256 * n - 2048])
        for s in range(32):
            part[s, :, cols] = grad[24 * s : 24 * s + 24].astype(BF16)
    groups[0].begin()
    for group in across:
        group.total()
    first_grad = dot_nt(jg[...], jo_ref[:, :2304])
    wide, xhat, root = normalized(x_ref[...])
    input_out[...] = (grad_ref[...] + norm_back(first_grad, vec_ref[0:1, :], xhat, root)).astype(BF16)
    rows = jnp.concatenate(
        [column_sum(first_grad * xhat), column_sum(first_grad), sums_ref[2:6, :]]
        + [column_sum(jg[:, n * D : n * D + D].astype(F32)) for n in range(3)]
        + [sums_ref[9:13, :], jnp.zeros((115, D), F32)],
        axis=0,
    )
    for s, tile in enumerate(columns_to_planes(rows.T)):
        part_small[s, :, :128] = tile.astype(BF16)
        part_small[s, :, 128:] = jnp.zeros((24, 128), BF16)
    groups[1].begin()
    ticks = total_ticks(groups, 1, RINGS + CROSS)
    ticks[0]()
    layer_out[...] = (base_ref[...] + dot(ctx[...], jo_ref[:, 2304:])).astype(BF16)
    for tick in ticks[1:]:
        tick()
    for group in groups + across:
        group.end()
    columns = jnp.concatenate([small_sum[:, :128].astype(F32), jnp.zeros((104, 128), F32)], axis=0)
    turned = columns.T
    small_out[...] = jnp.concatenate(
        [
            turned[:6],
            jnp.concatenate([turned[6 + c : 7 + c, :24] for c in range(3)] + [jnp.zeros((1, 56), F32)], axis=1),
            jnp.concatenate([turned[9 + c : 10 + c, :24] for c in range(4)] + [jnp.zeros((1, 32), F32)], axis=1),
        ],
        axis=0,
    )


def back(tokens, g, jo, first_in, x, base, base_grad, vec, sums, tables, up_left, down_left):
    any_spec, vmem = pl.BlockSpec(memory_space=pl.ANY), pl.BlockSpec(memory_space=pltpu.VMEM)
    shape = jax.ShapeDtypeStruct
    return pl.pallas_call(
        back_kernel,
        out_shape=[shape((BLK, D), BF16), shape((BLK, D), BF16), shape((24, 3072), BF16), shape((8, 128), F32), shape((24, FF), BF16), shape((96, D), BF16)],
        in_specs=[vmem] * 14,
        out_specs=[vmem] * 6,
        scratch_shapes=[
            pltpu.VMEM((BLK, D), BF16),
            pltpu.VMEM((BLK, 2304), BF16),
            pltpu.VMEM((32, 24, 3072), BF16),
            pltpu.VMEM((32, 24, 256), BF16),
            pltpu.VMEM((24, 256), BF16),
        ]
        + total_scratch((32, 24, 3072))
        + total_scratch((32, 24, 256))
        + total_scratch((32, 24, FF))[2:]
        + total_scratch((32, 96, D))[2:],
        compiler_params=pltpu.CompilerParams(
            collective_id=3, has_side_effects=True, vmem_limit_bytes=60 << 20
        ),
        cost_estimate=pl.CostEstimate(flops=6_000_000_000, bytes_accessed=20_000_000, transcendentals=1000),
        name="back",
    )(tokens, g, jo, first_in, x, base, base_grad, vec, sums, *tables, up_left, down_left)


HEAD_DIM = 64
ROT = 16


def rotary_tables(places):
    dim = jnp.arange(128, dtype=jnp.int32) % HEAD_DIM
    freqs = jnp.where(dim < ROT, 10000.0 ** (-2.0 * (dim % 8).astype(F32) / ROT), 0.0)
    turned = places.astype(F32)[:, None] * freqs[None, :]
    sine = jnp.sin(turned)
    return jnp.cos(turned), jnp.where(dim < 8, -sine, 0.0), jnp.where(dim >= 8, sine, 0.0)


def pad_row(v):
    return jnp.pad(v.astype(F32), (0, 128 - v.shape[0]))[None]


def finish_kernel(pack, up, down, small, layer, grad, *outs):
    joint_out, output_out, up_out, down_out, layer_out, grad_out = outs[:6]
    layer_out[...] = layer[...]
    grad_out[...] = grad[...]
    joint_out[...] = pack[:, :2304].astype(F32)
    output_out[...] = pack[:, 2304:].astype(F32)
    up_out[...] = up[...].astype(F32)
    down_out[...] = down[...].astype(F32)
    for n, out in enumerate(outs[6:]):
        out[...] = small[n, : out.shape[0]]


def finish(pack, up, down, small, layer, grad):
    shape = jax.ShapeDtypeStruct
    return pl.pallas_call(
        finish_kernel,
        out_shape=[shape(s, F32) for s in ((24, 2304), (24, D), (24, FF), (96, D))]
        + [shape((BLK, D), BF16)] * 2
        + [shape((n,), F32) for n in (24, 24, 24, 24, 24, 24, 72, 96)],
        in_specs=[pl.BlockSpec(memory_space=pltpu.VMEM)] * 6,
        out_specs=[pl.BlockSpec(memory_space=pltpu.VMEM)] * 14,
        name="finish",
    )(pack, up, down, small, layer, grad)


def body(
    hidden_states,
    positions,
    documents,
    cotangent,
    first_gain,
    first_shift,
    second_gain,
    second_shift,
    joint_weight,
    joint_bias,
    output_weight,
    output_bias,
    up_weight,
    up_bias,
    down_weight,
    down_bias,
):
    small = jnp.concatenate(
        [
            pad_row(v)
            for v in (first_gain, first_shift, second_gain, second_shift, output_bias, down_bias, joint_bias, up_bias)
        ],
        axis=0,
    )
    tables = rotary_tables(positions[0])
    docs = jnp.broadcast_to(documents[0].astype(F32)[None], (8, 512))
    by_heads, doc_rows, jo, du, dd, first_in, vec, base, base_grad, sums = front(
        joint_weight, output_weight, up_weight, down_weight, small, hidden_states[0], cotangent[0], tables, docs
    )
    tokens, up_left, down_left = middle(by_heads, doc_rows, du, dd.reshape(32, 96, D))
    layer_output, input_grad, pack_sum, small_sum, up_sum, down_sum = back(
        tokens, cotangent[0], jo, first_in, hidden_states[0], base, base_grad, vec, sums, tables, up_left, down_left
    )
    (
        joint_sum, output_sum, up_total, down_total, layer_output, input_grad,
        gain_one, shift_one, gain_two, shift_two, output_shift, down_shift, joint_shift, up_shift,
    ) = finish(
        pack_sum, up_sum, down_sum, small_sum, layer_output, input_grad
    )
    return (
        layer_output[None],
        input_grad[None],
        gain_one,
        shift_one,
        gain_two,
        shift_two,
        joint_sum,
        joint_shift,
        output_sum,
        output_shift,
        up_total,
        up_shift,
        down_total,
        down_shift,
    )


def solution(mesh):
    in_specs = (
        P("fsdp", "seq", None),
        P("fsdp", "seq"),
        P("fsdp", "seq"),
        P("fsdp", "seq", None),
        P("fsdp"),
        P("fsdp"),
        P("fsdp"),
        P("fsdp"),
        P("fsdp", None),
        P("fsdp"),
        P("fsdp", None),
        P("fsdp"),
        P("fsdp", None),
        P("fsdp"),
        P("fsdp", None),
        P("fsdp"),
    )
    out_specs = (
        P("fsdp", "seq", None),
        P("fsdp", "seq", None),
        P("fsdp"),
        P("fsdp"),
        P("fsdp"),
        P("fsdp"),
        P("fsdp", None),
        P("fsdp"),
        P("fsdp", None),
        P("fsdp"),
        P("fsdp", None),
        P("fsdp"),
        P("fsdp", None),
        P("fsdp"),
    )
    return jax.shard_map(body, mesh=mesh, in_specs=in_specs, out_specs=out_specs, check_vma=False)
```

```python
import functools
import jax
import jax.numpy as jnp
from jax import lax
from jax.sharding import PartitionSpec as P
from jax.experimental import pallas as pl
from jax.experimental.pallas import tpu as pltpu

MESH = pl.DeviceIdType.MESH


class Place:
    def __init__(self):
        self.seq = lax.axis_index("seq")
        self.fs = lax.axis_index("fsdp")
        self.core = lax.rem(self.seq, 2)
        self.hi = self.seq // 2
        z, xl, y = self.fs // 8, lax.rem(self.fs // 4, 2), lax.rem(self.fs, 4)
        c = self.core
        self.xl = xl
        self.pa, self.pb = y * (1 - c) + z * c, z * (1 - c) + y * c
        self.sa, self.sb = 1 + 7 * c, 8 - 7 * c

    def shard(self, da, dx, db):
        return (
            lax.rem(self.pa + da, 4) * self.sa
            + lax.rem(self.xl + dx, 2) * 4
            + lax.rem(self.pb + db, 4) * self.sb
        )

    def device(self, da, dx, db):
        return (self.seq, self.shard(da, dx, db))

    def sibling(self):
        return (self.seq + 1 - 2 * self.core, self.fs)

    def far(self, dx):
        return (self.seq + 2 - 4 * self.hi, self.shard(0, dx, 0))


def gather_partners(me):
    return [
        me.sibling(),
        me.device(0, 1, 0),
        me.device(1, 0, 0),
        me.device(3, 0, 0),
        me.device(0, 0, 1),
        me.device(0, 0, 3),
    ]


def enter(partners):
    barrier = pltpu.get_barrier_semaphore()
    for partner in partners:
        pl.semaphore_signal(barrier, inc=1, device_id=partner, device_id_type=MESH)
    pl.semaphore_wait(barrier, len(partners))


class Gather:
    def __init__(self, me, src, dst, send, recv, local):
        self.me, self.src, self.dst = me, src, dst
        self.send, self.recv, self.local = send, recv, local
        self.half = dst.shape[2] // 2
        self.sent = []
        self.cols = pl.ds(pl.multiple_of(me.core * self.half, 128), self.half)
        self.other = pl.ds(pl.multiple_of((1 - me.core) * self.half, 128), self.half)

    def slot(self, piece, cols=None):
        return self.dst.at[self.me.shard(*piece), :, self.cols if cols is None else cols]

    def key(self, piece):
        return piece[0] * 8 + piece[1] * 4 + piece[2]

    def push(self, piece, device, lands):
        own = piece == (0, 0, 0)
        src = self.src.at[:, self.cols] if own else self.slot(piece)
        copy = pltpu.make_async_remote_copy(
            src_ref=src,
            dst_ref=self.slot(piece),
            send_sem=self.send.at[len(self.sent)],
            recv_sem=self.recv.at[lands],
            device_id=device,
            device_id_type=MESH,
        )
        copy.start()
        self.sent.append(copy)

    def arrived(self, piece):
        ref = self.slot(piece)
        pltpu.make_async_copy(ref, ref, self.recv.at[self.key(piece)]).wait()
        self.push(piece, self.me.sibling(), 32 + self.key(piece))

    def ring_a(self, piece, step):
        da, dx, db = piece
        to = ((da - step) % 4, dx, db)
        self.push(piece, self.me.device(step % 4, 0, 0), self.key(to))

    def ring_b(self, piece, step):
        da, dx, db = piece
        to = (da, dx, (db - step) % 4)
        self.push(piece, self.me.device(0, 0, step % 4), self.key(to))

    def begin(self):
        self.keep = pltpu.make_async_copy(self.src, self.dst.at[self.me.fs], self.local)
        self.keep.start()
        self.push((0, 0, 0), self.me.device(0, 1, 0), self.key((0, 1, 0)))
        self.ring_a((0, 0, 0), 1)
        self.ring_a((0, 0, 0), -1)
        self.ring_b((0, 0, 0), 1)
        self.ring_b((0, 0, 0), -1)

    def spread_a(self):
        self.arrived((0, 1, 0))
        self.ring_a((0, 1, 0), 1)
        self.ring_a((0, 1, 0), -1)
        self.ring_b((0, 1, 0), 1)
        self.ring_b((0, 1, 0), -1)
        self.arrived((3, 0, 0))
        self.ring_a((3, 0, 0), 1)
        self.arrived((1, 0, 0))
        self.arrived((1, 1, 0))
        self.ring_a((1, 1, 0), -1)
        self.arrived((3, 1, 0))

    def spread_b(self):
        for da in (3, 1):
            for dx in range(2):
                self.ring_b((da, dx, 0), 1)
                self.ring_b((da, dx, 0), -1)
        for dx in range(2):
            self.arrived((2, dx, 0))
            self.ring_b((2, dx, 0), 1)
            self.ring_b((2, dx, 0), -1)

    def finish_b(self, offsets=(0, 3, 1, 2)):
        for da in offsets:
            self.arrived((da, 0, 3))
            self.ring_b((da, 0, 3), 1)
            self.arrived((da, 1, 1))
            self.ring_b((da, 1, 1), -1)
            self.arrived((da, 0, 1))
            self.arrived((da, 1, 3))

    def last_b(self):
        for da in (0, 3, 1, 2):
            self.arrived((da, 0, 2))
            self.arrived((da, 1, 2))

    def settle(self):
        for da in range(4):
            for dx in range(2):
                for db in range(4):
                    if (da, dx, db) != (0, 0, 0):
                        ref = self.slot((da, dx, db), self.other)
                        pltpu.make_async_copy(ref, ref, self.recv.at[32 + db * 8 + dx * 4 + da]).wait()
        self.keep.wait()

    def drain(self):
        for copy in self.sent:
            copy.wait_send()


def total_partners(me):
    return gather_partners(me) + [me.far(0), me.far(1)]


class Total:
    def __init__(self, me, part, out, acc, sib, inbox, mine, theirs, send, recv, local, near=False):
        self.me, self.part, self.out = me, part, out
        self.acc, self.sib, self.inbox, self.mine, self.theirs = acc, sib, inbox, mine, theirs
        self.send, self.recv, self.local = send, recv, local
        self.half = part.shape[2] // 2
        self.cols = pl.ds(pl.multiple_of(me.core * self.half, 128), self.half)
        self.other = pl.ds(pl.multiple_of((1 - me.core) * self.half, 128), self.half)
        self.near = near
        self.planes = 4
        self.sent = 0

    def push(self, src, dst, device, lands):
        copy = pltpu.make_async_remote_copy(
            src_ref=src,
            dst_ref=dst,
            send_sem=self.send.at[self.sent],
            recv_sem=self.recv.at[lands],
            device_id=device,
            device_id_type=MESH,
        )
        copy.start()
        self.sent += 1

    def arrived(self, ref, lands):
        pltpu.make_async_copy(ref, ref, self.recv.at[lands]).wait()

    def plane(self, n):
        return pl.ds(8 * n, 8)

    def load(self):
        return pltpu.make_async_copy(self.part.at[:, :, self.cols], self.acc, self.local.at[0])

    def begin(self):
        for n in range(4):
            self.push(self.part.at[self.plane(n), :, self.other], self.sib.at[self.plane(n)], self.me.sibling(), n)
        if not self.near:
            self.load().start()

    def meet(self):
        for n in range(4):
            self.arrived(self.sib.at[self.plane(n)], n)
        if not self.near:
            self.load().wait()

    def at(self, da, dx, db):
        return self.me.shard(da % 4, dx, db % 4)

    def add(self, k, ref):
        self.acc[k] = self.acc[k] + ref[...]

    def add_sib(self, da, dx, db):
        k = self.at(da, dx, db)
        if self.near:
            self.acc[k] = self.part[k, :, self.cols] + self.sib[k]
        else:
            self.add(k, self.sib.at[k])

    def hop(self, piece, device, slot):
        self.push(self.acc.at[self.at(*piece)], self.inbox.at[slot], device, 32 + slot)

    def take(self, piece, slot):
        self.arrived(self.inbox.at[slot], 32 + slot)
        self.add(self.at(*piece), self.inbox.at[slot])

    def first_b(self):
        me = self.me
        up, down = me.device(0, 0, 1), me.device(0, 0, 3)
        self.meet()
        for da in (2, 1, 3, 0):
            self.add_sib(da, 0, 2)
            self.hop((da, 0, 2), up, da * 2)
            self.add_sib(da, 1, 2)
            self.hop((da, 1, 2), down, da * 2 + 1)
        for da in (2, 1, 3, 0):
            self.add_sib(da, 1, 1)
            self.hop((da, 1, 1), up, 8 + da * 4 + 2)
            self.add_sib(da, 0, 3)
            self.hop((da, 0, 3), down, 8 + da * 4 + 1)
        for da in (2, 1, 3, 0):
            self.add_sib(da, 0, 1)
            self.add_sib(da, 1, 3)

    def second_b(self):
        me = self.me
        up, down = me.device(0, 0, 1), me.device(0, 0, 3)
        for da in (2, 1, 3, 0):
            self.take((da, 0, 1), da * 2)
            self.hop((da, 0, 1), up, 8 + da * 4)
            self.take((da, 1, 3), da * 2 + 1)
            self.hop((da, 1, 3), down, 8 + da * 4 + 3)
        for da in (2, 1, 3, 0):
            for dx in range(2):
                self.add_sib(da, dx, 0)

    def first_a(self):
        me = self.me
        up, down = me.device(1, 0, 0), me.device(3, 0, 0)
        for da in (2, 1, 3, 0):
            for dx in range(2):
                for side in range(2):
                    self.take((da, dx, 0), 8 + da * 4 + dx * 2 + side)
            if da == 2:
                self.hop((2, 0, 0), up, 24)
                self.hop((2, 1, 0), down, 25)
            if da == 1:
                self.hop((1, 1, 0), up, 28)
            if da == 3:
                self.hop((3, 0, 0), down, 27)

    def second_a(self):
        me = self.me
        self.take((1, 0, 0), 24)
        self.hop((1, 0, 0), me.device(1, 0, 0), 26)
        self.take((3, 1, 0), 25)
        self.hop((3, 1, 0), me.device(3, 0, 0), 29)

    def last_a(self):
        for dx in (1, 0):
            for side in range(2):
                self.take((0, dx, 0), 26 + dx * 2 + side)

    def own(self, dx):
        return self.acc.at[self.at(0, dx, 0)]

    def along_x(self):
        me = self.me
        for slot, dx, device in ((30, 1, me.device(0, 1, 0)), (31, 1, me.far(1)), (32, 0, me.far(0))):
            self.push(self.own(dx), self.inbox.at[slot], device, 32 + slot)

    def total(self):
        for slot in (30, 31, 32):
            self.arrived(self.inbox.at[slot], 32 + slot)
        wide = lambda ref: ref[...].astype(jnp.float32)
        own = wide(self.own(0)) + wide(self.inbox.at[32])
        near = wide(self.inbox.at[30]) + wide(self.inbox.at[31])
        done = (own + near).astype(jnp.bfloat16)
        self.mine[...] = done
        self.push(self.mine, self.theirs, self.me.sibling(), 65)
        self.out[:, self.cols] = done

    def drain(self):
        for k in range(self.sent):
            ref = self.sib.at[self.plane(k)] if k < self.planes else self.mine
            pltpu.make_async_copy(ref, ref, self.send.at[k]).wait()

    def end(self):
        self.arrived(self.theirs, 65)
        self.out[:, self.other] = self.theirs[...]
        self.drain()


class Across(Total):
    def __init__(self, me, left, out, *scratch):
        super().__init__(me, left, out, left, None, *scratch)
        self.half = out.shape[1] // 2
        self.cols = pl.ds(pl.multiple_of(me.core * self.half, 128), self.half)
        self.other = pl.ds(pl.multiple_of((1 - me.core) * self.half, 128), self.half)
        self.planes = 0

    def own(self, dx):
        return self.acc.at[dx]


def total_scratch(shape):
    rows, half = shape[1], shape[2] // 2
    return [
        pltpu.VMEM((32, rows, half), jnp.bfloat16),
        pltpu.VMEM((32, rows, half), jnp.bfloat16),
        pltpu.VMEM((33, rows, half), jnp.bfloat16),
        pltpu.VMEM((rows, half), jnp.bfloat16),
        pltpu.VMEM((rows, half), jnp.bfloat16),
        pltpu.SemaphoreType.DMA((80,)),
        pltpu.SemaphoreType.DMA((66,)),
        pltpu.SemaphoreType.DMA((1,)),
    ]


RINGS = ("first_b", "second_b", "first_a", "second_a", "last_a")
CROSS = ("along_x", "total")


def total_ticks(groups, lag, stages):
    def run(tick):
        for g, group in enumerate(groups):
            if 0 <= tick - lag * g < len(stages):
                getattr(group, stages[tick - lag * g])()

    count = len(stages) + lag * (len(groups) - 1)
    return [functools.partial(run, tick) for tick in range(count)]


BLK = 512
F32, BF16 = jnp.float32, jnp.bfloat16


def dot(a, b):
    return jnp.dot(a, b, preferred_element_type=F32)


def split_heads(x_ref, rows, s):
    q, qt, k, kt, v, vt, g, gt = s
    sl = pl.ds(rows * BLK, BLK)
    x = x_ref[rows]
    for h in range(3):
        for a, (r, t) in enumerate(((q, qt), (k, kt), (v, vt), (g, gt))):
            part = x[:, a * 192 + h * 64 : a * 192 + h * 64 + 64]
            if a == 0:
                part = part * jnp.asarray(0.125, BF16)
            r[h, sl, :] = part
            t[h, :, sl] = part.T


def wide(doc_col, j):
    return jnp.concatenate([doc_col[pl.ds(j * BLK, BLK), :]] * (BLK // 128), axis=1)


def masked(scores, i, j, doc_row, doc_col):
    if i == j:
        key = lax.broadcasted_iota(jnp.int32, (BLK, BLK), 0)
        query = lax.broadcasted_iota(jnp.int32, (BLK, BLK), 1)
        allowed = key <= query
        if i in (0, 3):
            allowed = allowed & (wide(doc_col, j) == doc_row[:, pl.ds(i * BLK, BLK)])
        return jnp.where(allowed, scores, -1e30)
    if i == 3 or j == 0:
        allowed = wide(doc_col, j) == doc_row[:, pl.ds(i * BLK, BLK)]
        return jnp.where(allowed, scores, -1e30)
    return scores


def attend_block(h, i, s, doc_row, doc_col, score, expo, dk, dv, out):
    q, qt, k, kt, v, vt, g, gt = s
    me = pl.ds(i * BLK, BLK)
    q_i, qt_i, gt_i = q[h, me, :], qt[h, :, me], gt[h, :, me]
    peak = None
    for j in range(i + 1):
        rows = pl.ds(j * BLK, BLK)
        sc = masked(dot(k[h, rows, :], qt_i), i, j, doc_row, doc_col)
        score[rows, :] = sc
        top = jnp.max(sc, axis=0, keepdims=True)
        peak = top if peak is None else jnp.maximum(peak, top)
    total, ctx = 0.0, 0.0
    for j in range(i + 1):
        rows = pl.ds(j * BLK, BLK)
        e = jnp.exp(score[rows, :] - peak)
        total = total + jnp.sum(e, axis=0, keepdims=True)
        e = e.astype(BF16)
        expo[rows, :] = e
        ctx = ctx + dot(vt[h, :, rows], e)
    inverse = 1.0 / total
    ctx = ctx * inverse
    gt_wide = gt_i.astype(F32)
    weighted = jnp.sum(ctx * gt_wide, axis=0, keepdims=True) * inverse
    scaled = (gt_wide * inverse).astype(BF16)
    scaled_rows = scaled.T
    dq = 0.0
    for j in range(i, -1, -1):
        rows = pl.ds(j * BLK, BLK)
        e = expo[rows, :]
        dp = dot(v[h, rows, :], scaled)
        ds = (e.astype(F32) * (dp - weighted)).astype(BF16)
        add_v, add_k = dot(e, scaled_rows), dot(ds, q_i)
        if (i, j) in ((0, 0), (1, 1), (3, 3), (3, 2)):
            dv[rows, :], dk[rows, :] = add_v, add_k
        else:
            dv[rows, :] += add_v
            dk[rows, :] += add_k
        dq = dq + dot(kt[h, :, rows], ds)
    out[i, :, pl.ds(pl.multiple_of(256 * h, 128), 128)] = jnp.concatenate(
        [ctx.T.astype(BF16), (dq * 0.125).T.astype(BF16)], axis=1
    )


def keep_block(h, j, dk, dv, out):
    rows = pl.ds(j * BLK, BLK)
    out[j, :, pl.ds(pl.multiple_of(256 * h + 128, 128), 128)] = jnp.concatenate(
        [dk[rows, :].astype(BF16), dv[rows, :].astype(BF16)], axis=1
    )


def attn_scratch():
    rows, cols = pltpu.VMEM((3, 2048, 64), BF16), pltpu.VMEM((3, 64, 2048), BF16)
    return [rows, cols] * 4 + [
        pltpu.VMEM((2048, BLK), F32),
        pltpu.VMEM((2048, BLK), BF16),
        pltpu.VMEM((2048, 64), F32),
        pltpu.VMEM((2048, 64), F32),
    ]


D = 768
FF = 3072
ROWS = 128
SQRT_HALF = 0.7071067811865476
PHI_SCALE = 0.3989422804014327


def dot_nt(a, b):
    return lax.dot_general(a, b, (((1,), (1,)), ((), ())), preferred_element_type=F32)


def dot_tn(a, b):
    return lax.dot_general(a, b, (((0,), (0,)), ((), ())), preferred_element_type=F32)


def move_lane(tile, lane, source, target):
    if source != target:
        tile = pltpu.roll(tile, (target - source) % 128, axis=1)
    return jnp.where(lane == target, tile, 0.0)


def planes_to_columns(plane):
    lane = lax.broadcasted_iota(jnp.int32, (24, 128), 1)
    tiles = [plane(s) for s in range(32)]
    out = []
    for r in range(32):
        tile = jnp.where(lane < 6, tiles[r], 0.0)
        for count, base in ((3, 6), (4, 9)):
            for a in range(count):
                chunk = 32 * a + r
                tile = tile + move_lane(tiles[chunk // count], lane, base + chunk % count, base + a)
        out.append(tile)
    return jnp.concatenate(out, axis=0)


def columns_to_planes(columns):
    lane = lax.broadcasted_iota(jnp.int32, (24, 128), 1)
    tiles = [columns[24 * r : 24 * r + 24] for r in range(32)]
    out = []
    for s in range(32):
        tile = jnp.where(lane < 6, tiles[s], 0.0)
        for count, base in ((3, 6), (4, 9)):
            for c in range(count):
                chunk = count * s + c
                tile = tile + move_lane(tiles[chunk % 32], lane, base + chunk // 32, base + c)
        out.append(tile)
    return out


def join_planes(planes, out, cols):
    def pair(p, c):
        tile = jnp.concatenate(
            [planes[2 * p, :, cols].astype(F32), planes[2 * p + 1, :, cols].astype(F32)], axis=0
        )
        out[pl.ds(pl.multiple_of(48 * p, 16), 48), cols] = tile.astype(BF16)
        return c

    lax.fori_loop(0, 16, pair, 0)


def turn(x, cosine, low, high):
    n = x.shape[1]
    wide = lambda t: jnp.concatenate([t[...]] * (n // 128), axis=1)
    return (
        x * wide(cosine)
        + pltpu.roll(x, n - 8, axis=1) * wide(low)
        + pltpu.roll(x, 8, axis=1) * wide(high)
    )


def normalized(x):
    wide = x.astype(F32)
    centered = wide - jnp.mean(wide, axis=1, keepdims=True)
    root = lax.rsqrt(jnp.mean(centered * centered, axis=1, keepdims=True) + 1e-05)
    return wide, centered * root, root


def norm_back(grad, gain, xhat, root):
    scaled = grad * gain
    mean_one = jnp.mean(scaled, axis=1, keepdims=True)
    mean_two = jnp.mean(scaled * xhat, axis=1, keepdims=True)
    return root * (scaled - mean_one - xhat * mean_two)


def column_sum(x):
    return jnp.sum(x, axis=0, keepdims=True)


def front_kernel(
    joint_src, output_src, up_src, down_src, small_ref, x_ref, g_ref, cos_ref, low_ref, high_ref, doc_ref,
    heads_out, docs_out, jo_out, du_out, dd_out, first_out, vec_out, base_out, grad_out, sums_out,
    pack_src, pack_all, up_all, down_all, jo, uw, first, second, second_t, heads, act, slope,
    bias_rows, up_stage, down_stage,
    g_send, g_recv, g_local, x_send, x_recv, d_send, d_recv, local,
):
    me = Place()
    far = lax.rem(me.seq + 2, 4)
    far_sibling = far + 1 - 2 * me.core
    peers = [(far, me.fs), (far_sibling, me.fs), me.sibling()]

    loads = [
        pltpu.make_async_copy(joint_src, pack_src.at[:, pl.ds(0, 2304)], local.at[0]),
        pltpu.make_async_copy(output_src, pack_src.at[:, pl.ds(2304, D)], local.at[1]),
    ]
    for load in loads:
        load.start()
    turned = small_ref[...].T
    tile = jnp.concatenate(
        [turned[:24, :6]]
        + [turned[24 * c : 24 * c + 24, 6:7] for c in range(3)]
        + [turned[24 * c : 24 * c + 24, 7:8] for c in range(4)]
        + [jnp.zeros((24, 243), F32)],
        axis=1,
    )
    pack_src[:, 3072:] = tile.astype(BF16)
    a = Gather(me, pack_src, pack_all, g_send.at[0], g_recv.at[0], g_local.at[0])
    b = Gather(me, up_src, up_all, g_send.at[1], g_recv.at[1], g_local.at[1])
    c = Gather(me, down_src, down_all, g_send.at[2], g_recv.at[2], g_local.at[2])
    enter(gather_partners(me) + peers[:2])
    for load in loads:
        load.wait()
    a.begin()
    docs = []
    for k, peer in enumerate(peers):
        copy = pltpu.make_async_remote_copy(
            src_ref=doc_ref, dst_ref=docs_out.at[me.seq], send_sem=d_send.at[k], recv_sem=d_recv.at[k],
            device_id=peer, device_id_type=MESH,
        )
        copy.start()
        docs.append(copy)
    keep_docs = pltpu.make_async_copy(doc_ref, docs_out.at[me.seq], local.at[2])
    keep_docs.start()
    wide, xhat, root = normalized(x_ref[...])
    a.spread_a()
    b.begin()
    a.spread_b()
    b.spread_a()
    a.finish_b()
    c.begin()
    b.spread_b()
    c.spread_a()
    a.last_b()
    a.settle()

    columns = planes_to_columns(lambda s: pack_all[s, :, 3072:3200].astype(F32))
    vec = columns.T[:16]
    vec_out[...] = vec
    for f in range(4):
        for part in range(3):
            bias_rows[3 * f + part : 3 * f + part + 1, :] = vec[9 + f : 10 + f, 256 * part : 256 * part + 256]
    join_planes(pack_all, jo, pl.ds(0, 3072))
    keep_jo = pltpu.make_async_copy(jo, jo_out, local.at[3])
    keep_jo.start()
    first[...] = (xhat * vec[0:1] + vec[1:2]).astype(BF16)
    second_wide = xhat * vec[2:3] + vec[3:4]
    second[...] = second_wide.astype(BF16)
    first_out[...] = first[...]
    base_out[...] = wide + vec[4:5] + vec[5:6]

    sends = []
    for r in range(4):
        rows = pl.ds(r * ROWS, ROWS)
        tables = [t.at[rows, :] for t in (cos_ref, low_ref, high_ref)]
        x_r = first[rows, :]
        parts = []
        for n in range(2):
            y = dot(x_r, jo[:, n * D : n * D + D]) + vec[6 + n : 7 + n]
            parts.append(turn(y, *tables).astype(BF16))
        parts.append((dot(x_r, jo[:, 2 * D : 3 * D]) + vec[8:9]).astype(BF16))
        parts.append(dot_nt(g_ref[rows, :], jo[:, 3 * D :]).astype(BF16))
        for d in range(4):
            heads[d, rows, :] = jnp.concatenate([p[:, 192 * d : 192 * d + 192] for p in parts], axis=1)
        for k, peer in enumerate(peers):
            copy = pltpu.make_async_remote_copy(
                src_ref=heads.at[peer[0], rows, :], dst_ref=heads_out.at[me.seq, rows, :],
                send_sem=x_send.at[r, k], recv_sem=x_recv.at[r, k], device_id=peer, device_id_type=MESH,
            )
            copy.start()
            sends.append(copy)
        if r == 0:
            b.finish_b()
        if r == 2:
            c.spread_b()
    keep_heads = pltpu.make_async_copy(heads.at[me.seq], heads_out.at[me.seq], local.at[4])
    keep_heads.start()
    b.last_b()
    b.settle()

    join_planes(up_all, uw, pl.ds(0, FF))
    second_t[...] = second_wide.T.astype(BF16)

    def hidden(n, carry):
        cols = pl.ds(pl.multiple_of(256 * n, 256), 256)
        h = dot(second[...], uw[:, cols]) + bias_rows[pl.ds(n, 1), :]
        half = 0.5 + 0.5 * lax.erf(h * SQRT_HALF)
        act[:, cols] = (h * half).astype(BF16)
        slope[:, cols] = (half + h * (jnp.exp(-0.5 * (h * h)) * PHI_SCALE)).astype(BF16)
        return carry

    for n, da in enumerate((0, 3, 1, 2)):
        c.finish_b((da,))
        lax.fori_loop(3 * n, 3 * n + 3, hidden, 0)
    c.last_b()
    c.settle()
    down = down_all.reshape(FF, D)

    def hidden_back(n, carry):
        cols = pl.ds(pl.multiple_of(256 * n, 256), 256)
        back = dot_nt(g_ref[...], down[cols, :])
        grad = (back * slope[:, cols].astype(F32)).astype(BF16)
        slope[:, cols] = grad
        bias_rows[pl.ds(n, 1), :] = column_sum(grad.astype(F32))
        return carry

    lax.fori_loop(0, 12, hidden_back, 0)

    def up_copy(n):
        cols = pl.ds(pl.multiple_of(256 * n, 256), 256)
        slot = lax.rem(n, 2)
        return pltpu.make_async_copy(up_stage.at[slot], du_out.at[:, :, cols], local.at[6 + slot])

    def down_copy(n):
        rows = pl.ds(pl.multiple_of(256 * n, 256), 256)
        slot = lax.rem(n, 2)
        return pltpu.make_async_copy(down_stage.at[slot], dd_out.at[rows, :], local.at[8 + slot])

    def weight_grads(n, carry):
        cols = pl.ds(pl.multiple_of(256 * n, 256), 256)
        slot = lax.rem(n, 2)

        @pl.when(n >= 2)
        def _():
            up_copy(n - 2).wait()
            down_copy(n - 2).wait()

        up_grad = dot(second_t[...], slope[:, cols])
        for s in range(32):
            up_stage[slot, s] = up_grad[24 * s : 24 * s + 24].astype(BF16)
        up_copy(n).start()
        down_stage[slot] = dot_tn(act[:, cols], g_ref[...]).astype(BF16)
        down_copy(n).start()
        return carry

    lax.fori_loop(0, 12, weight_grads, 0)
    for n in (10, 11):
        up_copy(jnp.int32(n)).wait()
        down_copy(jnp.int32(n)).wait()

    for n in range(3):
        cols = pl.ds(256 * n, 256)
        base_out[:, cols] += dot(act[...], down[:, cols])
        grad_out[:, cols] = dot_nt(slope[...], uw[cols, :])
    second_grad = grad_out[...]
    wide, xhat, root = normalized(x_ref[...])
    g_wide = g_ref[...].astype(F32)
    sums_out[...] = jnp.zeros_like(sums_out)
    sums_out[2:3, :] = column_sum(second_grad * xhat)
    sums_out[3:4, :] = column_sum(second_grad)
    total = column_sum(g_wide)
    sums_out[4:5, :] = total
    sums_out[5:6, :] = total
    for f in range(4):
        for part in range(3):
            sums_out[9 + f : 10 + f, 256 * part : 256 * part + 256] = bias_rows[3 * f + part : 3 * f + part + 1, :]
    grad_out[...] = g_wide + norm_back(second_grad, vec_out[2:3, :], xhat, root)

    keep_docs.wait()
    keep_jo.wait()
    keep_heads.wait()
    for copy in docs + sends:
        copy.wait()
    for group in (a, b, c):
        group.drain()


def front(joint, output, up, down, small, x, g, tables, docs):
    any_spec, vmem = pl.BlockSpec(memory_space=pl.ANY), pl.BlockSpec(memory_space=pltpu.VMEM)
    shape = jax.ShapeDtypeStruct
    dma = pltpu.SemaphoreType.DMA
    return pl.pallas_call(
        front_kernel,
        out_shape=[
            shape((4, 512, D), BF16),
            shape((4, 8, 512), F32),
            shape((D, 3072), BF16),
            shape((32, 24, FF), BF16),
            shape((FF, D), BF16),
            shape((512, D), BF16),
            shape((16, D), F32),
            shape((512, D), F32),
            shape((512, D), F32),
            shape((16, D), F32),
        ],
        in_specs=[any_spec] * 4 + [vmem] * 7,
        out_specs=[any_spec] * 5 + [vmem] * 5,
        scratch_shapes=[
            pltpu.VMEM((24, 3328), BF16),
            pltpu.VMEM((32, 24, 3328), BF16),
            pltpu.VMEM((32, 24, FF), BF16),
            pltpu.VMEM((32, 96, D), BF16),
            pltpu.VMEM((D, 3072), BF16),
            pltpu.VMEM((D, FF), BF16),
            pltpu.VMEM((512, D), BF16),
            pltpu.VMEM((512, D), BF16),
            pltpu.VMEM((D, 512), BF16),
            pltpu.VMEM((4, 512, D), BF16),
            pltpu.VMEM((512, FF), BF16),
            pltpu.VMEM((512, FF), BF16),
            pltpu.VMEM((16, 256), F32),
            pltpu.VMEM((2, 32, 24, 256), BF16),
            pltpu.VMEM((2, 256, D), BF16),
            dma((3, 64)),
            dma((3, 64)),
            dma((3,)),
            dma((4, 3)),
            dma((4, 3)),
            dma((3,)),
            dma((3,)),
            dma((10,)),
        ],
        compiler_params=pltpu.CompilerParams(
            collective_id=1, has_side_effects=True, vmem_limit_bytes=60 << 20
        ),
        cost_estimate=pl.CostEstimate(flops=20_000_000_000, bytes_accessed=60_000_000, transcendentals=3_000_000),
        name="front",
    )(joint, output, up, down, small, x, g, *tables, docs)


SLOTS = {2: (0,), 4: (1,), 6: (2,), 7: (3,), 9: (4,), 10: (5,)}


def middle_kernel(
    heads_ref, docs_ref, du, dd, tokens_out, up_left, down_left, *scr
):
    attn, rest = scr[:12], scr[12:]
    s, (score, expo, dk, dv) = attn[:8], attn[8:]
    y, doc_row, doc_col, t_send, t_recv, t_local = rest[:6]
    up_scr, down_scr = rest[6:14], rest[14:22]
    me = Place()
    groups = [Total(me, du, None, *up_scr), Total(me, dd, None, *down_scr)]
    far_sibling = (lax.rem(me.seq + 2, 4) + 1 - 2 * me.core, me.fs)
    enter(total_partners(me) + [far_sibling])
    for group in groups:
        group.begin()
    for b in range(4):
        split_heads(heads_ref, b, s)
        doc_row[:, b * BLK : b * BLK + BLK] = docs_ref[b][:1]
        doc_col[b * BLK : b * BLK + BLK, :] = jnp.broadcast_to(docs_ref[b][:1], (128, BLK)).T
    ticks = total_ticks(groups, 1, RINGS)

    def columns(h, part):
        return pl.ds(pl.multiple_of(256 * h + 128 * part, 128), 128)

    def remote(h, part, i):
        return pltpu.make_async_remote_copy(
            src_ref=y.at[i, :, columns(h, part)],
            dst_ref=tokens_out.at[me.seq, :, columns(h, part)],
            send_sem=t_send.at[h, part, i],
            recv_sem=t_recv.at[h, part, lax.rem(i + 4 - me.seq, 4)],
            device_id=(jnp.int32(i), me.fs),
            device_id_type=MESH,
        )

    def kept(h, part, i):
        return pltpu.make_async_copy(
            y.at[i, :, columns(h, part)], tokens_out.at[i, :, columns(h, part)], t_local.at[h, part]
        )

    def leave(h, part, i):
        pl.when(me.seq != i)(lambda: remote(h, part, i).start())
        pl.when(me.seq == i)(lambda: kept(h, part, i).start())

    def head(h, carry):
        for n, i in enumerate((0, 1, 3, 2)):
            attend_block(h, i, s, doc_row, doc_col, score, expo, dk, dv, y)
            leave(h, 0, i)
            for j in {3: (3,), 2: (1, 2, 0)}.get(i, ()):
                keep_block(h, j, dk, dv, y)
                leave(h, 1, j)
            for turn_of in range(3):
                for tick in SLOTS.get(4 * turn_of + n, ()):
                    pl.when(h == turn_of)(ticks[tick])
        return carry

    lax.fori_loop(0, 3, head, 0)
    for group, left in zip(groups, (up_left, down_left)):
        for dx in range(2):
            left[dx] = group.own(dx)[...]
        group.drain()
    for h in range(3):
        for part in range(2):
            for i in range(4):
                pl.when(me.seq != i)(lambda: remote(h, part, i).wait_send())
                pl.when(me.seq == i)(lambda: kept(h, part, i).wait())
            for k in (1, 2, 3):
                ref = tokens_out.at[lax.rem(me.seq + 4 - k, 4), :, columns(h, part)]
                pltpu.make_async_copy(ref, ref, t_recv.at[h, part, k]).wait()


def middle(heads, docs, du, dd):
    any_spec, vmem = pl.BlockSpec(memory_space=pl.ANY), pl.BlockSpec(memory_space=pltpu.VMEM)
    shape = jax.ShapeDtypeStruct
    dma = pltpu.SemaphoreType.DMA
    return pl.pallas_call(
        middle_kernel,
        out_shape=[shape((4, BLK, D), BF16), shape((2, 24, FF // 2), BF16), shape((2, 96, D // 2), BF16)],
        in_specs=[vmem, vmem, any_spec, any_spec],
        out_specs=[any_spec, vmem, vmem],
        scratch_shapes=attn_scratch()
        + [
            pltpu.VMEM((4, BLK, D), BF16),
            pltpu.VMEM((1, 2048), F32),
            pltpu.VMEM((2048, 128), F32),
            dma((3, 2, 4)),
            dma((3, 2, 4)),
            dma((3, 2)),
        ]
        + total_scratch((32, 24, FF))
        + total_scratch((32, 96, D)),
        compiler_params=pltpu.CompilerParams(
            collective_id=2, has_side_effects=True, vmem_limit_bytes=60 << 20
        ),
        cost_estimate=pl.CostEstimate(flops=12_000_000_000, bytes_accessed=40_000_000, transcendentals=8_000_000),
        name="middle",
    )(heads, docs, du, dd)


def back_kernel(
    tokens_ref, g_ref, jo_hbm, first_ref, x_ref, base_hbm, grad_hbm, vec_ref, sums_ref, cos_ref, low_ref, high_ref,
    up_left, down_left,
    layer_out, input_out, pack_out, small_out, up_out, down_out,
    ctx, jg, part, part_small, small_sum, jo_ref, base_ref, grad_ref, late, *scr
):
    loads = [
        pltpu.make_async_copy(src, dst, late.at[n])
        for n, (src, dst) in enumerate(((jo_hbm, jo_ref), (grad_hbm, grad_ref), (base_hbm, base_ref)))
    ]
    for load in loads:
        load.start()
    me = Place()
    groups = [
        Total(me, part, pack_out, *scr[:8], near=True),
        Total(me, part_small, small_sum, *scr[8:16], near=True),
    ]
    across = [Across(me, up_left, up_out, *scr[16:22]), Across(me, down_left, down_out, *scr[22:28])]
    enter(total_partners(me))
    for group in across:
        group.along_x()
    for r in range(4):
        rows = pl.ds(r * ROWS, ROWS)
        cosine, low, high = (t[rows, :] for t in (cos_ref, low_ref, high_ref))
        tokens = [tokens_ref[s, rows, :] for s in range(4)]
        column = lambda a: jnp.concatenate(
            [t[:, 256 * h + 64 * a : 256 * h + 64 * a + 64] for t in tokens for h in range(3)], axis=1
        )
        ctx[rows, :] = column(0)
        for n in range(2):
            y = column(1 + n).astype(F32)
            jg[rows, n * D : n * D + D] = turn(y, cosine, -low, -high).astype(BF16)
        jg[rows, 2 * D :] = column(3)
    first_t = first_ref[...].astype(F32).T.astype(BF16)
    ctx_t = ctx[...].astype(F32).T.astype(BF16)
    for n in range(12):
        cols = slice(256 * n, 256 * n + 256)
        if n < 9:
            grad = dot(first_t, jg[:, cols])
        else:
            grad = dot(ctx_t, g_ref[:, 256 * n - 2304 : 256 * n - 2048])
        for s in range(32):
            part[s, :, cols] = grad[24 * s : 24 * s + 24].astype(BF16)
    groups[0].begin()
    for load in loads:
        load.wait()
    first_grad = dot_nt(jg[...], jo_ref[:, :2304])
    wide, xhat, root = normalized(x_ref[...])
    input_out[...] = (grad_ref[...] + norm_back(first_grad, vec_ref[0:1, :], xhat, root)).astype(BF16)
    rows = jnp.concatenate(
        [column_sum(first_grad * xhat), column_sum(first_grad), sums_ref[2:6, :]]
        + [column_sum(jg[:, n * D : n * D + D].astype(F32)) for n in range(3)]
        + [sums_ref[9:13, :], jnp.zeros((115, D), F32)],
        axis=0,
    )
    for s, tile in enumerate(columns_to_planes(rows.T)):
        part_small[s, :, :128] = tile.astype(BF16)
        part_small[s, :, 128:] = jnp.zeros((24, 128), BF16)
    groups[1].begin()
    ticks = total_ticks(groups, 0, RINGS + CROSS)
    ticks[0]()
    layer_out[...] = (base_ref[...] + dot(ctx[...], jo_ref[:, 2304:])).astype(BF16)
    for n, tick in enumerate(ticks[1:]):
        tick()
        if n == 1:
            for group in across:
                group.total()
    for group in groups + across:
        group.end()
    columns = jnp.concatenate([small_sum[:, :128].astype(F32), jnp.zeros((104, 128), F32)], axis=0)
    turned = columns.T
    small_out[...] = jnp.concatenate(
        [
            turned[:6],
            jnp.concatenate([turned[6 + c : 7 + c, :24] for c in range(3)] + [jnp.zeros((1, 56), F32)], axis=1),
            jnp.concatenate([turned[9 + c : 10 + c, :24] for c in range(4)] + [jnp.zeros((1, 32), F32)], axis=1),
        ],
        axis=0,
    )


def back(tokens, g, jo, first_in, x, base, base_grad, vec, sums, tables, up_left, down_left):
    any_spec, vmem = pl.BlockSpec(memory_space=pl.ANY), pl.BlockSpec(memory_space=pltpu.VMEM)
    shape = jax.ShapeDtypeStruct
    return pl.pallas_call(
        back_kernel,
        out_shape=[shape((BLK, D), BF16), shape((BLK, D), BF16), shape((24, 3072), BF16), shape((8, 128), F32), shape((24, FF), BF16), shape((96, D), BF16)],
        in_specs=[vmem, vmem, any_spec, vmem, vmem, any_spec, any_spec] + [vmem] * 7,
        out_specs=[vmem] * 6,
        scratch_shapes=[
            pltpu.VMEM((BLK, D), BF16),
            pltpu.VMEM((BLK, 2304), BF16),
            pltpu.VMEM((32, 24, 3072), BF16),
            pltpu.VMEM((32, 24, 256), BF16),
            pltpu.VMEM((24, 256), BF16),
            pltpu.VMEM((D, 3072), BF16),
            pltpu.VMEM((BLK, D), F32),
            pltpu.VMEM((BLK, D), F32),
            pltpu.SemaphoreType.DMA((3,)),
        ]
        + total_scratch((32, 24, 3072))
        + total_scratch((32, 24, 256))
        + total_scratch((32, 24, FF))[2:]
        + total_scratch((32, 96, D))[2:],
        compiler_params=pltpu.CompilerParams(
            collective_id=3, has_side_effects=True, vmem_limit_bytes=60 << 20
        ),
        cost_estimate=pl.CostEstimate(flops=6_000_000_000, bytes_accessed=20_000_000, transcendentals=1000),
        name="back",
    )(tokens, g, jo, first_in, x, base, base_grad, vec, sums, *tables, up_left, down_left)


HEAD_DIM = 64
ROT = 16


def rotary_tables(places):
    dim = jnp.arange(128, dtype=jnp.int32) % HEAD_DIM
    freqs = jnp.where(dim < ROT, 10000.0 ** (-2.0 * (dim % 8).astype(F32) / ROT), 0.0)
    turned = places.astype(F32)[:, None] * freqs[None, :]
    sine = jnp.sin(turned)
    return jnp.cos(turned), jnp.where(dim < 8, -sine, 0.0), jnp.where(dim >= 8, sine, 0.0)


def pad_row(v):
    return jnp.pad(v.astype(F32), (0, 128 - v.shape[0]))[None]


def finish_kernel(pack, up, down, small, layer, grad, *outs):
    joint_out, output_out, up_out, down_out, layer_out, grad_out = outs[:6]
    layer_out[...] = layer[...]
    grad_out[...] = grad[...]
    joint_out[...] = pack[:, :2304].astype(F32)
    output_out[...] = pack[:, 2304:].astype(F32)
    up_out[...] = up[...].astype(F32)
    down_out[...] = down[...].astype(F32)
    for n, out in enumerate(outs[6:]):
        out[...] = small[n, : out.shape[0]]


def finish(pack, up, down, small, layer, grad):
    shape = jax.ShapeDtypeStruct
    return pl.pallas_call(
        finish_kernel,
        out_shape=[shape(s, F32) for s in ((24, 2304), (24, D), (24, FF), (96, D))]
        + [shape((BLK, D), BF16)] * 2
        + [shape((n,), F32) for n in (24, 24, 24, 24, 24, 24, 72, 96)],
        in_specs=[pl.BlockSpec(memory_space=pltpu.VMEM)] * 6,
        out_specs=[pl.BlockSpec(memory_space=pltpu.VMEM)] * 14,
        name="finish",
    )(pack, up, down, small, layer, grad)


def body(
    hidden_states,
    positions,
    documents,
    cotangent,
    first_gain,
    first_shift,
    second_gain,
    second_shift,
    joint_weight,
    joint_bias,
    output_weight,
    output_bias,
    up_weight,
    up_bias,
    down_weight,
    down_bias,
):
    small = jnp.concatenate(
        [
            pad_row(v)
            for v in (first_gain, first_shift, second_gain, second_shift, output_bias, down_bias, joint_bias, up_bias)
        ],
        axis=0,
    )
    tables = rotary_tables(positions[0])
    docs = jnp.broadcast_to(documents[0].astype(F32)[None], (8, 512))
    by_heads, doc_rows, jo, du, dd, first_in, vec, base, base_grad, sums = front(
        joint_weight, output_weight, up_weight, down_weight, small, hidden_states[0], cotangent[0], tables, docs
    )
    tokens, up_left, down_left = middle(by_heads, doc_rows, du, dd.reshape(32, 96, D))
    layer_output, input_grad, pack_sum, small_sum, up_sum, down_sum = back(
        tokens, cotangent[0], jo, first_in, hidden_states[0], base, base_grad, vec, sums, tables, up_left, down_left
    )
    (
        joint_sum, output_sum, up_total, down_total, layer_output, input_grad,
        gain_one, shift_one, gain_two, shift_two, output_shift, down_shift, joint_shift, up_shift,
    ) = finish(
        pack_sum, up_sum, down_sum, small_sum, layer_output, input_grad
    )
    return (
        layer_output[None],
        input_grad[None],
        gain_one,
        shift_one,
        gain_two,
        shift_two,
        joint_sum,
        joint_shift,
        output_sum,
        output_shift,
        up_total,
        up_shift,
        down_total,
        down_shift,
    )


def solution(mesh):
    in_specs = (
        P("fsdp", "seq", None),
        P("fsdp", "seq"),
        P("fsdp", "seq"),
        P("fsdp", "seq", None),
        P("fsdp"),
        P("fsdp"),
        P("fsdp"),
        P("fsdp"),
        P("fsdp", None),
        P("fsdp"),
        P("fsdp", None),
        P("fsdp"),
        P("fsdp", None),
        P("fsdp"),
        P("fsdp", None),
        P("fsdp"),
    )
    out_specs = (
        P("fsdp", "seq", None),
        P("fsdp", "seq", None),
        P("fsdp"),
        P("fsdp"),
        P("fsdp"),
        P("fsdp"),
        P("fsdp", None),
        P("fsdp"),
        P("fsdp", None),
        P("fsdp"),
        P("fsdp", None),
        P("fsdp"),
        P("fsdp", None),
        P("fsdp"),
    )
    return jax.shard_map(body, mesh=mesh, in_specs=in_specs, out_specs=out_specs, check_vma=False)
```
